128 devices in a mesh: ctx: 16 (over x_hi, z, core), dp: 8 (over y, x_lo).
Axes of the slice: x: 4 (x_hi: 2, x_lo: 2; x = x_hi * 2 + x_lo), y: 4, z: 4, core: 2. Of those that a mesh axis runs over, the one named last changes fastest.
Arguments:
- layer_input: bfloat16 [8, 2048, 768], P('dp', 'ctx'), may hold values from -6 to 6
- encoder_states: bfloat16 [8, 2048, 768], P('dp', 'ctx'), may hold values from -6 to 6
- cotangent: bfloat16 [8, 2048, 768], P('dp', 'ctx'), may hold values from -6 to 6
- bucket_ids: int32 [2048], replicated, may hold values from 0 to 31
- bias_table: float32 [32, 12], replicated, may hold values from -4 to 4
- gain_first: float32 [768], replicated, may hold values from 0.1 to 1.9
- gain_second: float32 [768], replicated, may hold values from 0.1 to 1.9
- gain_third: float32 [768], replicated, may hold values from 0.1 to 1.9
- self_query: bfloat16 [768, 768], P('dp'), may hold values from -0.09375 to 0.09375
- self_key: bfloat16 [768, 768], P('dp'), may hold values from -0.09375 to 0.09375
- self_value: bfloat16 [768, 768], P('dp'), may hold values from -0.21875 to 0.21875
- self_output: bfloat16 [768, 768], P('dp'), may hold values from -1.25 to 1.25
- cross_query: bfloat16 [768, 768], P('dp'), may hold values from -0.09375 to 0.09375
- cross_key: bfloat16 [768, 768], P('dp'), may hold values from -0.09375 to 0.09375
- cross_value: bfloat16 [768, 768], P('dp'), may hold values from -0.21875 to 0.21875
- cross_output: bfloat16 [768, 768], P('dp'), may hold values from -1.75 to 1.75
- gate_weight: bfloat16 [768, 2048], P('dp'), may hold values from -0.21875 to 0.21875
- up_weight: bfloat16 [768, 2048], P('dp'), may hold values from -0.21875 to 0.21875
- down_weight: bfloat16 [2048, 768], P('dp'), may hold values from -0.125 to 0.125
Outputs:
- layer_output: bfloat16 [8, 2048, 768], P('dp', 'ctx')
- grad_input: float32 [8, 2048, 768], P('dp', 'ctx')
- grad_encoder: float32 [8, 2048, 768], P('dp', 'ctx')
- grad_bias_table: float32 [32, 12], replicated
- grad_gain_first: float32 [768], replicated
- grad_gain_second: float32 [768], replicated
- grad_gain_third: float32 [768], replicated
- grad_self_query: float32 [768, 768], P('dp')
- grad_self_key: float32 [768, 768], P('dp')
- grad_self_value: float32 [768, 768], P('dp')
- grad_self_output: float32 [768, 768], P('dp')
- grad_cross_query: float32 [768, 768], P('dp')
- grad_cross_key: float32 [768, 768], P('dp')
- grad_cross_value: float32 [768, 768], P('dp')
- grad_cross_output: float32 [768, 768], P('dp')
- grad_gate_weight: float32 [768, 2048], P('dp')
- grad_up_weight: float32 [768, 2048], P('dp')
- grad_down_weight: float32 [2048, 768], P('dp')
The draws below stay inside these ranges and needn't reach their ends.
All inputs are finite; a program needn't handle non-finite values.
Results may differ from the reference program's by a relative error of at most 0.04.
Values may be sent and summed in bfloat16 or wider, within the bound.
A program may use at most 192 MiB of HBM per device.

```python
import math
import jax
import jax.numpy as jnp
from jax import lax

D = 768
H = 12
FF = 2048
NB = 32
LENGTH = 2048
ENC_LEN = 2048
BATCH = 8


def set_ends(result, key, low, top_value):
    dims = result.shape
    index_at = [jax.random.randint(jax.random.fold_in(key, axis), (), 0, dims[axis]) for axis in range(len(dims))]
    result = result.at[tuple(index_at)].set(low)
    longest = dims.index(max(dims))
    index_at[longest] = (index_at[longest] + 1) % dims[longest]
    return result.at[tuple(index_at)].set(top_value)


def level_of(stream_key, shape, cuts, smallest, high):
    level, own = 1.0, jax.random.fold_in(stream_key, 6)
    for dim, blocks in cuts:
        steps = jnp.exp(jax.random.uniform(jax.random.fold_in(own, dim), (blocks,), jnp.float32, smallest / len(cuts), high / len(cuts)))
        level = level * jnp.repeat(steps, shape[dim] // blocks).reshape([-1 if axis == dim else 1 for axis in range(len(shape))])
    return level


def gaussian(key, shape, spread, most, cuts=(), kind=jnp.bfloat16):
    entries = spread * jax.random.normal(key, shape, jnp.float32)
    if cuts:
        entries = entries * level_of(key, shape, cuts, -0.22, 0.18)
    return jnp.clip(entries, -most, most).astype(kind)


def setup_inputs(seed: int = 0) -> dict:
    splits = jax.random.split(jax.random.key(seed), 20)
    layer_input = gaussian(splits[0], (BATCH, LENGTH, D), 1.0, 6.0, ((0, 8), (1, 16)))
    encoder_states = gaussian(splits[1], (BATCH, ENC_LEN, D), 1.0, 6.0, ((0, 8), (1, 16)))
    cotangent = gaussian(splits[2], (BATCH, LENGTH, D), 1.0, 6.0, ((0, 8), (1, 16)))
    bucket_ids = set_ends(jax.random.randint(splits[3], (LENGTH,), 0, NB), jax.random.fold_in(splits[3], 1), 0, NB - 1).astype(jnp.int32)
    bias_table = gaussian(splits[4], (NB, H), 1.0, 4.0, (), jnp.float32)
    gain_first = jnp.clip(1.0 + 0.18 * jax.random.normal(splits[5], (D,), jnp.float32), 0.1, 1.9)
    gain_second = jnp.clip(1.0 + 0.18 * jax.random.normal(splits[6], (D,), jnp.float32), 0.1, 1.9)
    gain_third = jnp.clip(1.0 + 0.18 * jax.random.normal(splits[7], (D,), jnp.float32), 0.1, 1.9)
    self_query = gaussian(splits[8], (D, D), (6 * D) ** -0.5, 0.09375, ((0, 8),))
    self_key = gaussian(splits[9], (D, D), (6 * D) ** -0.5, 0.09375, ((0, 8),))
    self_value = gaussian(splits[10], (D, D), D ** -0.5, 0.21875, ((0, 8),))
    self_output = gaussian(splits[11], (D, D), (D // 32) ** -0.5, 1.25, ((0, 8),))
    cross_query = gaussian(splits[12], (D, D), (6 * D) ** -0.5, 0.09375, ((0, 8),))
    cross_key = gaussian(splits[13], (D, D), (6 * D) ** -0.5, 0.09375, ((0, 8),))
    cross_value = gaussian(splits[14], (D, D), D ** -0.5, 0.21875, ((0, 8),))
    cross_output = gaussian(splits[15], (D, D), (D // 64) ** -0.5, 1.75, ((0, 8),))
    gate_weight = gaussian(splits[16], (D, FF), D ** -0.5, 0.21875, ((0, 8),))
    up_weight = gaussian(splits[17], (D, FF), D ** -0.5, 0.21875, ((0, 8),))
    down_weight = gaussian(splits[18], (FF, D), FF ** -0.5, 0.125, ((0, 8),))
    return dict(layer_input=layer_input, encoder_states=encoder_states, cotangent=cotangent, bucket_ids=bucket_ids, bias_table=bias_table, gain_first=gain_first, gain_second=gain_second, gain_third=gain_third, self_query=self_query, self_key=self_key, self_value=self_value, self_output=self_output, cross_query=cross_query, cross_key=cross_key, cross_value=cross_value, cross_output=cross_output, gate_weight=gate_weight, up_weight=up_weight, down_weight=down_weight)


@jax.custom_vjp
def low(v):
    return lax.optimization_barrier(v.astype(jnp.bfloat16)).astype(jnp.float32)

@jax.custom_vjp
def low_back(v):
    return v

def low_keep(v):
    return (low(v), None)

def low_pass(kept, grad):
    return (grad,)

def back_keep(v):
    return (v, None)

def back_low(kept, grad):
    return (low(grad),)
low.defvjp(low_keep, low_pass)
low_back.defvjp(back_keep, back_low)
EPSILON = 1e-06
NEGATIVE = -1e+30
PRECISE = lax.Precision.HIGHEST

def rms_norm(values, gain):
    return values * lax.rsqrt(lax.optimization_barrier(jnp.mean(values * values, axis=-1, keepdims=True)) + EPSILON) * gain

def self_sequence(queries, keys, values, table, buckets):
    length = queries.shape[0]
    block_len = math.gcd(512, length)
    key_pos = jnp.arange(length, dtype=jnp.int32)

    def one_block(begin_row, queries, keys, values, table):
        query_rows = lax.dynamic_slice_in_dim(queries, begin_row, block_len, 0)
        query_pos = begin_row + jnp.arange(block_len, dtype=jnp.int32)
        offset = query_pos[:, None] - key_pos[None, :]
        bucket_rows = jnp.take(buckets, jnp.clip(offset, 0, length - 1).astype(jnp.int32))
        bias_block = jnp.transpose(jnp.take(table, bucket_rows, axis=0), (2, 0, 1))
        scores = low_back(jnp.einsum('qhe,khe->hqk', query_rows, keys, precision=PRECISE) + bias_block)
        scores = jnp.where((offset >= 0)[None], scores, NEGATIVE)
        row_max = lax.optimization_barrier(jnp.max(scores, axis=-1, keepdims=True))
        expo_rows = jnp.exp(scores - row_max)
        probs = low(expo_rows / lax.optimization_barrier(jnp.sum(expo_rows, axis=-1, keepdims=True)))
        return jnp.einsum('hqk,khe->qhe', probs, values, precision=PRECISE)
    saved_block = jax.checkpoint(one_block)
    starts = jnp.arange(0, length, block_len, dtype=jnp.int32)
    pieces = lax.map(lambda begin_row: saved_block(begin_row, queries, keys, values, table), starts)
    return pieces.reshape(queries.shape)

def cross_sequence(queries, keys, values):
    length = queries.shape[0]
    block_len = math.gcd(512, length)

    def one_block(begin_row, queries, keys, values):
        query_rows = lax.dynamic_slice_in_dim(queries, begin_row, block_len, 0)
        scores = low_back(jnp.einsum('qhe,khe->hqk', query_rows, keys, precision=PRECISE))
        row_max = lax.optimization_barrier(jnp.max(scores, axis=-1, keepdims=True))
        expo_rows = jnp.exp(scores - row_max)
        probs = low(expo_rows / lax.optimization_barrier(jnp.sum(expo_rows, axis=-1, keepdims=True)))
        return jnp.einsum('hqk,khe->qhe', probs, values, precision=PRECISE)
    saved_block = jax.checkpoint(one_block)
    starts = jnp.arange(0, length, block_len, dtype=jnp.int32)
    pieces = lax.map(lambda begin_row: saved_block(begin_row, queries, keys, values), starts)
    return pieces.reshape(queries.shape)

def layer_forward(residual, encoder, table, gains, weights, buckets):
    seq_count, length, model_width = residual.shape
    head_count = table.shape[1]
    head_size = model_width // head_count

    def project(activity, weight):
        return jnp.dot(activity, weight, precision=PRECISE)

    def split_heads(activity):
        return activity.reshape(activity.shape[0], activity.shape[1], head_count, head_size)

    def self_one(triple):
        return jax.checkpoint(self_sequence)(triple[0], triple[1], triple[2], table, buckets)

    def cross_one(triple):
        return jax.checkpoint(cross_sequence)(triple[0], triple[1], triple[2])
    normed_one = low(rms_norm(residual, gains[0]))
    queries = split_heads(low(low_back(project(normed_one, weights[0]))))
    keys = split_heads(low(low_back(project(normed_one, weights[1]))))
    values = split_heads(low(low_back(project(normed_one, weights[2]))))
    attended = lax.map(self_one, (queries, keys, values)).reshape(seq_count, length, model_width)
    attended = low(low_back(attended))
    middle = residual + low_back(project(attended, weights[3]))
    normed_two = low(rms_norm(middle, gains[1]))
    cross_queries = split_heads(low(low_back(project(normed_two, weights[4]))))
    cross_keys = split_heads(low(low_back(project(encoder, weights[5]))))
    cross_values = split_heads(low(low_back(project(encoder, weights[6]))))
    crossed = lax.map(cross_one, (cross_queries, cross_keys, cross_values)).reshape(seq_count, length, model_width)
    crossed = low(low_back(crossed))
    after_cross = middle + low_back(project(crossed, weights[7]))
    normed_three = low(rms_norm(after_cross, gains[2]))
    gate_act = low_back(project(normed_three, weights[8]))
    up_act = low_back(project(normed_three, weights[9]))
    mixed = low(jax.nn.gelu(gate_act, approximate=True) * up_act)
    return after_cross + low_back(project(mixed, weights[10]))

def reference(layer_input, encoder_states, cotangent, bucket_ids, bias_table, gain_first, gain_second, gain_third, self_query, self_key, self_value, self_output, cross_query, cross_key, cross_value, cross_output, gate_weight, up_weight, down_weight):
    weights = (self_query.astype(jnp.float32), self_key.astype(jnp.float32), self_value.astype(jnp.float32), self_output.astype(jnp.float32), cross_query.astype(jnp.float32), cross_key.astype(jnp.float32), cross_value.astype(jnp.float32), cross_output.astype(jnp.float32), gate_weight.astype(jnp.float32), up_weight.astype(jnp.float32), down_weight.astype(jnp.float32))
    residual = layer_input.astype(jnp.float32)
    encoder = encoder_states.astype(jnp.float32)

    def run_layer(residual, encoder, table, gains, weights):
        return layer_forward(residual, encoder, table, gains, weights, bucket_ids)
    final, pullback = jax.vjp(run_layer, residual, encoder, bias_table, (gain_first, gain_second, gain_third), weights)
    grad_input, grad_encoder, grad_table, grad_gains, grad_weights = pullback(cotangent.astype(jnp.float32))
    return (final.astype(jnp.bfloat16), grad_input, grad_encoder, grad_table, grad_gains[0], grad_gains[1], grad_gains[2], grad_weights[0], grad_weights[1], grad_weights[2], grad_weights[3], grad_weights[4], grad_weights[5], grad_weights[6], grad_weights[7], grad_weights[8], grad_weights[9], grad_weights[10])
```

```python
import functools
import math
import jax
import jax.numpy as jnp
from jax import lax
from jax.experimental import pallas as pl
from jax.experimental.pallas import tpu as pltpu
from jax.sharding import PartitionSpec as P

MESH = pl.DeviceIdType.MESH
ANY = pl.BlockSpec(memory_space=pl.ANY)
VMEM = pl.BlockSpec(memory_space=pltpu.VMEM)


class Place:
    def __init__(self):
        c = lax.axis_index("ctx")
        d = lax.axis_index("dp")
        self.c, self.d = c, d
        self.x_hi = c // 8
        self.z = (c // 2) % 4
        self.core = c % 2
        self.y = d // 2
        self.x_lo = d % 2
        self.y_a = self.y + 1 - 2 * (self.y % 2)
        self.y_b = 3 - self.y
        self.y_ab = 3 - self.y_a
        self.z_a = self.z + 1 - 2 * (self.z % 2)
        self.z_b = 3 - self.z
        self.z_ab = 3 - self.z_a
        far_lo, far_hi = 1 - self.x_lo, 1 - self.x_hi
        self.x = self.x_lo * 2 + self.x_hi
        self.x_a = far_lo * 2 + self.x_hi
        self.x_b = far_lo * 2 + far_hi
        self.x_ab = self.x_lo * 2 + far_hi
        same = self.x_hi * 8 + self.z * 2 + self.core
        self.dev = {
            "core": (self.x_hi * 8 + self.z * 2 + 1 - self.core, d),
            "ya": (same, self.y_a * 2 + self.x_lo),
            "yb": (same, self.y_b * 2 + self.x_lo),
            "za": (self.x_hi * 8 + self.z_a * 2 + self.core, d),
            "zb": (self.x_hi * 8 + self.z_b * 2 + self.core, d),
            "xa": (same, self.y * 2 + far_lo),
            "xb": (far_hi * 8 + self.z * 2 + self.core, self.y * 2 + far_lo),
            "xab": (far_hi * 8 + self.z * 2 + self.core, d),
        }

    def greet(self, names):
        barrier = pltpu.get_barrier_semaphore()
        for name in names:
            pl.semaphore_signal(
                barrier, inc=1, device_id=self.dev[name], device_id_type=MESH
            )
        pl.semaphore_wait(barrier, len(names))

    def send(self, name, src, dst, send_sem, recv_sem):
        copy = pltpu.make_async_remote_copy(
            src_ref=src,
            dst_ref=dst,
            send_sem=send_sem,
            recv_sem=recv_sem,
            device_id=self.dev[name],
            device_id_type=MESH,
        )
        copy.start()
        return copy


GATHER_PLAN = (
    ((0, "pair", 0), (8, "za", 0), (9, "zb", 0)),
    ((1, "pair", 0), (8, "za", 1), (9, "zb", 1)),
    ((2, "pair", 0), (3, "za", 0), (10, "zb", 0)),
    ((5, "pair", 0), (4, "za", 0), (10, "zb", 1)),
    ((6, "pair", 0), (7, "za", 0), (10, "zb", 2)),
)


class Chain:
    def __init__(self, me, source, target, kind, half, piece, pieces, sems):
        rows, cols = source.shape
        width = cols // 2 // pieces
        self.me, self.source, self.target, self.kind = me, source, target, kind
        self.sems, self.slot, self.copies = sems, 0, []
        self.all_rows = pl.ds(0, rows)
        if kind == "pair":
            self.rows = pl.ds(half * (rows // 2), rows // 2)
            self.all_rows = self.rows
            flip = half == 1
        else:
            bit = me.z % 2 if kind == "za" else me.z // 2
            self.rows = pl.ds(pl.multiple_of(bit * (rows // 2), 16), rows // 2)
            flip = kind == "zb"
        self.cols = pl.ds(pl.multiple_of(me.core * (cols // 2) + piece * width, 128), width)
        self.other = pl.ds(pl.multiple_of((1 - me.core) * (cols // 2) + piece * width, 128), width)
        self.first, self.second = ("yb", "ya") if flip else ("ya", "yb")
        self.near = me.y_b if flip else me.y_a
        self.side = "xb" if flip else "xa"
        self.stages = 4 if kind == "pair" else 5

    def go(self, name, src, dst):
        send_sem, recv_sem, index = self.sems
        copy = self.me.send(
            name, src, dst, send_sem.at[index, self.slot], recv_sem.at[index, self.slot]
        )
        self.slot += 1
        self.copies.append(copy)
        return copy

    def run(self, stage):
        me, out = self.me, self.target
        if stage == 0:
            mine = self.source.at[self.rows, self.cols]
            spot = out.at[me.y, me.x_lo, self.rows, self.cols]
            self.first_copy = self.go(self.first, mine, spot)
            self.second_copy = self.go(self.second, mine, spot)
            self.own_copy = self.go(
                "core",
                self.source.at[self.rows, self.other],
                out.at[me.y, me.x_lo, self.rows, self.other],
            )
        elif stage == 1:
            self.first_copy.wait_recv()
            got = out.at[self.near, me.x_lo, self.rows, self.cols]
            self.third_copy = self.go(self.second, got, got)
        elif stage == 2:
            self.second_copy.wait_recv()
            self.own_copy.wait_recv()
            self.third_copy.wait_recv()
            got = out.at[:, me.x_lo, self.rows, self.cols]
            self.last = self.go(self.side, got, got)
        elif stage == 3 and self.kind != "pair":
            self.last.wait_recv()
            got = out.at[:, :, self.rows, self.cols]
            self.last = self.go(self.kind, got, got)
        elif stage == self.stages - 1:
            self.last.wait_recv()
            got = out.at[:, :, self.all_rows, self.cols]
            self.last = self.go("core", got, got)
        elif stage == self.stages:
            self.last.wait_recv()


def gather_kernel(count, plan, *refs):
    ins, outs = refs[:count], refs[count : 2 * count]
    send_sem, recv_sem = refs[2 * count :]
    me = Place()
    me.greet(("ya", "yb", "xa", "xb", "za", "zb", "core"))
    pieces = {}
    for group in plan:
        for array, kind, piece in group:
            pieces[array] = max(pieces.get(array, 0), piece + 1)
    groups = []
    index = 0
    for group in plan:
        chains = []
        for array, kind, piece in group:
            for half in range(2 if kind == "pair" else 1):
                chains.append(
                    Chain(
                        me, ins[array], outs[array], kind, half, piece, pieces[array],
                        (send_sem, recv_sem, index),
                    )
                )
                index += 1
        groups.append(chains)
    for chain in groups[0]:
        chain.run(0)
    for tick in range(1, len(groups) + 6):
        for stage in (5, 4, 3, 2, 1, 0):
            spot = tick - stage
            if stage == 0 and tick < len(groups):
                for chain in groups[tick]:
                    chain.run(0)
            elif stage > 0 and 0 <= spot < len(groups):
                for chain in groups[spot]:
                    chain.run(stage)
    for chains in groups:
        for chain in chains:
            for copy in chain.copies:
                copy.wait_send()


def gather_weights(shards, plan, collective_id):
    count = len(shards)
    chains = sum(2 if kind == "pair" else 1 for group in plan for _, kind, _ in group)
    outs = pl.pallas_call(
        functools.partial(gather_kernel, count, plan),
        out_shape=[
            jax.ShapeDtypeStruct((4, 2) + shard.shape, shard.dtype) for shard in shards
        ],
        in_specs=[ANY] * count,
        out_specs=[ANY] * count,
        scratch_shapes=[
            pltpu.SemaphoreType.DMA((chains, 7)),
            pltpu.SemaphoreType.DMA((chains, 7)),
        ],
        compiler_params=pltpu.CompilerParams(collective_id=collective_id, has_side_effects=True),
        name="gather_weights",
    )(*shards)
    return [out.reshape(8 * out.shape[2], out.shape[3]) for out in outs]

AXES = ("y", "x", "z")


def reduce_kernel(
    grads, small, *refs
):
    outs, small_out = refs[:11], refs[11]
    (acc, r0, r1, r2, r3, r4, r5, r6, full, sm_in,
     load_sem, send_sem, recv_sem, sm_send, sm_recv, ag_send, ag_recv) = refs[12:]
    recvs = (r1, r2, r3, r4, r5, r6)
    me = Place()
    me.greet(("core", "ya", "yb", "xa", "xb", "za", "zb", "xab"))
    spots = {
        "y": (me.y, me.y_a, me.y_b, me.y_ab),
        "x": (me.x, me.x_a, me.x_b, me.x_ab),
        "z": (me.z, me.z_a, me.z_b, me.z_ab),
    }
    parts = range(6)
    started = []

    def go(name, src, dst, send, recv):
        copy = me.send(name, src, dst, send, recv)
        started.append(copy)
        return copy

    small_out[...] = small[...]
    small_steps = ("core", "ya", "yb", "xa", "xb", "za", "zb")
    small_copies = []

    def small_start(step):
        small_copies.append(
            me.send(small_steps[step], small_out, sm_in.at[step], sm_send.at[step], sm_recv.at[step])
        )

    def small_end(step):
        small_copies[step].wait()
        small_out[...] = small_out[...] + sm_in[step]

    small_start(0)

    def order(part):
        first = (part // 2) % 3
        return [AXES[(first + k) % 3] for k in range(3)]

    def region(part, picks):
        return (part,) + tuple(picks.get(axis, slice(None)) for axis in AXES)

    def at(ref, index):
        return ref.at[index]

    core_copies, loads = [], []
    for part in parts:
        core_copies.append(
            go("core", grads.at[1 - me.core, part], r0.at[part], send_sem.at[part, 0], recv_sem.at[part, 0])
        )
        load = pltpu.make_async_copy(grads.at[me.core, part], acc.at[part], load_sem.at[part])
        load.start()
        loads.append(load)

    def add(index, source, source_index):
        acc[index] = acc[index] + source[source_index]

    def dims(part):
        return ("a", "b") if part % 2 == 0 else ("b", "a")

    def add_first(part, picks):
        axis = order(part)[0]
        rest = [name for name in AXES if name != axis]

        def step(k, carry):
            index = region(part, {**picks, rest[0]: k})
            acc[index] = acc[index] + r0[index]
            return carry

        lax.fori_loop(0, 4, step, 0)

    pending = {}
    for part in parts:
        axis = order(part)[0]
        me_at, a_at, b_at, ab_at = spots[axis]
        first, second = dims(part)
        sent = (a_at, ab_at) if first == "a" else (b_at, ab_at)
        core_copies[part].wait_recv()
        loads[part].wait()
        pending[part] = []
        for slot, spot in enumerate(sent):
            add_first(part, {axis: spot})
            pending[part].append(
                go(
                    axis + first,
                    at(acc, region(part, {axis: spot})),
                    r1.at[part, slot],
                    send_sem.at[part, 1 + slot],
                    recv_sem.at[part, 1 + slot],
                )
            )
    small_end(0)
    small_start(1)
    for part in parts:
        axis = order(part)[0]
        me_at, a_at, b_at, ab_at = spots[axis]
        first, second = dims(part)
        kept = b_at if first == "a" else a_at
        add_first(part, {axis: kept})
        add_first(part, {axis: me_at})

    sem_at = {part: 3 for part in parts}

    def next_sem(part):
        sem_at[part] += 1
        return send_sem.at[part, sem_at[part] - 1], recv_sem.at[part, sem_at[part] - 1]

    for level in range(3):
        one, two = recvs[2 * level], recvs[2 * level + 1]
        for part in parts:
            axes = order(part)
            axis = axes[level]
            first, second = dims(part)
            me_at, a_at, b_at, ab_at = spots[axis]
            kept = b_at if first == "a" else a_at
            fixed = {name: spots[name][0] for name in axes[:level]}
            for copy in pending[part]:
                copy.wait_recv()
            add(region(part, {**fixed, axis: kept}), one, (part, 1))
            send, recv = next_sem(part)
            pending[part] = [
                go(axis + second, at(acc, region(part, {**fixed, axis: kept})), two.at[part], send, recv)
            ]
        for part in parts:
            axes = order(part)
            fixed = {name: spots[name][0] for name in axes[: level + 1]}
            add(region(part, fixed), one, (part, 0))
        small_end(2 * level + 1)
        small_start(2 * level + 2)
        for part in parts:
            axes = order(part)
            fixed = {name: spots[name][0] for name in axes[: level + 1]}
            for copy in pending[part]:
                copy.wait_recv()
            add(region(part, fixed), two, (part,))
            if level == 2:
                continue
            axis = axes[level + 1]
            first, second = dims(part)
            me_at, a_at, b_at, ab_at = spots[axis]
            sent = (a_at, ab_at) if first == "a" else (b_at, ab_at)
            pending[part] = []
            for slot, spot in enumerate(sent):
                send, recv = next_sem(part)
                pending[part].append(
                    go(
                        axis + first,
                        at(acc, region(part, {**fixed, axis: spot})),
                        recvs[2 * level + 2].at[part, slot],
                        send,
                        recv,
                    )
                )
        small_end(2 * level + 2)
        if level < 2:
            small_start(2 * level + 3)

    here = me.x_hi * 4 + me.z
    there = (1 - me.x_hi) * 4 + me.z
    for part in parts:
        full[here, me.core, part] = acc[part, me.y, me.x, me.z]
    used = [0]

    def pass_on(name, group, half):
        index = used[0]
        used[0] += 1
        src = full.at[group, me.core, pl.ds(3 * half, 3)]
        return go(name, src, src, ag_send.at[index], ag_recv.at[index])

    early = [pass_on("xab", here, half) for half in range(2)]
    near = [pass_on("za", here, 0), pass_on("zb", here, 1)]
    far = []
    for half in range(2):
        early[half].wait_recv()
        far.append(pass_on(("za", "zb")[half], there, half))
    base, base_far = me.x_hi * 4, (1 - me.x_hi) * 4
    ends = [pass_on("zb", here, 0), pass_on("za", here, 1)]
    ends += [pass_on("zb", there, 0), pass_on("za", there, 1)]
    for half in range(2):
        got = (me.z_a, me.z_b)[half]
        near[half].wait_recv()
        ends.append(pass_on(("zb", "za")[half], base + got, half))
    for half in range(2):
        got = (me.z_a, me.z_b)[half]
        far[half].wait_recv()
        ends.append(pass_on(("zb", "za")[half], base_far + got, half))
    for copy in ends:
        copy.wait_recv()
    last = go("core", full.at[:, me.core], full.at[:, me.core], ag_send.at[used[0]], ag_recv.at[used[0]])

    def place(o):
        group, core = o // 2, o % 2
        for part in parts:
            rows = pl.ds(16 * part, 16)
            outs[group][rows, pl.ds(core * 384, 384)] = full[group, core, part, :, 0:384]
            outs[8][rows, pl.ds(128 * o, 128)] = full[group, core, part, :, 384:512]
            outs[9][rows, pl.ds(128 * o, 128)] = full[group, core, part, :, 512:640]
            outs[10][pl.ds(16 * o, 16), pl.ds(128 * part, 128)] = full[group, core, part, :, 640:768]

    last.wait_recv()
    for o in range(16):
        place(o)
    for copy in started:
        copy.wait_send()


def reduce_weights(grads, small, collective_id):
    bf = jnp.bfloat16
    shapes = [(96, 768)] * 8 + [(96, 2048)] * 2 + [(256, 768)]
    return pl.pallas_call(
        reduce_kernel,
        out_shape=[jax.ShapeDtypeStruct(shape, bf) for shape in shapes]
        + [jax.ShapeDtypeStruct(small.shape, small.dtype)],
        in_specs=[ANY, VMEM],
        out_specs=[VMEM] * 12,
        scratch_shapes=[
            pltpu.VMEM((6, 4, 4, 4, 16, 768), bf),
            pltpu.VMEM((6, 4, 4, 4, 16, 768), bf),
            pltpu.VMEM((6, 2, 4, 4, 16, 768), bf),
            pltpu.VMEM((6, 4, 4, 16, 768), bf),
            pltpu.VMEM((6, 2, 4, 16, 768), bf),
            pltpu.VMEM((6, 4, 16, 768), bf),
            pltpu.VMEM((6, 2, 16, 768), bf),
            pltpu.VMEM((6, 16, 768), bf),
            pltpu.VMEM((8, 2, 6, 16, 768), bf),
            pltpu.VMEM((7,) + small.shape, small.dtype),
            pltpu.SemaphoreType.DMA((6,)),
            pltpu.SemaphoreType.DMA((6, 10)),
            pltpu.SemaphoreType.DMA((6, 10)),
            pltpu.SemaphoreType.DMA((7,)),
            pltpu.SemaphoreType.DMA((7,)),
            pltpu.SemaphoreType.DMA((16,)),
            pltpu.SemaphoreType.DMA((16,)),
        ],
        compiler_params=pltpu.CompilerParams(
            collective_id=collective_id, has_side_effects=True, vmem_limit_bytes=56 * 2**20
        ),
        name="reduce_weights",
    )(grads, small)


def outer_kernel(acts, grads, third, gate, up, mixed, cot, out):
    def transposed_dot(left, right):
        return lax.dot_general(
            left, right, (((0,), (0,)), ((), ())), preferred_element_type=jnp.float32
        ).astype(jnp.bfloat16)

    attn = transposed_dot(acts[0], grads[0])
    wide = transposed_dot(third[...], jnp.concatenate([gate[...], up[...]], axis=1))
    down = transposed_dot(mixed[0], cot[...])
    for row in range(8):
        for part in range(6):
            begin = row * 96 + part * 16
            where = (0, part, row // 2, row % 2, 0, 0)
            out[where + (slice(None), slice(0, 384))] = attn[begin : begin + 16]
            out[where + (slice(None), slice(384, 640))] = wide[begin : begin + 16]
            out[where + (slice(None), slice(640, 768))] = down[
                row * 16 : row * 16 + 16, part * 128 : part * 128 + 128
            ]


def outer_products(acts, grads, third, gate, up, mixed, cot):
    tokens = third.shape[0]
    mixed_cut = mixed.reshape(tokens, 8, 16, 16).transpose(2, 0, 1, 3).reshape(16, tokens, 128)
    out = pl.pallas_call(
        outer_kernel,
        grid=(16,),
        out_shape=jax.ShapeDtypeStruct((2, 6, 4, 2, 2, 4, 16, 768), jnp.bfloat16),
        in_specs=[
            pl.BlockSpec((1, tokens, 768), lambda o: (o // 2, 0, 0)),
            pl.BlockSpec((1, tokens, 384), lambda o: (o // 2, 0, o % 2)),
            pl.BlockSpec((tokens, 768), lambda o: (0, 0)),
            pl.BlockSpec((tokens, 128), lambda o: (0, o)),
            pl.BlockSpec((tokens, 128), lambda o: (0, o)),
            pl.BlockSpec((1, tokens, 128), lambda o: (o, 0, 0)),
            pl.BlockSpec((tokens, 768), lambda o: (0, 0)),
        ],
        out_specs=pl.BlockSpec(
            (1, 6, 4, 2, 1, 1, 16, 768),
            lambda o: (o % 2, 0, 0, 0, o // 8, (o // 2) % 4, 0, 0),
        ),
        compiler_params=pltpu.CompilerParams(vmem_limit_bytes=32 * 2**20),
        name="outer_products",
    )(acts, grads, third, gate, up, mixed_cut, cot)
    return out.reshape(2, 6, 4, 4, 4, 16, 768)
EPSILON = 1e-06
NEGATIVE = -1e30
PRECISE = lax.Precision.HIGHEST


def rms_norm(values, gain):
    return values * lax.rsqrt(jnp.mean(values * values, axis=-1, keepdims=True) + EPSILON) * gain


def gated_gelu(gate_act, up_act):
    return jax.nn.gelu(gate_act, approximate=True) * up_act


def project(activity, weight):
    return jnp.einsum("scd,df->scf", activity, weight, preferred_element_type=jnp.float32)


def project_back(gradient, weight):
    return jnp.einsum("scf,df->scd", gradient, weight, preferred_element_type=jnp.float32)


def outer_sum(activity, gradient):
    return jnp.einsum("scd,scf->df", activity, gradient, preferred_element_type=jnp.float32)


def split_heads(activity, head_count):
    return activity.reshape(
        activity.shape[0], activity.shape[1], head_count, activity.shape[2] // head_count
    )


def join_heads(activity):
    return activity.reshape(
        activity.shape[0], activity.shape[1], activity.shape[2] * activity.shape[3]
    )


def toeplitz(vector, row_count, key_count):
    head_count, span = vector.shape
    reverse = vector[:, ::-1]
    tiled = jnp.tile(reverse, (1, row_count + 1))
    flat = tiled[:, row_count - 1 : row_count - 1 + row_count * (span - 1)]
    return flat.reshape(head_count, row_count, span - 1)[:, :, :key_count]


def diagonal_sums(block, span):
    head_count, row_count, key_count = block.shape
    widened = jnp.pad(block, ((0, 0), (0, 0), (0, span - 1 - key_count)))
    widened = widened.reshape(head_count, row_count * (span - 1))
    placed = jnp.pad(widened, ((0, 0), (row_count - 1, span + 1))).reshape(
        head_count, row_count + 1, span
    )
    return jnp.sum(placed, axis=1)[:, ::-1]


def causal_bias(bias_info, query_begin, row_count, key_begin, key_count):
    bias_pad, margin = bias_info
    span = row_count + key_count - 1
    slice_start = margin + query_begin - key_begin - (key_count - 1)
    vector = lax.dynamic_slice_in_dim(bias_pad, slice_start, span, 1)
    bias_block = toeplitz(vector, row_count, key_count)[None]
    query_pos = query_begin + jnp.arange(row_count, dtype=jnp.int32)
    key_pos = key_begin + jnp.arange(key_count, dtype=jnp.int32)
    allowed = (query_pos[:, None] >= key_pos[None, :])[None, None]
    return (bias_block, allowed, slice_start)


def make_fold(queries, query_begin, bias_info):

    def fold_step(running, pieces, begin_row):
        key_block, value_block = pieces
        row_max, row_sum, weighted = running
        scores = jnp.einsum(
            "sqhe,skhe->shqk", queries, key_block, preferred_element_type=jnp.float32
        )
        if bias_info is not None:
            bias_block, allowed, unused = causal_bias(
                bias_info, query_begin, queries.shape[1], begin_row, key_block.shape[1]
            )
            scores = jnp.where(allowed, scores + bias_block, NEGATIVE)
        new_max = jnp.maximum(row_max, jnp.max(scores, axis=-1))
        unscaled = jnp.exp(scores - new_max[..., None])
        if bias_info is not None:
            unscaled = jnp.where(allowed, unscaled, 0.0)
        row_sum = jnp.sum(unscaled, axis=-1)
        weighted = jnp.einsum(
            "shqk,skhe->shqe",
            unscaled.astype(jnp.bfloat16),
            value_block,
            preferred_element_type=jnp.float32,
        )
        return (new_max, row_sum, weighted)

    return fold_step


def finish_rows(running):
    row_max, row_sum, weighted = running
    out_heads = jnp.transpose(weighted / row_sum[..., None], (0, 2, 1, 3))
    return (out_heads, row_max + jnp.log(row_sum))


def attend_back(queries, out_heads, grad_heads, row_lse, pair, bias_info, query_begin):
    key_all, value_all = pair
    seq_count, row_count, head_count, head_size = queries.shape
    key_total = key_all.shape[1]
    block_len = math.gcd(512, key_total)
    span = row_count + block_len - 1
    delta = jnp.transpose(jnp.sum(grad_heads.astype(jnp.float32) * out_heads, axis=-1), (0, 2, 1))

    def back_step(block_index, running):
        grad_query, grad_keys, grad_values, grad_offsets = running
        begin_row = block_index * block_len
        key_block = lax.dynamic_slice_in_dim(key_all, begin_row, block_len, 1)
        value_block = lax.dynamic_slice_in_dim(value_all, begin_row, block_len, 1)
        scores = jnp.einsum(
            "sqhe,skhe->shqk", queries, key_block, preferred_element_type=jnp.float32
        )
        if bias_info is not None:
            bias_block, allowed, slice_start = causal_bias(
                bias_info, query_begin, row_count, begin_row, block_len
            )
            scores = jnp.where(allowed, scores + bias_block, NEGATIVE)
        probs = jnp.exp(scores - row_lse[..., None])
        grad_probs = jnp.einsum(
            "sqhe,skhe->shqk", grad_heads, value_block, preferred_element_type=jnp.float32
        )
        grad_scores = (probs * (grad_probs - delta[..., None])).astype(jnp.bfloat16)
        grad_query = grad_query + jnp.einsum(
            "shqk,skhe->sqhe", grad_scores, key_block, preferred_element_type=jnp.float32
        )
        key_part = jnp.einsum(
            "shqk,sqhe->skhe", grad_scores, queries, preferred_element_type=jnp.float32
        )
        value_part = jnp.einsum(
            "shqk,sqhe->skhe",
            probs.astype(jnp.bfloat16),
            grad_heads,
            preferred_element_type=jnp.float32,
        )
        grad_keys = lax.dynamic_update_slice_in_dim(grad_keys, key_part, begin_row, 1)
        grad_values = lax.dynamic_update_slice_in_dim(grad_values, value_part, begin_row, 1)
        if bias_info is not None:
            summed = jnp.sum(grad_scores.astype(jnp.float32), axis=0)
            along = diagonal_sums(summed, span)
            current = lax.dynamic_slice_in_dim(grad_offsets, slice_start, span, 1)
            grad_offsets = lax.dynamic_update_slice_in_dim(
                grad_offsets, current + along, slice_start, 1
            )
        return (grad_query, grad_keys, grad_values, grad_offsets)

    key_shape = key_all.shape
    offset_shape = bias_info[0].shape if bias_info is not None else (1,)
    initial = (
        jnp.zeros(queries.shape, jnp.float32),
        jnp.zeros(key_shape, jnp.float32),
        jnp.zeros(key_shape, jnp.float32),
        jnp.zeros(offset_shape, jnp.float32),
    )
    return lax.fori_loop(0, key_total // block_len, back_step, initial)


def body(
    layer_input,
    encoder_states,
    cotangent,
    bucket_ids,
    bias_table,
    gain_first,
    gain_second,
    gain_third,
    self_query,
    self_key,
    self_value,
    self_output,
    cross_query,
    cross_key,
    cross_value,
    cross_output,
    gate_weight,
    up_weight,
    down_weight,
):
    head_count = bias_table.shape[1]
    bucket_count = bias_table.shape[0]
    seq_count, row_count, model_width = layer_input.shape
    head_size = model_width // head_count
    weights = gather_weights(
        (
            self_query, self_key, self_value, self_output,
            cross_query, cross_key, cross_value, cross_output,
            gate_weight, up_weight, down_weight,
        ),
        GATHER_PLAN,
        0,
    )
    position = lax.axis_index("ctx")
    query_begin = position * row_count
    distance_count = bucket_ids.shape[0]
    margin = 2 * distance_count
    table_hot = (bucket_ids[:, None] == jnp.arange(bucket_count, dtype=jnp.int32)[None, :]).astype(
        jnp.float32
    )
    bias_rows = jnp.dot(table_hot, bias_table, precision=PRECISE)
    bias_pad = jnp.pad(jnp.transpose(bias_rows), ((0, 0), (margin, margin)))
    bias_info = (bias_pad, margin)
    initial = (
        jnp.full((seq_count, head_count, row_count), NEGATIVE, jnp.float32),
        jnp.zeros((seq_count, head_count, row_count), jnp.float32),
        jnp.zeros((seq_count, head_count, row_count, head_size), jnp.float32),
    )
    residual = layer_input.astype(jnp.float32)
    normed, back_first = jax.vjp(rms_norm, residual, gain_first)
    normed_one = normed.astype(jnp.bfloat16)
    queries = split_heads(project(normed_one, weights[0]).astype(jnp.bfloat16), head_count)
    self_pair = (
        split_heads(project(normed_one, weights[1]).astype(jnp.bfloat16), head_count),
        split_heads(project(normed_one, weights[2]).astype(jnp.bfloat16), head_count),
    )
    self_fold = make_fold(queries, query_begin, bias_info)
    self_state = self_fold(
        initial,
        (
            lax.all_gather(self_pair[0], "ctx", axis=1, tiled=True),
            lax.all_gather(self_pair[1], "ctx", axis=1, tiled=True),
        ),
        jnp.int32(0),
    )
    self_heads, self_lse = finish_rows(self_state)
    attended = join_heads(self_heads).astype(jnp.bfloat16)
    middle = residual + project(attended, weights[3])
    normed, back_second = jax.vjp(rms_norm, middle, gain_second)
    normed_two = normed.astype(jnp.bfloat16)
    cross_queries = split_heads(project(normed_two, weights[4]).astype(jnp.bfloat16), head_count)
    cross_pair = (
        split_heads(project(encoder_states, weights[5]).astype(jnp.bfloat16), head_count),
        split_heads(project(encoder_states, weights[6]).astype(jnp.bfloat16), head_count),
    )
    cross_fold = make_fold(cross_queries, query_begin, None)
    cross_state = cross_fold(
        initial,
        (
            lax.all_gather(cross_pair[0], "ctx", axis=1, tiled=True),
            lax.all_gather(cross_pair[1], "ctx", axis=1, tiled=True),
        ),
        jnp.int32(0),
    )
    cross_heads, cross_lse = finish_rows(cross_state)
    crossed = join_heads(cross_heads).astype(jnp.bfloat16)
    after_cross = middle + project(crossed, weights[7])
    normed, back_third = jax.vjp(rms_norm, after_cross, gain_third)
    normed_three = normed.astype(jnp.bfloat16)
    gate_act = project(normed_three, weights[8])
    up_act = project(normed_three, weights[9])
    mixed_act, back_mix = jax.vjp(gated_gelu, gate_act, up_act)
    mixed_low = mixed_act.astype(jnp.bfloat16)
    final = after_cross + project(mixed_low, weights[10])
    layer_output = final.astype(jnp.bfloat16)
    grad_gate, grad_up = back_mix(project_back(cotangent, weights[10]))
    grad_gate = grad_gate.astype(jnp.bfloat16)
    grad_up = grad_up.astype(jnp.bfloat16)
    grad_normed = project_back(grad_gate, weights[8]) + project_back(grad_up, weights[9])
    grad_back, grad_gain_three = back_third(grad_normed)
    grad_after = cotangent.astype(jnp.float32) + grad_back
    branch_after = grad_after.astype(jnp.bfloat16)
    grad_crossed = project_back(branch_after, weights[7]).astype(jnp.bfloat16)
    grad_cross_heads = split_heads(grad_crossed, head_count)
    cross_all = (
        lax.all_gather(cross_pair[0], "ctx", axis=1, tiled=True),
        lax.all_gather(cross_pair[1], "ctx", axis=1, tiled=True),
    )
    cross_back = attend_back(
        cross_queries, cross_heads, grad_cross_heads, cross_lse, cross_all, None, query_begin
    )
    cross_kv_sum = (
        lax.psum_scatter(
            cross_back[1].astype(jnp.bfloat16), "ctx", scatter_dimension=1, tiled=True
        ).astype(jnp.float32),
        lax.psum_scatter(
            cross_back[2].astype(jnp.bfloat16), "ctx", scatter_dimension=1, tiled=True
        ).astype(jnp.float32),
    )
    grad_cquery = join_heads(cross_back[0]).astype(jnp.bfloat16)
    grad_ckeys = join_heads(cross_kv_sum[0]).astype(jnp.bfloat16)
    grad_cvalues = join_heads(cross_kv_sum[1]).astype(jnp.bfloat16)
    grad_encoder = project_back(grad_ckeys, weights[5]) + project_back(grad_cvalues, weights[6])
    grad_back, grad_gain_two = back_second(project_back(grad_cquery, weights[4]))
    grad_middle = grad_after + grad_back
    branch_grad = grad_middle.astype(jnp.bfloat16)
    grad_attended = project_back(branch_grad, weights[3]).astype(jnp.bfloat16)
    grad_self_heads = split_heads(grad_attended, head_count)
    self_all = (
        lax.all_gather(self_pair[0], "ctx", axis=1, tiled=True),
        lax.all_gather(self_pair[1], "ctx", axis=1, tiled=True),
    )
    self_back = attend_back(
        queries, self_heads, grad_self_heads, self_lse, self_all, bias_info, query_begin
    )
    self_kv_sum = (
        lax.psum_scatter(
            self_back[1].astype(jnp.bfloat16), "ctx", scatter_dimension=1, tiled=True
        ).astype(jnp.float32),
        lax.psum_scatter(
            self_back[2].astype(jnp.bfloat16), "ctx", scatter_dimension=1, tiled=True
        ).astype(jnp.float32),
    )
    grad_queries = join_heads(self_back[0]).astype(jnp.bfloat16)
    grad_keys = join_heads(self_kv_sum[0]).astype(jnp.bfloat16)
    grad_values = join_heads(self_kv_sum[1]).astype(jnp.bfloat16)
    grad_normed = (
        project_back(grad_queries, weights[0])
        + project_back(grad_keys, weights[1])
        + project_back(grad_values, weights[2])
    )
    grad_back, grad_gain_one = back_first(grad_normed)
    grad_input = grad_middle + grad_back
    offset_grads = self_back[3][:, margin : margin + distance_count]
    local_table = jnp.transpose(jnp.dot(offset_grads, table_hot, precision=PRECISE))
    small = jnp.concatenate(
        [grad_gain_one, grad_gain_two, grad_gain_three, local_table.reshape(-1)]
    )
    small = jnp.pad(small, (0, 24 * 128 - small.shape[0])).reshape(24, 128)
    partials = outer_products(
        jnp.concatenate(
            [normed_one, normed_one, normed_one, attended, normed_two, encoder_states, encoder_states, crossed]
        ),
        jnp.concatenate(
            [grad_queries, grad_keys, grad_values, branch_grad, grad_cquery, grad_ckeys, grad_cvalues, branch_after]
        ),
        normed_three[0],
        grad_gate[0],
        grad_up[0],
        mixed_low[0],
        cotangent[0],
    )
    *shards, sums = reduce_weights(partials, small, 1)
    sums = sums.reshape(-1)
    width = model_width
    return (
        layer_output,
        grad_input,
        grad_encoder,
        sums[3 * width : 3 * width + bucket_count * head_count].reshape(bucket_count, head_count),
        sums[:width],
        sums[width : 2 * width],
        sums[2 * width : 3 * width],
    ) + tuple(shard.astype(jnp.float32) for shard in shards)


def solution(mesh):
    placed = (
        P("dp", "ctx", None),
        P("dp", "ctx", None),
        P("dp", "ctx", None),
        P(),
        P(),
        P(),
        P(),
        P(),
        P("dp", None),
        P("dp", None),
        P("dp", None),
        P("dp", None),
        P("dp", None),
        P("dp", None),
        P("dp", None),
        P("dp", None),
        P("dp", None),
        P("dp", None),
        P("dp", None),
    )
    return jax.shard_map(
        body,
        mesh=mesh,
        in_specs=placed,
        out_specs=(
            P("dp", "ctx", None),
            P("dp", "ctx", None),
            P("dp", "ctx", None),
            P(),
            P(),
            P(),
            P(),
            P("dp", None),
            P("dp", None),
            P("dp", None),
            P("dp", None),
            P("dp", None),
            P("dp", None),
            P("dp", None),
            P("dp", None),
            P("dp", None),
            P("dp", None),
            P("dp", None),
        ),
        check_vma=False,
    )
```

```python
import functools
import math
import jax
import jax.numpy as jnp
from jax import lax
from jax.experimental import pallas as pl
from jax.experimental.pallas import tpu as pltpu
from jax.sharding import PartitionSpec as P

MESH = pl.DeviceIdType.MESH
ANY = pl.BlockSpec(memory_space=pl.ANY)
VMEM = pl.BlockSpec(memory_space=pltpu.VMEM)


class Place:
    def __init__(self):
        c = lax.axis_index("ctx")
        d = lax.axis_index("dp")
        self.c, self.d = c, d
        self.x_hi = c // 8
        self.z = (c // 2) % 4
        self.core = c % 2
        self.y = d // 2
        self.x_lo = d % 2
        self.y_a = self.y + 1 - 2 * (self.y % 2)
        self.y_b = 3 - self.y
        self.y_ab = 3 - self.y_a
        self.z_a = self.z + 1 - 2 * (self.z % 2)
        self.z_b = 3 - self.z
        self.z_ab = 3 - self.z_a
        far_lo, far_hi = 1 - self.x_lo, 1 - self.x_hi
        self.x = self.x_lo * 2 + self.x_hi
        self.x_a = far_lo * 2 + self.x_hi
        self.x_b = far_lo * 2 + far_hi
        self.x_ab = self.x_lo * 2 + far_hi
        same = self.x_hi * 8 + self.z * 2 + self.core
        self.dev = {
            "core": (self.x_hi * 8 + self.z * 2 + 1 - self.core, d),
            "ya": (same, self.y_a * 2 + self.x_lo),
            "yb": (same, self.y_b * 2 + self.x_lo),
            "za": (self.x_hi * 8 + self.z_a * 2 + self.core, d),
            "zb": (self.x_hi * 8 + self.z_b * 2 + self.core, d),
            "xa": (same, self.y * 2 + far_lo),
            "xb": (far_hi * 8 + self.z * 2 + self.core, self.y * 2 + far_lo),
            "xab": (far_hi * 8 + self.z * 2 + self.core, d),
        }

    def greet(self, names):
        barrier = pltpu.get_barrier_semaphore()
        for name in names:
            pl.semaphore_signal(
                barrier, inc=1, device_id=self.dev[name], device_id_type=MESH
            )
        pl.semaphore_wait(barrier, len(names))

    def send(self, name, src, dst, send_sem, recv_sem):
        copy = pltpu.make_async_remote_copy(
            src_ref=src,
            dst_ref=dst,
            send_sem=send_sem,
            recv_sem=recv_sem,
            device_id=self.dev[name],
            device_id_type=MESH,
        )
        copy.start()
        return copy


GATHER_PLAN = (
    ((0, "pair", 0), (8, "za", 0), (9, "zb", 0)),
    ((1, "pair", 0), (8, "za", 1), (9, "zb", 1)),
    ((2, "pair", 0), (3, "za", 0), (10, "zb", 0)),
    ((5, "pair", 0), (4, "za", 0), (10, "zb", 1)),
    ((6, "pair", 0), (7, "za", 0), (10, "zb", 2)),
)


class Chain:
    def __init__(self, me, source, target, kind, half, piece, pieces, sems):
        rows, cols = source.shape
        width = cols // 2 // pieces
        self.me, self.source, self.target, self.kind = me, source, target, kind
        self.sems, self.slot, self.copies = sems, 0, []
        self.all_rows = pl.ds(0, rows)
        if kind == "pair":
            self.rows = pl.ds(half * (rows // 2), rows // 2)
            self.all_rows = self.rows
            flip = half == 1
        else:
            bit = me.z % 2 if kind == "za" else me.z // 2
            self.rows = pl.ds(pl.multiple_of(bit * (rows // 2), 16), rows // 2)
            flip = kind == "zb"
        self.cols = pl.ds(pl.multiple_of(me.core * (cols // 2) + piece * width, 128), width)
        self.other = pl.ds(pl.multiple_of((1 - me.core) * (cols // 2) + piece * width, 128), width)
        self.first, self.second = ("yb", "ya") if flip else ("ya", "yb")
        self.near = me.y_b if flip else me.y_a
        self.side = "xb" if flip else "xa"
        self.stages = 4 if kind == "pair" else 5

    def go(self, name, src, dst):
        send_sem, recv_sem, index = self.sems
        copy = self.me.send(
            name, src, dst, send_sem.at[index, self.slot], recv_sem.at[index, self.slot]
        )
        self.slot += 1
        self.copies.append(copy)
        return copy

    def run(self, stage):
        me, out = self.me, self.target
        if stage == 0:
            mine = self.source.at[self.rows, self.cols]
            spot = out.at[me.y, me.x_lo, self.rows, self.cols]
            self.first_copy = self.go(self.first, mine, spot)
            self.second_copy = self.go(self.second, mine, spot)
            self.own_copy = self.go(
                "core",
                self.source.at[self.rows, self.other],
                out.at[me.y, me.x_lo, self.rows, self.other],
            )
        elif stage == 1:
            self.first_copy.wait_recv()
            got = out.at[self.near, me.x_lo, self.rows, self.cols]
            self.third_copy = self.go(self.second, got, got)
        elif stage == 2:
            self.second_copy.wait_recv()
            self.own_copy.wait_recv()
            self.third_copy.wait_recv()
            got = out.at[:, me.x_lo, self.rows, self.cols]
            self.last = self.go(self.side, got, got)
        elif stage == 3 and self.kind != "pair":
            self.last.wait_recv()
            got = out.at[:, :, self.rows, self.cols]
            self.last = self.go(self.kind, got, got)
        elif stage == self.stages - 1:
            self.last.wait_recv()
            got = out.at[:, :, self.all_rows, self.cols]
            self.last = self.go("core", got, got)
        elif stage == self.stages:
            self.last.wait_recv()


def gather_kernel(count, plan, *refs):
    ins, outs = refs[:count], refs[count : 2 * count]
    send_sem, recv_sem = refs[2 * count :]
    me = Place()
    me.greet(("ya", "yb", "xa", "xb", "za", "zb", "core"))
    pieces = {}
    for group in plan:
        for array, kind, piece in group:
            pieces[array] = max(pieces.get(array, 0), piece + 1)
    groups = []
    index = 0
    for group in plan:
        chains = []
        for array, kind, piece in group:
            for half in range(2 if kind == "pair" else 1):
                chains.append(
                    Chain(
                        me, ins[array], outs[array], kind, half, piece, pieces[array],
                        (send_sem, recv_sem, index),
                    )
                )
                index += 1
        groups.append(chains)
    for chain in groups[0]:
        chain.run(0)
    for tick in range(1, len(groups) + 6):
        for stage in (5, 4, 3, 2, 1, 0):
            spot = tick - stage
            if stage == 0 and tick < len(groups):
                for chain in groups[tick]:
                    chain.run(0)
            elif stage > 0 and 0 <= spot < len(groups):
                for chain in groups[spot]:
                    chain.run(stage)
    for chains in groups:
        for chain in chains:
            for copy in chain.copies:
                copy.wait_send()


def gather_weights(shards, plan, collective_id):
    count = len(shards)
    chains = sum(2 if kind == "pair" else 1 for group in plan for _, kind, _ in group)
    outs = pl.pallas_call(
        functools.partial(gather_kernel, count, plan),
        out_shape=[
            jax.ShapeDtypeStruct((4, 2) + shard.shape, shard.dtype) for shard in shards
        ],
        in_specs=[ANY] * count,
        out_specs=[ANY] * count,
        scratch_shapes=[
            pltpu.SemaphoreType.DMA((chains, 7)),
            pltpu.SemaphoreType.DMA((chains, 7)),
        ],
        compiler_params=pltpu.CompilerParams(collective_id=collective_id, has_side_effects=True),
        name="gather_weights",
    )(*shards)
    return [out.reshape(8 * out.shape[2], out.shape[3]) for out in outs]

AXES = ("y", "x", "z")


def reduce_kernel(
    grads, small, *refs
):
    outs, small_out = refs[:11], refs[11]
    (acc, r0, r1, r2, r3, r4, r5, r6, full, sm_in,
     load_sem, send_sem, recv_sem, sm_send, sm_recv, ag_send, ag_recv) = refs[12:]
    recvs = (r1, r2, r3, r4, r5, r6)
    me = Place()
    me.greet(("core", "ya", "yb", "xa", "xb", "za", "zb", "xab"))
    spots = {
        "y": (me.y, me.y_a, me.y_b, me.y_ab),
        "x": (me.x, me.x_a, me.x_b, me.x_ab),
        "z": (me.z, me.z_a, me.z_b, me.z_ab),
    }
    parts = range(6)
    started = []

    def go(name, src, dst, send, recv):
        copy = me.send(name, src, dst, send, recv)
        started.append(copy)
        return copy

    small_out[...] = small[...]
    small_steps = ("core", "ya", "yb", "xa", "xb", "za", "zb")
    small_copies = []

    def small_start(step):
        small_copies.append(
            me.send(small_steps[step], small_out, sm_in.at[step], sm_send.at[step], sm_recv.at[step])
        )

    def small_end(step):
        small_copies[step].wait()
        small_out[...] = small_out[...] + sm_in[step]

    small_start(0)

    def order(part):
        first = (part // 2) % 3
        return [AXES[(first + k) % 3] for k in range(3)]

    def region(part, picks):
        return (part,) + tuple(picks.get(axis, slice(None)) for axis in AXES)

    def at(ref, index):
        return ref.at[index]

    core_copies, loads = [], []
    for part in parts:
        core_copies.append(
            go("core", grads.at[1 - me.core, part], r0.at[part], send_sem.at[part, 0], recv_sem.at[part, 0])
        )
        load = pltpu.make_async_copy(grads.at[me.core, part], acc.at[part], load_sem.at[part])
        load.start()
        loads.append(load)

    def add(index, source, source_index):
        acc[index] = acc[index] + source[source_index]

    def dims(part):
        return ("a", "b") if part % 2 == 0 else ("b", "a")

    def add_first(part, picks):
        axis = order(part)[0]
        rest = [name for name in AXES if name != axis]

        def step(k, carry):
            index = region(part, {**picks, rest[0]: k})
            acc[index] = acc[index] + r0[index]
            return carry

        lax.fori_loop(0, 4, step, 0)

    pending = {}
    for part in parts:
        axis = order(part)[0]
        me_at, a_at, b_at, ab_at = spots[axis]
        first, second = dims(part)
        sent = (a_at, ab_at) if first == "a" else (b_at, ab_at)
        core_copies[part].wait_recv()
        loads[part].wait()
        pending[part] = []
        for slot, spot in enumerate(sent):
            add_first(part, {axis: spot})
            pending[part].append(
                go(
                    axis + first,
                    at(acc, region(part, {axis: spot})),
                    r1.at[part, slot],
                    send_sem.at[part, 1 + slot],
                    recv_sem.at[part, 1 + slot],
                )
            )
    small_end(0)
    small_start(1)
    for part in parts:
        axis = order(part)[0]
        me_at, a_at, b_at, ab_at = spots[axis]
        first, second = dims(part)
        kept = b_at if first == "a" else a_at
        add_first(part, {axis: kept})
        add_first(part, {axis: me_at})

    sem_at = {part: 3 for part in parts}

    def next_sem(part):
        sem_at[part] += 1
        return send_sem.at[part, sem_at[part] - 1], recv_sem.at[part, sem_at[part] - 1]

    for level in range(3):
        one, two = recvs[2 * level], recvs[2 * level + 1]
        for part in parts:
            axes = order(part)
            axis = axes[level]
            first, second = dims(part)
            me_at, a_at, b_at, ab_at = spots[axis]
            kept = b_at if first == "a" else a_at
            fixed = {name: spots[name][0] for name in axes[:level]}
            for copy in pending[part]:
                copy.wait_recv()
            add(region(part, {**fixed, axis: kept}), one, (part, 1))
            send, recv = next_sem(part)
            pending[part] = [
                go(axis + second, at(acc, region(part, {**fixed, axis: kept})), two.at[part], send, recv)
            ]
        for part in parts:
            axes = order(part)
            fixed = {name: spots[name][0] for name in axes[: level + 1]}
            add(region(part, fixed), one, (part, 0))
        small_end(2 * level + 1)
        small_start(2 * level + 2)
        for part in parts:
            axes = order(part)
            fixed = {name: spots[name][0] for name in axes[: level + 1]}
            for copy in pending[part]:
                copy.wait_recv()
            add(region(part, fixed), two, (part,))
            if level == 2:
                continue
            axis = axes[level + 1]
            first, second = dims(part)
            me_at, a_at, b_at, ab_at = spots[axis]
            sent = (a_at, ab_at) if first == "a" else (b_at, ab_at)
            pending[part] = []
            for slot, spot in enumerate(sent):
                send, recv = next_sem(part)
                pending[part].append(
                    go(
                        axis + first,
                        at(acc, region(part, {**fixed, axis: spot})),
                        recvs[2 * level + 2].at[part, slot],
                        send,
                        recv,
                    )
                )
        small_end(2 * level + 2)
        if level < 2:
            small_start(2 * level + 3)

    here = me.x_hi * 4 + me.z
    there = (1 - me.x_hi) * 4 + me.z
    for part in parts:
        full[here, me.core, part] = acc[part, me.y, me.x, me.z]
    used = [0]

    def pass_on(name, group, half):
        index = used[0]
        used[0] += 1
        src = full.at[group, me.core, pl.ds(3 * half, 3)]
        return go(name, src, src, ag_send.at[index], ag_recv.at[index])

    early = [pass_on("xab", here, half) for half in range(2)]
    near = [pass_on("za", here, 0), pass_on("zb", here, 1)]
    far = []
    for half in range(2):
        early[half].wait_recv()
        far.append(pass_on(("za", "zb")[half], there, half))
    base, base_far = me.x_hi * 4, (1 - me.x_hi) * 4
    ends = [pass_on("zb", here, 0), pass_on("za", here, 1)]
    ends += [pass_on("zb", there, 0), pass_on("za", there, 1)]
    for half in range(2):
        got = (me.z_a, me.z_b)[half]
        near[half].wait_recv()
        ends.append(pass_on(("zb", "za")[half], base + got, half))
    for half in range(2):
        got = (me.z_a, me.z_b)[half]
        far[half].wait_recv()
        ends.append(pass_on(("zb", "za")[half], base_far + got, half))
    for copy in ends:
        copy.wait_recv()
    last = go("core", full.at[:, me.core], full.at[:, me.core], ag_send.at[used[0]], ag_recv.at[used[0]])

    def place(o):
        group, core = o // 2, o % 2
        for part in parts:
            rows = pl.ds(16 * part, 16)
            outs[group][rows, pl.ds(core * 384, 384)] = full[group, core, part, :, 0:384]
            outs[8][rows, pl.ds(128 * o, 128)] = full[group, core, part, :, 384:512]
            outs[9][rows, pl.ds(128 * o, 128)] = full[group, core, part, :, 512:640]
            outs[10][pl.ds(16 * o, 16), pl.ds(128 * part, 128)] = full[group, core, part, :, 640:768]

    last.wait_recv()
    for o in range(16):
        place(o)
    for copy in started:
        copy.wait_send()


def reduce_weights(grads, small, collective_id):
    bf = jnp.bfloat16
    shapes = [(96, 768)] * 8 + [(96, 2048)] * 2 + [(256, 768)]
    return pl.pallas_call(
        reduce_kernel,
        out_shape=[jax.ShapeDtypeStruct(shape, bf) for shape in shapes]
        + [jax.ShapeDtypeStruct(small.shape, small.dtype)],
        in_specs=[ANY, VMEM],
        out_specs=[VMEM] * 12,
        scratch_shapes=[
            pltpu.VMEM((6, 4, 4, 4, 16, 768), bf),
            pltpu.VMEM((6, 4, 4, 4, 16, 768), bf),
            pltpu.VMEM((6, 2, 4, 4, 16, 768), bf),
            pltpu.VMEM((6, 4, 4, 16, 768), bf),
            pltpu.VMEM((6, 2, 4, 16, 768), bf),
            pltpu.VMEM((6, 4, 16, 768), bf),
            pltpu.VMEM((6, 2, 16, 768), bf),
            pltpu.VMEM((6, 16, 768), bf),
            pltpu.VMEM((8, 2, 6, 16, 768), bf),
            pltpu.VMEM((7,) + small.shape, small.dtype),
            pltpu.SemaphoreType.DMA((6,)),
            pltpu.SemaphoreType.DMA((6, 10)),
            pltpu.SemaphoreType.DMA((6, 10)),
            pltpu.SemaphoreType.DMA((7,)),
            pltpu.SemaphoreType.DMA((7,)),
            pltpu.SemaphoreType.DMA((16,)),
            pltpu.SemaphoreType.DMA((16,)),
        ],
        compiler_params=pltpu.CompilerParams(
            collective_id=collective_id, has_side_effects=True, vmem_limit_bytes=56 * 2**20
        ),
        name="reduce_weights",
    )(grads, small)


def outer_kernel(acts, grads, third, gate, up, mixed, cot, out):
    def transposed_dot(left, right):
        return lax.dot_general(
            left, right, (((0,), (0,)), ((), ())), preferred_element_type=jnp.float32
        ).astype(jnp.bfloat16)

    attn = transposed_dot(acts[0], grads[0])
    wide = transposed_dot(third[...], jnp.concatenate([gate[...], up[...]], axis=1))
    down = transposed_dot(mixed[0], cot[...])
    for row in range(8):
        for part in range(6):
            begin = row * 96 + part * 16
            where = (0, part, row // 2, row % 2, 0, 0)
            out[where + (slice(None), slice(0, 384))] = attn[begin : begin + 16]
            out[where + (slice(None), slice(384, 640))] = wide[begin : begin + 16]
            out[where + (slice(None), slice(640, 768))] = down[
                row * 16 : row * 16 + 16, part * 128 : part * 128 + 128
            ]


def outer_products(acts, grads, third, gate, up, mixed, cot):
    tokens = third.shape[0]
    mixed_cut = mixed.reshape(tokens, 8, 16, 16).transpose(2, 0, 1, 3).reshape(16, tokens, 128)
    out = pl.pallas_call(
        outer_kernel,
        grid=(16,),
        out_shape=jax.ShapeDtypeStruct((2, 6, 4, 2, 2, 4, 16, 768), jnp.bfloat16),
        in_specs=[
            pl.BlockSpec((1, tokens, 768), lambda o: (o // 2, 0, 0)),
            pl.BlockSpec((1, tokens, 384), lambda o: (o // 2, 0, o % 2)),
            pl.BlockSpec((tokens, 768), lambda o: (0, 0)),
            pl.BlockSpec((tokens, 128), lambda o: (0, o)),
            pl.BlockSpec((tokens, 128), lambda o: (0, o)),
            pl.BlockSpec((1, tokens, 128), lambda o: (o, 0, 0)),
            pl.BlockSpec((tokens, 768), lambda o: (0, 0)),
        ],
        out_specs=pl.BlockSpec(
            (1, 6, 4, 2, 1, 1, 16, 768),
            lambda o: (o % 2, 0, 0, 0, o // 8, (o // 2) % 4, 0, 0),
        ),
        compiler_params=pltpu.CompilerParams(vmem_limit_bytes=32 * 2**20),
        name="outer_products",
    )(acts, grads, third, gate, up, mixed_cut, cot)
    return out.reshape(2, 6, 4, 4, 4, 16, 768)

NEGATIVE = -1e30
TILES = 23
USED = 16


class Share(Place):
    def __init__(self):
        super().__init__()
        self.dev["zab"] = (self.x_hi * 8 + self.z_ab * 2 + self.core, self.d)
        self.mine = self.x_hi * 2 + self.core
        self.slot = self.c // 4
        rest = self.c % 4
        self.owner = rest + (self.slot % 2) * (3 - 2 * rest)
        self.at_home = self.owner == self.mine

    def block(self, slot):
        return 4 * slot + (self.mine if slot % 2 == 0 else 3 - self.mine)

    def worker(self, group):
        return (self.owner // 2) * 8 + group * 2 + self.owner % 2

    def greet_all(self):
        barrier = pltpu.get_barrier_semaphore()
        for step in range(1, 16):
            pl.semaphore_signal(
                barrier, inc=1, device_id=((self.c + step) % 16, self.d), device_id_type=MESH
            )
        pl.semaphore_wait(barrier, 15)

    def copy_to(self, ctx, src, dst, send_sem, recv_sem):
        return pltpu.make_async_remote_copy(
            src_ref=src,
            dst_ref=dst,
            send_sem=send_sem,
            recv_sem=recv_sem,
            device_id=(ctx, self.d),
            device_id_type=MESH,
        )


def spread_kernel(q_count, kv_count, *refs):
    n = q_count + kv_count
    ins, outs = refs[:n], refs[n : 2 * n]
    q_send, q_recv, kv_send, kv_recv = refs[2 * n :]
    me = Share()
    me.greet_all()
    groups = (me.z_a, me.z_b, me.z_ab)
    done = []

    def go(name, src, dst, index, slot):
        copy = me.send(name, src, dst, kv_send.at[index, slot], kv_recv.at[index, slot])
        done.append(copy)
        return copy

    first = []
    for index in range(kv_count):
        src, out = ins[q_count + index], outs[q_count + index]
        out[me.c] = src[me.z]
        across = [
            go(name, src.at[group], out.at[me.c], index, slot)
            for slot, (name, group) in enumerate(zip(("za", "zb", "zab"), groups))
        ]
        first.append(across)
    for index in range(q_count):
        src, out = ins[index], outs[index]
        for group in range(4):
            away = jnp.logical_not(jnp.logical_and(me.at_home, me.z == group))

            @pl.when(away)
            def _():
                me.copy_to(
                    me.worker(group), src.at[group], out.at[me.slot],
                    q_send.at[index, group], q_recv.at[index, me.slot],
                ).start()

        @pl.when(me.at_home)
        def _():
            out[me.slot] = src[me.z]

    second = []
    for index in range(kv_count):
        out = outs[q_count + index]
        pairs = []
        for step, group in enumerate((me.z,) + groups):
            if step:
                first[index][step - 1].wait_recv()
            block = me.x_hi * 8 + group * 2 + me.core
            pairs.append(go("xab", out.at[block], out.at[block], index, 3 + step))
            pairs.append(go("core", out.at[block], out.at[block], index, 7 + step))
        second.append(pairs)
    third = []
    for index in range(kv_count):
        out = outs[q_count + index]
        for step, group in enumerate((me.z,) + groups):
            second[index][2 * step].wait_recv()
            block = (1 - me.x_hi) * 8 + group * 2 + me.core
            third.append(go("core", out.at[block], out.at[block], index, 11 + step))
    for pairs in second:
        for copy in pairs[1::2]:
            copy.wait_recv()
    for copy in third:
        copy.wait_recv()
    for index in range(q_count):
        src, out = ins[index], outs[index]
        for group in range(4):
            away = jnp.logical_not(jnp.logical_and(me.at_home, me.z == group))

            @pl.when(away)
            def _():
                me.copy_to(
                    me.worker(group), src.at[group], out.at[me.slot],
                    q_send.at[index, group], q_recv.at[index, me.slot],
                ).wait_send()

        for slot in range(4):
            @pl.when(me.block(slot) != me.c)
            def _():
                me.copy_to(
                    me.block(slot), src.at[0], out.at[slot],
                    q_send.at[index, 0], q_recv.at[index, slot],
                ).wait_recv()

    for copy in done:
        copy.wait_send()


def spread(q_list, kv_list, collective_id):
    nq, nkv = len(q_list), len(kv_list)
    return pl.pallas_call(
        functools.partial(spread_kernel, nq, nkv),
        out_shape=[jax.ShapeDtypeStruct((4, 128, 256), jnp.bfloat16)] * nq
        + [jax.ShapeDtypeStruct((16, 128, 384), jnp.bfloat16)] * nkv,
        in_specs=[VMEM] * (nq + nkv),
        out_specs=[VMEM] * (nq + nkv),
        scratch_shapes=[
            pltpu.SemaphoreType.DMA((max(nq, 1), 4)),
            pltpu.SemaphoreType.DMA((max(nq, 1), 4)),
            pltpu.SemaphoreType.DMA((max(nkv, 1), 15)),
            pltpu.SemaphoreType.DMA((max(nkv, 1), 15)),
        ],
        compiler_params=pltpu.CompilerParams(
            collective_id=collective_id, has_side_effects=True, vmem_limit_bytes=32 * 2**20
        ),
        name="spread_%d_%d" % (nq, nkv),
    )(*q_list, *kv_list)


def collect_kernel(with_kv, *refs):
    if with_kv:
        (o_in, kv_in, o_out, kv_out, o_send, o_recv, kv_send, kv_recv,
         got_core, part, got_x, total) = refs
    else:
        o_in, o_out, o_send, o_recv = refs
    me = Share()
    me.greet_all()
    done = []
    if with_kv:
        def go(name, src, dst, slot):
            copy = me.send(name, src, dst, kv_send.at[slot], kv_recv.at[slot])
            done.append(copy)
            return copy

        near, far = me.x_hi * 4, (1 - me.x_hi) * 4
        to_core = [
            go("core", kv_in.at[pl.ds(begin, 4), 1 - me.core], got_core.at[pl.ds(begin, 4)], slot)
            for slot, begin in enumerate((far, near))
        ]
    for slot in range(4):
        @pl.when(me.block(slot) != me.c)
        def _():
            me.copy_to(
                me.block(slot), o_in.at[slot], o_out.at[me.z], o_send.at[slot], o_recv.at[me.z]
            ).start()

    @pl.when(me.at_home)
    def _():
        o_out[me.z] = o_in[me.slot]

    if with_kv:
        to_core[0].wait_recv()
        part[pl.ds(far, 4)] = kv_in[pl.ds(far, 4), me.core] + got_core[pl.ds(far, 4)]
        over_x = go("xab", part.at[pl.ds(far, 4)], got_x, 2)
        to_core[1].wait_recv()
        part[pl.ds(near, 4)] = kv_in[pl.ds(near, 4), me.core] + got_core[pl.ds(near, 4)]
        over_x.wait_recv()
        total[...] = part[pl.ds(near, 4)] + got_x[...]
        across = [
            go(name, total.at[group], kv_out.at[me.z], 3 + step)
            for step, (name, group) in enumerate(
                zip(("za", "zb", "zab"), (me.z_a, me.z_b, me.z_ab))
            )
        ]
        kv_out[me.z] = total[me.z]
        for copy in across:
            copy.wait_recv()
    for slot in range(4):
        @pl.when(me.block(slot) != me.c)
        def _():
            me.copy_to(
                me.block(slot), o_in.at[slot], o_out.at[me.z], o_send.at[slot], o_recv.at[me.z]
            ).wait_send()

    for group in range(4):
        away = jnp.logical_not(jnp.logical_and(me.at_home, me.z == group))

        @pl.when(away)
        def _():
            me.copy_to(
                me.worker(group), o_in.at[0], o_out.at[group], o_send.at[0], o_recv.at[group]
            ).wait_recv()

    for copy in done:
        copy.wait_send()


def collect(rows, pairs, collective_id):
    bf = jnp.bfloat16
    with_kv = pairs is not None
    shapes = [jax.ShapeDtypeStruct((4, 128, 256), bf)]
    scratch = [pltpu.SemaphoreType.DMA((4,)), pltpu.SemaphoreType.DMA((4,))]
    args = [rows]
    if with_kv:
        shapes.append(jax.ShapeDtypeStruct((4, 128, 384), bf))
        args.append(pairs.reshape(8, 2, 128, 384))
        scratch += [
            pltpu.SemaphoreType.DMA((6,)),
            pltpu.SemaphoreType.DMA((6,)),
            pltpu.VMEM((8, 128, 384), bf),
            pltpu.VMEM((8, 128, 384), bf),
            pltpu.VMEM((4, 128, 384), bf),
            pltpu.VMEM((4, 128, 384), bf),
        ]
    return pl.pallas_call(
        functools.partial(collect_kernel, with_kv),
        out_shape=shapes,
        in_specs=[VMEM] * len(args),
        out_specs=[VMEM] * len(shapes),
        scratch_shapes=scratch,
        compiler_params=pltpu.CompilerParams(
            collective_id=collective_id, has_side_effects=True, vmem_limit_bytes=32 * 2**20
        ),
        name="collect_kv" if with_kv else "collect",
    )(*args)


def dot_nn(left, right):
    return jnp.dot(left, right, preferred_element_type=jnp.float32)


def dot_nt(left, right):
    return lax.dot_general(
        left, right, (((1,), (1,)), ((), ())), preferred_element_type=jnp.float32
    )


def head_lanes(value, head):
    lane = lax.broadcasted_iota(jnp.int32, value.shape, 1)
    return jnp.where(lane // 64 == head, value, jnp.zeros_like(value))


def head_rows(value, head):
    row = lax.broadcasted_iota(jnp.int32, value.shape, 0)
    return jnp.where(row // 64 == head, value, jnp.zeros_like(value))


def bias_offset(pair, side, chunk):
    c = lax.axis_index("ctx")
    mine = (c // 8) * 2 + c % 2
    block = 8 * pair + (mine if side == 0 else 7 - mine)
    return pl.multiple_of((15 - block) * 128 + chunk * 256, 128)


def bias_at(wide, head, pair, chunk):
    return jnp.concatenate(
        [wide[head, pl.ds(bias_offset(pair, side, chunk), 256), :] for side in range(2)], axis=1
    )


def forward_kernel(causal, *refs):
    if causal:
        q, kv, waves, o_low, o_full, lse, wide, values_t, score, total = refs
        def build(head, carry):
            for tile in range(USED):
                row = jnp.broadcast_to(waves[head, tile : tile + 1, :], (128, 256))
                turned = pltpu.roll(row, 129, 1, stride=1, stride_axis=0)
                wide[head, tile * 128 : tile * 128 + 128, :] = turned[:, :128]
            wide[head, USED * 128 :, :] = jnp.full(
                ((TILES - USED) * 128, 128), NEGATIVE, jnp.float32
            )
            return carry

        lax.fori_loop(0, 3, build, 0)
    else:
        q, kv, o_low, o_full, lse, values_t, score, total = refs

    for chunk in range(8):
        values_t[chunk] = kv[2 * chunk : 2 * chunk + 2, :, 128:384].reshape(256, 256).T
    for pair in range(2):
        chunks = 4 if causal and pair == 0 else 8
        rows = q[2 * pair : 2 * pair + 2].reshape(256, 256)
        total[...] = jnp.zeros_like(total)

        def one_head(head, carry):
            masked = head_lanes(rows, head)

            top = jnp.full((8, 256), NEGATIVE, jnp.float32)
            for chunk in range(chunks):
                keys = kv[2 * chunk : 2 * chunk + 2, :, 0:256].reshape(256, 256)
                block = dot_nt(keys, masked)
                if causal:
                    block = block + bias_at(wide, head, pair, chunk)
                score[chunk] = block
                top = jnp.maximum(top, jnp.max(block.reshape(32, 8, 256), axis=0))
            top = jnp.max(top, axis=0, keepdims=True)
            summed = jnp.zeros((8, 256), jnp.float32)
            held = jnp.zeros((256, 256), jnp.float32)
            for chunk in range(chunks):
                expo = jnp.exp(score[chunk] - top)
                summed = summed + jnp.sum(expo.reshape(32, 8, 256), axis=0)
                held = held + dot_nn(values_t[chunk], expo.astype(jnp.bfloat16))
            summed = jnp.sum(summed, axis=0, keepdims=True)
            total[...] += head_rows(held * (1.0 / summed), head + 1)
            lse[head, pair] = top + jnp.log(summed)
            return carry

        lax.fori_loop(0, 3, one_head, 0)
        final = total[...].T.reshape(2, 128, 256)
        o_full[2 * pair : 2 * pair + 2] = final
        o_low[2 * pair : 2 * pair + 2] = final.astype(jnp.bfloat16)


def attend(q, kv, waves):
    causal = waves is not None
    shapes = [
        jax.ShapeDtypeStruct((4, 128, 256), jnp.bfloat16),
        jax.ShapeDtypeStruct((4, 128, 256), jnp.float32),
        jax.ShapeDtypeStruct((3, 2, 1, 256), jnp.float32),
    ]
    args = [q, kv]
    if causal:
        shapes.append(jax.ShapeDtypeStruct((3, TILES * 128, 128), jnp.float32))
        args.append(waves)
    return pl.pallas_call(
        functools.partial(forward_kernel, causal),
        out_shape=shapes,
        in_specs=[VMEM] * len(args),
        out_specs=[VMEM] * len(shapes),
        scratch_shapes=[
            pltpu.VMEM((8, 256, 256), jnp.bfloat16),
            pltpu.VMEM((8, 256, 256), jnp.float32),
            pltpu.VMEM((256, 256), jnp.float32),
        ],
        compiler_params=pltpu.CompilerParams(vmem_limit_bytes=40 * 2**20),
        name="attend_self" if causal else "attend_cross",
    )(*args)


def backward_kernel(causal, *refs):
    if causal:
        (q, kv, grad, o_full, lse, wide, dq, dkv, waves,
         keys_t, dk, dv, dq_t, turned, along) = refs
        along[...] = jnp.zeros_like(along)
    else:
        q, kv, grad, o_full, lse, dq, dkv, keys_t, dk, dv, dq_t, turned = refs
    dk[...] = jnp.zeros_like(dk)
    dv[...] = jnp.zeros_like(dv)

    for chunk in range(8):
        keys_t[chunk] = kv[2 * chunk : 2 * chunk + 2, :, 0:256].reshape(256, 256).T
    for pair in range(2):
        chunks = 4 if causal and pair == 0 else 8
        both = slice(2 * pair, 2 * pair + 2)
        rows = q[both].reshape(256, 256)
        grads = grad[both].reshape(256, 256)
        turned[...] = (grads.astype(jnp.float32) * o_full[both].reshape(256, 256)).T
        dq_t[...] = jnp.zeros_like(dq_t)

        def one_head(head, carry):
            masked = head_lanes(rows, head)
            masked_grads = head_lanes(grads, head + 1)
            delta = jnp.sum(head_rows(turned[...], head + 1), axis=0, keepdims=True)
            row_lse = lse[head, pair]

            held = jnp.zeros((256, 256), jnp.float32)
            for chunk in range(chunks):
                block = kv[2 * chunk : 2 * chunk + 2].reshape(256, 384)
                scores = dot_nt(block[:, 0:256], masked)
                if causal:
                    scores = scores + bias_at(wide, head, pair, chunk)
                probs = jnp.exp(scores - row_lse)
                grad_probs = dot_nt(block[:, 128:384], masked_grads)
                grad_scores = probs * (grad_probs - delta)
                low = grad_scores.astype(jnp.bfloat16)
                spot = slice(chunk * 256, chunk * 256 + 256)
                dk[spot] += dot_nn(low, masked)
                dv[spot] += dot_nn(probs.astype(jnp.bfloat16), masked_grads)
                if causal:
                    for side in range(2):
                        where = pl.ds(bias_offset(pair, side, chunk), 256)
                        along[head, where, :] += grad_scores[:, 128 * side : 128 * side + 128]
                held = held + dot_nn(keys_t[chunk], low)
            dq_t[...] += head_rows(held, head)
            return carry

        lax.fori_loop(0, 3, one_head, 0)
        dq[both] = dq_t[...].T.reshape(2, 128, 256).astype(jnp.bfloat16)

    def pack(block, carry):
        spot = pl.ds(pl.multiple_of(block * 128, 128), 128)
        key_part, value_part = dk[spot], dv[spot]
        dkv[block, :, 0:128] = key_part[:, 0:128].astype(jnp.bfloat16)
        dkv[block, :, 128:256] = (key_part[:, 128:256] + value_part[:, 0:128]).astype(jnp.bfloat16)
        dkv[block, :, 256:384] = value_part[:, 128:256].astype(jnp.bfloat16)
        return carry

    lax.fori_loop(0, 16, pack, 0)
    if causal:
        waves[...] = jnp.zeros_like(waves)

        def fold(head, carry):
            for tile in range(USED):
                value = along[head, tile * 128 : tile * 128 + 128, :]
                value = jnp.concatenate([value, jnp.zeros_like(value)], axis=1)
                count = 64
                while count >= 1:
                    value = pltpu.roll(value[:count], count, 1) + value[count:]
                    count //= 2
                waves[head, tile : tile + 1, :] = value
            return carry

        lax.fori_loop(0, 3, fold, 0)


def attend_back(q, kv, grad, o_full, lse, wide):
    causal = wide is not None
    shapes = [
        jax.ShapeDtypeStruct((4, 128, 256), jnp.bfloat16),
        jax.ShapeDtypeStruct((16, 128, 384), jnp.bfloat16),
    ]
    args = [q, kv, grad, o_full, lse]
    scratch = [
        pltpu.VMEM((8, 256, 256), jnp.bfloat16),
        pltpu.VMEM((2048, 256), jnp.float32),
        pltpu.VMEM((2048, 256), jnp.float32),
        pltpu.VMEM((256, 256), jnp.float32),
        pltpu.VMEM((256, 256), jnp.float32),
    ]
    if causal:
        shapes.append(jax.ShapeDtypeStruct((3, TILES, 256), jnp.float32))
        args.append(wide)
        scratch.append(pltpu.VMEM((3, TILES * 128, 128), jnp.float32))
    return pl.pallas_call(
        functools.partial(backward_kernel, causal),
        out_shape=shapes,
        in_specs=[VMEM] * len(args),
        out_specs=[VMEM] * len(shapes),
        scratch_shapes=scratch,
        compiler_params=pltpu.CompilerParams(vmem_limit_bytes=48 * 2**20),
        name="attend_back_self" if causal else "attend_back_cross",
    )(*args)


def to_groups(activity, before):
    cut = activity.reshape(activity.shape[0], 4, 192).transpose(1, 0, 2)
    return jnp.pad(cut, ((0, 0), (0, 0), (64, 0) if before else (0, 64)))


def from_groups(grouped, begin):
    cut = grouped[:, :, begin : begin + 192].transpose(1, 0, 2)
    return cut.reshape(cut.shape[0], 768)


def pair_groups(keys, values):
    cut = lambda activity: activity.reshape(activity.shape[0], 4, 192).transpose(1, 0, 2)
    return jnp.concatenate([cut(keys), cut(values)], axis=2)
EPSILON = 1e-06
PRECISE = lax.Precision.HIGHEST


def rms_norm(values, gain):
    return values * lax.rsqrt(jnp.mean(values * values, axis=-1, keepdims=True) + EPSILON) * gain


def gated_gelu(gate_act, up_act):
    return jax.nn.gelu(gate_act, approximate=True) * up_act


def project(activity, weight):
    return jnp.einsum("td,df->tf", activity, weight, preferred_element_type=jnp.float32)


def project_back(gradient, weight):
    return jnp.einsum("tf,df->td", gradient, weight, preferred_element_type=jnp.float32)


def body(
    layer_input,
    encoder_states,
    cotangent,
    bucket_ids,
    bias_table,
    gain_first,
    gain_second,
    gain_third,
    self_query,
    self_key,
    self_value,
    self_output,
    cross_query,
    cross_key,
    cross_value,
    cross_output,
    gate_weight,
    up_weight,
    down_weight,
):
    bucket_count, head_count = bias_table.shape
    width = layer_input.shape[-1]
    layer_input, encoder_states, cotangent = layer_input[0], encoder_states[0], cotangent[0]
    weights = gather_weights(
        (
            self_query, self_key, self_value, self_output,
            cross_query, cross_key, cross_value, cross_output,
            gate_weight, up_weight, down_weight,
        ),
        GATHER_PLAN,
        0,
    )
    low = jnp.bfloat16
    first_head = 3 * ((lax.axis_index("ctx") // 2) % 4)
    padded = jnp.pad(bucket_ids, (TILES * 128 - bucket_ids.shape[0] + 128, 0), constant_values=-1)
    last = padded.shape[0]
    ids = jnp.stack([padded[last - 255 - 128 * k - 0 : last - 128 * k] for k in range(TILES)])
    ids = jnp.pad(ids, ((0, 0), (0, 1)), constant_values=-1)
    hot = (ids[:, :, None] == jnp.arange(bucket_count, dtype=jnp.int32)).astype(jnp.float32)
    own_table = lax.dynamic_slice_in_dim(bias_table, first_head, 3, 1)
    waves = jnp.einsum("kxb,bh->hkx", hot, own_table, precision=PRECISE)
    waves = jnp.where((ids >= 0)[None], waves, NEGATIVE)

    residual = layer_input.astype(jnp.float32)
    normed, back_first = jax.vjp(rms_norm, residual, gain_first)
    normed_one = normed.astype(low)
    queries = project(normed_one, weights[0]).astype(low)
    keys = project(normed_one, weights[1]).astype(low)
    values = project(normed_one, weights[2]).astype(low)
    cross_keys = project(encoder_states, weights[5]).astype(low)
    cross_values = project(encoder_states, weights[6]).astype(low)
    self_q, self_kv, cross_kv = spread(
        [to_groups(queries, False)],
        [pair_groups(keys, values), pair_groups(cross_keys, cross_values)],
        2,
    )
    self_low, self_full, self_lse, wide = attend(self_q, self_kv, waves)
    attended = from_groups(collect(self_low, None, 3)[0], 64)
    middle = residual + project(attended, weights[3])
    normed, back_second = jax.vjp(rms_norm, middle, gain_second)
    normed_two = normed.astype(low)
    cross_queries = project(normed_two, weights[4]).astype(low)
    (cross_q,) = spread([to_groups(cross_queries, False)], [], 4)
    cross_low, cross_full, cross_lse = attend(cross_q, cross_kv, None)
    crossed = from_groups(collect(cross_low, None, 5)[0], 64)
    after_cross = middle + project(crossed, weights[7])
    normed, back_third = jax.vjp(rms_norm, after_cross, gain_third)
    normed_three = normed.astype(low)
    gate_act = project(normed_three, weights[8])
    up_act = project(normed_three, weights[9])
    mixed_act, back_mix = jax.vjp(gated_gelu, gate_act, up_act)
    mixed_low = mixed_act.astype(low)
    layer_output = (after_cross + project(mixed_low, weights[10])).astype(low)

    grad_gate, grad_up = back_mix(project_back(cotangent, weights[10]))
    grad_gate = grad_gate.astype(low)
    grad_up = grad_up.astype(low)
    grad_normed = project_back(grad_gate, weights[8]) + project_back(grad_up, weights[9])
    grad_back, grad_gain_three = back_third(grad_normed)
    grad_after = cotangent.astype(jnp.float32) + grad_back
    branch_after = grad_after.astype(low)
    grad_crossed = project_back(branch_after, weights[7]).astype(low)
    (cross_grads,) = spread([to_groups(grad_crossed, True)], [], 6)
    cross_dq, cross_dkv = attend_back(cross_q, cross_kv, cross_grads, cross_full, cross_lse, None)
    cross_dq, cross_dkv = collect(cross_dq, cross_dkv, 7)
    grad_cquery = from_groups(cross_dq, 0)
    grad_ckeys = from_groups(cross_dkv, 0)
    grad_cvalues = from_groups(cross_dkv, 192)
    grad_encoder = project_back(grad_ckeys, weights[5]) + project_back(grad_cvalues, weights[6])
    grad_back, grad_gain_two = back_second(project_back(grad_cquery, weights[4]))
    grad_middle = grad_after + grad_back
    branch_middle = grad_middle.astype(low)
    grad_attended = project_back(branch_middle, weights[3]).astype(low)
    (self_grads,) = spread([to_groups(grad_attended, True)], [], 8)
    self_dq, self_dkv, grad_waves = attend_back(
        self_q, self_kv, self_grads, self_full, self_lse, wide
    )
    self_dq, self_dkv = collect(self_dq, self_dkv, 9)
    grad_queries = from_groups(self_dq, 0)
    grad_keys = from_groups(self_dkv, 0)
    grad_values = from_groups(self_dkv, 192)
    grad_normed = (
        project_back(grad_queries, weights[0])
        + project_back(grad_keys, weights[1])
        + project_back(grad_values, weights[2])
    )
    grad_back, grad_gain_one = back_first(grad_normed)
    grad_input = grad_middle + grad_back
    own_grads = jnp.einsum("kxb,hkx->bh", hot, grad_waves, precision=PRECISE)
    local_table = lax.dynamic_update_slice_in_dim(
        jnp.zeros_like(bias_table), own_grads, first_head, 1
    )
    small = jnp.concatenate(
        [grad_gain_one, grad_gain_two, grad_gain_three, local_table.reshape(-1)]
    )
    small = jnp.pad(small, (0, 24 * 128 - small.shape[0])).reshape(24, 128)
    partials = outer_products(
        jnp.stack(
            [normed_one, normed_one, normed_one, attended, normed_two, encoder_states, encoder_states, crossed]
        ),
        jnp.stack(
            [grad_queries, grad_keys, grad_values, branch_middle, grad_cquery, grad_ckeys, grad_cvalues, branch_after]
        ),
        normed_three,
        grad_gate,
        grad_up,
        mixed_low,
        cotangent,
    )
    *shards, sums = reduce_weights(partials, small, 1)
    sums = sums.reshape(-1)
    return (
        layer_output[None],
        grad_input[None],
        grad_encoder[None],
        sums[3 * width : 3 * width + bucket_count * head_count].reshape(bucket_count, head_count),
        sums[:width],
        sums[width : 2 * width],
        sums[2 * width : 3 * width],
    ) + tuple(shard.astype(jnp.float32) for shard in shards)


def solution(mesh):
    placed = (
        P("dp", "ctx", None),
        P("dp", "ctx", None),
        P("dp", "ctx", None),
        P(),
        P(),
        P(),
        P(),
        P(),
        P("dp", None),
        P("dp", None),
        P("dp", None),
        P("dp", None),
        P("dp", None),
        P("dp", None),
        P("dp", None),
        P("dp", None),
        P("dp", None),
        P("dp", None),
        P("dp", None),
    )
    return jax.shard_map(
        body,
        mesh=mesh,
        in_specs=placed,
        out_specs=(
            P("dp", "ctx", None),
            P("dp", "ctx", None),
            P("dp", "ctx", None),
            P(),
            P(),
            P(),
            P(),
            P("dp", None),
            P("dp", None),
            P("dp", None),
            P("dp", None),
            P("dp", None),
            P("dp", None),
            P("dp", None),
            P("dp", None),
            P("dp", None),
            P("dp", None),
            P("dp", None),
        ),
        check_vma=False,
    )
```

```python
import functools
import math
import jax
import jax.numpy as jnp
from jax import lax
from jax.experimental import pallas as pl
from jax.experimental.pallas import tpu as pltpu
from jax.sharding import PartitionSpec as P

MESH = pl.DeviceIdType.MESH
VMEM_BYTES = 62 * 2**20
ANY = pl.BlockSpec(memory_space=pl.ANY)
HBM = pl.BlockSpec(memory_space=pltpu.HBM)
VMEM = pl.BlockSpec(memory_space=pltpu.VMEM)


class Place:
    def __init__(self):
        c = lax.axis_index("ctx")
        d = lax.axis_index("dp")
        self.c, self.d = c, d
        self.x_hi = c // 8
        self.z = (c // 2) % 4
        self.core = c % 2
        self.y = d // 2
        self.x_lo = d % 2
        self.y_a = self.y + 1 - 2 * (self.y % 2)
        self.y_b = 3 - self.y
        self.y_ab = 3 - self.y_a
        self.z_a = self.z + 1 - 2 * (self.z % 2)
        self.z_b = 3 - self.z
        self.z_ab = 3 - self.z_a
        far_lo, far_hi = 1 - self.x_lo, 1 - self.x_hi
        self.x = self.x_lo * 2 + self.x_hi
        self.x_a = far_lo * 2 + self.x_hi
        self.x_b = far_lo * 2 + far_hi
        self.x_ab = self.x_lo * 2 + far_hi
        same = self.x_hi * 8 + self.z * 2 + self.core
        self.dev = {
            "core": (self.x_hi * 8 + self.z * 2 + 1 - self.core, d),
            "ya": (same, self.y_a * 2 + self.x_lo),
            "yb": (same, self.y_b * 2 + self.x_lo),
            "za": (self.x_hi * 8 + self.z_a * 2 + self.core, d),
            "zb": (self.x_hi * 8 + self.z_b * 2 + self.core, d),
            "xa": (same, self.y * 2 + far_lo),
            "xb": (far_hi * 8 + self.z * 2 + self.core, self.y * 2 + far_lo),
            "xab": (far_hi * 8 + self.z * 2 + self.core, d),
        }

    def greet(self, names):
        barrier = pltpu.get_barrier_semaphore()
        for name in names:
            pl.semaphore_signal(
                barrier, inc=1, device_id=self.dev[name], device_id_type=MESH
            )
        pl.semaphore_wait(barrier, len(names))

    def send(self, name, src, dst, send_sem, recv_sem):
        copy = pltpu.make_async_remote_copy(
            src_ref=src,
            dst_ref=dst,
            send_sem=send_sem,
            recv_sem=recv_sem,
            device_id=self.dev[name],
            device_id_type=MESH,
        )
        copy.start()
        return copy


EARLY_PLAN = (
    ((0, "pair", 0), (1, "pair", 0), (2, "pair", 0)),
    ((3, "pair", 0), (4, "pair", 0)),
)
LATE_PLAN = (((0, "zb", 0), (1, "za", 0)), ((2, "pair", 0),))
FEED_PLAN = (((0, "za", 0), (1, "zb", 0), (2, "pair", 0)),)


class Chain:
    def __init__(self, me, source, target, kind, half, piece, pieces, sems):
        rows, cols = source.shape[-2:]
        width = cols // 2 // pieces
        self.me, self.source, self.target, self.kind = me, source, target, kind
        self.sems, self.slot, self.copies = sems, 0, []
        self.all_rows = pl.ds(0, rows)
        if kind == "pair":
            self.rows = pl.ds(half * (rows // 2), rows // 2)
            self.all_rows = self.rows
            flip = half == 1
        else:
            bit = me.z % 2 if kind == "za" else me.z // 2
            self.rows = pl.ds(pl.multiple_of(bit * (rows // 2), 16), rows // 2)
            flip = kind == "zb"
        self.cols = pl.ds(pl.multiple_of(me.core * (cols // 2) + piece * width, 128), width)
        self.other = pl.ds(pl.multiple_of((1 - me.core) * (cols // 2) + piece * width, 128), width)
        self.first, self.second = ("yb", "ya") if flip else ("ya", "yb")
        self.near = me.y_b if flip else me.y_a
        self.side = "xb" if flip else "xa"
        self.stages = 4 if kind == "pair" else 5

    def go(self, name, src, dst):
        send_sem, recv_sem, index = self.sems
        copy = self.me.send(
            name, src, dst, send_sem.at[index, self.slot], recv_sem.at[index, self.slot]
        )
        self.slot += 1
        self.copies.append(copy)
        return copy

    def hop(self, name):
        me, out = self.me, self.target
        if name == "side":
            got = out.at[:, me.x_lo, self.rows, self.cols]
            return self.go(self.side, got, got)
        if name == "core":
            got = out.at[:, :, self.all_rows, self.cols]
            return self.go("core", got, got)
        got = out.at[:, :, self.rows, self.cols]
        return self.go(self.kind, got, got)

    def run(self, stage):
        me, out = self.me, self.target
        if stage == 0:
            mine = self.source.at[self.rows, self.cols]
            spot = out.at[me.y, me.x_lo, self.rows, self.cols]
            self.first_copy = self.go(self.first, mine, spot)
            self.second_copy = self.go(self.second, mine, spot)
            self.own_copy = self.go(
                "core",
                self.source.at[self.rows, self.other],
                out.at[me.y, me.x_lo, self.rows, self.other],
            )
        elif stage == 1:
            self.first_copy.wait_recv()
            got = out.at[self.near, me.x_lo, self.rows, self.cols]
            self.third_copy = self.go(self.second, got, got)
        elif stage == 2:
            self.second_copy.wait_recv()
            self.own_copy.wait_recv()
            self.third_copy.wait_recv()
            got = out.at[:, me.x_lo, self.rows, self.cols]
            self.last = self.go(self.side, got, got)
        elif stage == 3 and self.kind != "pair":
            self.last.wait_recv()
            got = out.at[:, :, self.rows, self.cols]
            self.last = self.go(self.kind, got, got)
        elif stage == self.stages - 1:
            self.last.wait_recv()
            got = out.at[:, :, self.all_rows, self.cols]
            self.last = self.go("core", got, got)
        elif stage == self.stages:
            self.last.wait_recv()


def make_groups(me, ins, outs, plan, send_sem, recv_sem):
    pieces = {}
    for group in plan:
        for array, kind, piece in group:
            pieces[array] = max(pieces.get(array, 0), piece + 1)
    groups = []
    index = 0
    for group in plan:
        chains = []
        for array, kind, piece in group:
            for half in range(2 if kind == "pair" else 1):
                chains.append(
                    Chain(
                        me, ins[array], outs[array], kind, half, piece, pieces[array],
                        (send_sem, recv_sem, index),
                    )
                )
                index += 1
        groups.append(chains)
    return groups


def run_stage(chains, stage):
    for chain in chains:
        chain.run(stage)


def chain_count(plan):
    return sum(2 if kind == "pair" else 1 for group in plan for _, kind, _ in group)


class Staged:
    def __init__(self, source, target, sem):
        self.copy = pltpu.make_async_copy(source, target, sem)
        self.copy.start()
        self.target, self.here = target, False

    def __call__(self):
        if not self.here:
            self.copy.wait()
            self.here = True
        return self.target

    def __getitem__(self, index):
        return self()[index]

    @property
    def at(self):
        return self().at


def staged_kernel(kernel, n_in, n_out, greet, hops, *refs):
    refs = list(refs)

    def take(count):
        taken = refs[:count]
        del refs[:count]
        return taken

    n_carry = 3 if hops else 0
    ins, _, outs, carried, targets = (
        take(n_in), take(n_carry), take(n_out), take(n_carry), take(n_in)
    )
    (sem,) = take(1)
    staged = [Staged(ref, target, sem.at[i]) for i, (ref, target) in enumerate(zip(ins, targets))]
    moved = []
    if hops:
        send_sem, recv_sem = take(2)
    if greet is not None:
        me = Share()
        if greet == "all":
            me.greet_all()
        else:
            me.greet(greet)
    if hops:
        (chains,) = make_groups(me, carried, carried, FEED_PLAN, send_sem, recv_sem)
        for chain, hop in zip(chains, hops):
            if hop is not None:
                moved.append(chain.hop(hop))
    if greet != "all":
        staged = [ref() for ref in staged]
    kernel(*staged, *outs, *refs)
    if greet == "all":
        for ref in staged:
            ref()
    for copy in moved:
        copy.wait()


def staged_call(
    kernel, name, args, shapes, scratch, collective_id=None, greet=None, carry=(), hops=()
):
    carry = tuple(carry)
    outs = pl.pallas_call(
        functools.partial(staged_kernel, kernel, len(args), len(shapes), greet, hops),
        out_shape=[jax.ShapeDtypeStruct(shape, kind) for shape, kind in shapes]
        + [jax.ShapeDtypeStruct(array.shape, array.dtype) for array in carry],
        in_specs=[HBM] * len(args) + [ANY] * len(carry),
        out_specs=[VMEM] * len(shapes) + [ANY] * len(carry),
        scratch_shapes=[pltpu.VMEM(arg.shape, arg.dtype) for arg in args]
        + [pltpu.SemaphoreType.DMA((len(args),))]
        + ([pltpu.SemaphoreType.DMA((4, 7))] * 2 if hops else [])
        + scratch,
        input_output_aliases={len(args) + i: len(shapes) + i for i in range(len(carry))},
        compiler_params=pltpu.CompilerParams(
            collective_id=collective_id,
            has_side_effects=greet is not None,
            vmem_limit_bytes=VMEM_BYTES,
        ),
        name=name,
    )(*args, *carry)
    return (outs[: len(shapes)], outs[len(shapes) :]) if carry else outs

AXES = ("y", "x", "z")


def reduce_kernel(
    grads, small, *refs
):
    outs, small_out = refs[:11], refs[11]
    (acc, r0, r1, r2, r3, r4, r5, r6, full, sm_in,
     load_sem, send_sem, recv_sem, sm_send, sm_recv, ag_send, ag_recv) = refs[12:]
    recvs = (r1, r2, r3, r4, r5, r6)
    me = Place()
    me.greet(("core", "ya", "yb", "xa", "xb", "za", "zb", "xab"))
    spots = {
        "y": (me.y, me.y_a, me.y_b, me.y_ab),
        "x": (me.x, me.x_a, me.x_b, me.x_ab),
        "z": (me.z, me.z_a, me.z_b, me.z_ab),
    }
    parts = range(6)
    started = []

    def go(name, src, dst, send, recv):
        copy = me.send(name, src, dst, send, recv)
        started.append(copy)
        return copy

    small_out[...] = small[...]
    small_steps = ("core", "ya", "yb", "xa", "xb", "za", "zb")
    small_copies = []

    def small_start(step):
        small_copies.append(
            me.send(small_steps[step], small_out, sm_in.at[step], sm_send.at[step], sm_recv.at[step])
        )

    def small_end(step):
        small_copies[step].wait()
        small_out[...] = small_out[...] + sm_in[step]

    small_start(0)

    def order(part):
        first = (part // 2) % 3
        return [AXES[(first + k) % 3] for k in range(3)]

    def region(part, picks):
        return (part,) + tuple(picks.get(axis, slice(None)) for axis in AXES)

    def at(ref, index):
        return ref.at[index]

    core_copies, loads = [], []
    for part in parts:
        core_copies.append(
            go("core", grads.at[1 - me.core, part], r0.at[part], send_sem.at[part, 0], recv_sem.at[part, 0])
        )
        load = pltpu.make_async_copy(grads.at[me.core, part], acc.at[part], load_sem.at[part])
        load.start()
        loads.append(load)

    def add(index, source, source_index):
        acc[index] = acc[index] + source[source_index]

    def dims(part):
        return ("a", "b") if part % 2 == 0 else ("b", "a")

    def add_first(part, picks):
        axis = order(part)[0]
        rest = [name for name in AXES if name != axis]

        def step(k, carry):
            index = region(part, {**picks, rest[0]: k})
            acc[index] = acc[index] + r0[index]
            return carry

        lax.fori_loop(0, 4, step, 0)

    pending = {}
    for part in parts:
        axis = order(part)[0]
        me_at, a_at, b_at, ab_at = spots[axis]
        first, second = dims(part)
        sent = (a_at, ab_at) if first == "a" else (b_at, ab_at)
        core_copies[part].wait_recv()
        loads[part].wait()
        pending[part] = []
        for slot, spot in enumerate(sent):
            add_first(part, {axis: spot})
            pending[part].append(
                go(
                    axis + first,
                    at(acc, region(part, {axis: spot})),
                    r1.at[part, slot],
                    send_sem.at[part, 1 + slot],
                    recv_sem.at[part, 1 + slot],
                )
            )
    small_end(0)
    small_start(1)
    for part in parts:
        axis = order(part)[0]
        me_at, a_at, b_at, ab_at = spots[axis]
        first, second = dims(part)
        kept = b_at if first == "a" else a_at
        add_first(part, {axis: kept})
        add_first(part, {axis: me_at})

    sem_at = {part: 3 for part in parts}

    def next_sem(part):
        sem_at[part] += 1
        return send_sem.at[part, sem_at[part] - 1], recv_sem.at[part, sem_at[part] - 1]

    for level in range(3):
        one, two = recvs[2 * level], recvs[2 * level + 1]
        for part in parts:
            axes = order(part)
            axis = axes[level]
            first, second = dims(part)
            me_at, a_at, b_at, ab_at = spots[axis]
            kept = b_at if first == "a" else a_at
            fixed = {name: spots[name][0] for name in axes[:level]}
            for copy in pending[part]:
                copy.wait_recv()
            add(region(part, {**fixed, axis: kept}), one, (part, 1))
            send, recv = next_sem(part)
            pending[part] = [
                go(axis + second, at(acc, region(part, {**fixed, axis: kept})), two.at[part], send, recv)
            ]
        for part in parts:
            axes = order(part)
            fixed = {name: spots[name][0] for name in axes[: level + 1]}
            add(region(part, fixed), one, (part, 0))
        small_end(2 * level + 1)
        small_start(2 * level + 2)
        for part in parts:
            axes = order(part)
            fixed = {name: spots[name][0] for name in axes[: level + 1]}
            for copy in pending[part]:
                copy.wait_recv()
            add(region(part, fixed), two, (part,))
            if level == 2:
                continue
            axis = axes[level + 1]
            first, second = dims(part)
            me_at, a_at, b_at, ab_at = spots[axis]
            sent = (a_at, ab_at) if first == "a" else (b_at, ab_at)
            pending[part] = []
            for slot, spot in enumerate(sent):
                send, recv = next_sem(part)
                pending[part].append(
                    go(
                        axis + first,
                        at(acc, region(part, {**fixed, axis: spot})),
                        recvs[2 * level + 2].at[part, slot],
                        send,
                        recv,
                    )
                )
        small_end(2 * level + 2)
        if level < 2:
            small_start(2 * level + 3)

    here = me.x_hi * 4 + me.z
    there = (1 - me.x_hi) * 4 + me.z
    for part in parts:
        full[here, me.core, part] = acc[part, me.y, me.x, me.z]
    used = [0]

    def pass_on(name, group, half):
        index = used[0]
        used[0] += 1
        src = full.at[group, me.core, pl.ds(3 * half, 3)]
        return go(name, src, src, ag_send.at[index], ag_recv.at[index])

    early = [pass_on("xab", here, half) for half in range(2)]
    near = [pass_on("za", here, 0), pass_on("zb", here, 1)]
    far = []
    for half in range(2):
        early[half].wait_recv()
        far.append(pass_on(("za", "zb")[half], there, half))
    base, base_far = me.x_hi * 4, (1 - me.x_hi) * 4
    ends = [pass_on("zb", here, 0), pass_on("za", here, 1)]
    ends += [pass_on("zb", there, 0), pass_on("za", there, 1)]
    for half in range(2):
        got = (me.z_a, me.z_b)[half]
        near[half].wait_recv()
        ends.append(pass_on(("zb", "za")[half], base + got, half))
    for half in range(2):
        got = (me.z_a, me.z_b)[half]
        far[half].wait_recv()
        ends.append(pass_on(("zb", "za")[half], base_far + got, half))
    for copy in ends:
        copy.wait_recv()
    last = go("core", full.at[:, me.core], full.at[:, me.core], ag_send.at[used[0]], ag_recv.at[used[0]])

    def place(o):
        group, core = o // 2, o % 2
        for part in parts:
            rows = pl.ds(16 * part, 16)
            outs[group][rows, pl.ds(core * 384, 384)] = full[group, core, part, :, 0:384]
            outs[8][rows, pl.ds(128 * o, 128)] = full[group, core, part, :, 384:512]
            outs[9][rows, pl.ds(128 * o, 128)] = full[group, core, part, :, 512:640]
            outs[10][pl.ds(16 * o, 16), pl.ds(128 * part, 128)] = full[group, core, part, :, 640:768]

    last.wait_recv()
    for o in range(16):
        place(o)
    for copy in started:
        copy.wait_send()


def reduce_weights(grads, small, collective_id):
    bf = jnp.bfloat16
    shapes = [(96, 768)] * 8 + [(96, 2048)] * 2 + [(256, 768)]
    return pl.pallas_call(
        reduce_kernel,
        out_shape=[jax.ShapeDtypeStruct(shape, bf) for shape in shapes]
        + [jax.ShapeDtypeStruct(small.shape, small.dtype)],
        in_specs=[ANY, VMEM],
        out_specs=[VMEM] * 12,
        scratch_shapes=[
            pltpu.VMEM((6, 4, 4, 4, 16, 768), bf),
            pltpu.VMEM((6, 4, 4, 4, 16, 768), bf),
            pltpu.VMEM((6, 2, 4, 4, 16, 768), bf),
            pltpu.VMEM((6, 4, 4, 16, 768), bf),
            pltpu.VMEM((6, 2, 4, 16, 768), bf),
            pltpu.VMEM((6, 4, 16, 768), bf),
            pltpu.VMEM((6, 2, 16, 768), bf),
            pltpu.VMEM((6, 16, 768), bf),
            pltpu.VMEM((8, 2, 6, 16, 768), bf),
            pltpu.VMEM((7,) + small.shape, small.dtype),
            pltpu.SemaphoreType.DMA((6,)),
            pltpu.SemaphoreType.DMA((6, 10)),
            pltpu.SemaphoreType.DMA((6, 10)),
            pltpu.SemaphoreType.DMA((7,)),
            pltpu.SemaphoreType.DMA((7,)),
            pltpu.SemaphoreType.DMA((16,)),
            pltpu.SemaphoreType.DMA((16,)),
        ],
        compiler_params=pltpu.CompilerParams(
            collective_id=collective_id, has_side_effects=True, vmem_limit_bytes=VMEM_BYTES
        ),
        name="reduce_weights",
    )(grads, small)


def outer_kernel(*refs):
    acts, grads = refs[:8], refs[8:16]
    third, gate, up, mixed, cot, out, act, grad = refs[16:]
    step = pl.program_id(0)
    for index in range(8):
        for half in range(2):
            @pl.when(step == 2 * index + half)
            def _():
                if half == 0:
                    act[...] = acts[index][...]
                grad[...] = grads[index][:, 384 * half : 384 * half + 384]

    def transposed_dot(left, right):
        return lax.dot_general(
            left, right, (((0,), (0,)), ((), ())), preferred_element_type=jnp.float32
        ).astype(jnp.bfloat16)

    attn = transposed_dot(act[...], grad[...])
    wide = transposed_dot(third[...], jnp.concatenate([gate[...], up[...]], axis=1))
    down = transposed_dot(mixed[0], cot[...])
    for row in range(8):
        for part in range(6):
            begin = row * 96 + part * 16
            where = (0, part, row // 2, row % 2, 0, 0)
            out[where + (slice(None), slice(0, 384))] = attn[begin : begin + 16]
            out[where + (slice(None), slice(384, 640))] = wide[begin : begin + 16]
            out[where + (slice(None), slice(640, 768))] = down[
                row * 16 : row * 16 + 16, part * 128 : part * 128 + 128
            ]


def outer_products(acts, grads, third, gate, up, mixed, cot):
    tokens = third.shape[0]
    mixed_cut = mixed.reshape(tokens, 8, 16, 16).transpose(2, 0, 1, 3).reshape(16, tokens, 128)
    whole = pl.BlockSpec((tokens, 768), lambda o: (0, 0))
    out = pl.pallas_call(
        outer_kernel,
        grid=(16,),
        out_shape=jax.ShapeDtypeStruct((2, 6, 4, 2, 2, 4, 16, 768), jnp.bfloat16),
        in_specs=[whole] * 17
        + [
            pl.BlockSpec((tokens, 128), lambda o: (0, o)),
            pl.BlockSpec((tokens, 128), lambda o: (0, o)),
            pl.BlockSpec((1, tokens, 128), lambda o: (o, 0, 0)),
            whole,
        ],
        out_specs=pl.BlockSpec(
            (1, 6, 4, 2, 1, 1, 16, 768),
            lambda o: (o % 2, 0, 0, 0, o // 8, (o // 2) % 4, 0, 0),
        ),
        scratch_shapes=[
            pltpu.VMEM((tokens, 768), jnp.bfloat16),
            pltpu.VMEM((tokens, 384), jnp.bfloat16),
        ],
        compiler_params=pltpu.CompilerParams(vmem_limit_bytes=VMEM_BYTES),
        name="outer_products",
    )(*acts, *grads, third, gate, up, mixed_cut, cot)
    return out.reshape(2, 6, 4, 4, 4, 16, 768)

NEGATIVE = -1e30
EPSILON = 1e-06
TILES = 23
USED = 16


class Share(Place):
    def __init__(self):
        super().__init__()
        self.dev["zab"] = (self.x_hi * 8 + self.z_ab * 2 + self.core, self.d)
        self.mine = self.x_hi * 2 + self.core
        self.slot = self.c // 4
        rest = self.c % 4
        self.owner = rest + (self.slot % 2) * (3 - 2 * rest)
        self.at_home = self.owner == self.mine

    def block(self, slot):
        return 4 * slot + (self.mine if slot % 2 == 0 else 3 - self.mine)

    def worker(self, group):
        return (self.owner // 2) * 8 + group * 2 + self.owner % 2

    def greet_all(self, extra=()):
        barrier = pltpu.get_barrier_semaphore()
        for name in extra:
            pl.semaphore_signal(
                barrier, inc=1, device_id=self.dev[name], device_id_type=MESH
            )
        for step in range(1, 16):
            pl.semaphore_signal(
                barrier, inc=1, device_id=((self.c + step) % 16, self.d), device_id_type=MESH
            )
        pl.semaphore_wait(barrier, 15 + len(extra))

    def copy_to(self, ctx, src, dst, send_sem, recv_sem):
        return pltpu.make_async_remote_copy(
            src_ref=src,
            dst_ref=dst,
            send_sem=send_sem,
            recv_sem=recv_sem,
            device_id=(ctx, self.d),
            device_id_type=MESH,
        )


class Rows:
    def __init__(self, me, src, dst, send_sem, recv_sem, back):
        self.me, self.src, self.dst = me, src, dst
        self.send_sem, self.recv_sem, self.back = send_sem, recv_sem, back

    def to_worker(self, group, ours):
        me = self.me
        away = jnp.logical_not(jnp.logical_and(me.at_home, me.z == group))
        if self.back:
            copy = me.copy_to(
                me.worker(group), self.src.at[0], self.dst.at[group],
                self.send_sem.at[0], self.recv_sem.at[group],
            )
        else:
            copy = me.copy_to(
                me.worker(group), self.src.at[group], self.dst.at[me.slot],
                self.send_sem.at[group], self.recv_sem.at[me.slot],
            )
        return away, copy

    def to_home(self, slot):
        me = self.me
        away = me.block(slot) != me.c
        if self.back:
            copy = me.copy_to(
                me.block(slot), self.src.at[slot], self.dst.at[me.z],
                self.send_sem.at[slot], self.recv_sem.at[me.z],
            )
        else:
            copy = me.copy_to(
                me.block(slot), self.src.at[0], self.dst.at[slot],
                self.send_sem.at[0], self.recv_sem.at[slot],
            )
        return away, copy

    def each(self, sending, action):
        for index in range(4):
            if sending != self.back:
                away, copy = self.to_worker(index, sending)
            else:
                away, copy = self.to_home(index)

            @pl.when(away)
            def _():
                action(copy)

    def start(self):
        me = self.me
        self.each(True, lambda copy: copy.start())

        @pl.when(me.at_home)
        def _():
            if self.back:
                self.dst[me.z] = self.src[me.slot]
            else:
                self.dst[me.slot] = self.src[me.z]

    def arrive(self):
        self.each(False, lambda copy: copy.wait_recv())

    def end(self):
        self.each(True, lambda copy: copy.wait_send())


class Pairs:
    def __init__(self, me, src, out, send_sem, recv_sem):
        self.me, self.src, self.out = me, src, out
        self.send_sem, self.recv_sem, self.done = send_sem, recv_sem, []
        self.groups = (me.z_a, me.z_b, me.z_ab)

    def go(self, name, src, dst, slot):
        copy = self.me.send(name, src, dst, self.send_sem.at[slot], self.recv_sem.at[slot])
        self.done.append(copy)
        return copy

    def start(self):
        me = self.me
        self.out[me.c] = self.src[me.z]
        self.first = [
            self.go(name, self.src.at[group], self.out.at[me.c], slot)
            for slot, (name, group) in enumerate(zip(("za", "zb", "zab"), self.groups))
        ]
        self.over_x, self.over_core = [], []
        self.pass_on(0)

    def pass_on(self, step):
        me = self.me
        block = me.x_hi * 8 + ((me.z,) + self.groups)[step] * 2 + me.core
        spot = self.out.at[block]
        self.over_x.append(self.go("xab", spot, spot, 3 + step))
        self.over_core.append(self.go("core", spot, spot, 7 + step))

    def second(self):
        for step in range(1, 4):
            self.first[step - 1].wait_recv()
            self.pass_on(step)

    def third(self):
        me = self.me
        for step, group in enumerate((me.z,) + self.groups):
            self.over_x[step].wait_recv()
            spot = self.out.at[(1 - me.x_hi) * 8 + group * 2 + me.core]
            self.over_core.append(self.go("core", spot, spot, 11 + step))

    def arrive(self):
        for copy in self.over_core:
            copy.wait_recv()

    def end(self):
        for copy in self.done:
            copy.wait_send()


class Sums:
    def __init__(self, me, src, total, send_sem, recv_sem, got_core, part, got_x):
        self.me, self.src, self.total = me, src, total
        self.send_sem, self.recv_sem, self.done = send_sem, recv_sem, []
        self.got_core, self.part, self.got_x = got_core, part, got_x
        self.order = (me.z_ab, me.z_a, me.z_b, me.z)

    def go(self, name, src, dst, slot):
        copy = self.me.send(name, src, dst, self.send_sem.at[slot], self.recv_sem.at[slot])
        self.done.append(copy)
        return copy

    def start(self):
        me = self.me
        self.near, self.far = me.x_hi * 4, (1 - me.x_hi) * 4
        self.core_copies = [
            self.go(
                "core",
                self.src.at[side + group, 1 - me.core],
                self.got_core.at[side + group],
                4 * index + step,
            )
            for index, side in enumerate((self.far, self.near))
            for step, group in enumerate(self.order)
        ]

    def over(self):
        me = self.me
        self.over_x = []
        for step, group in enumerate(self.order):
            self.core_copies[step].wait_recv()
            block = self.far + group
            self.part[block] = self.src[block, me.core] + self.got_core[block]
            self.over_x.append(self.go("xab", self.part.at[block], self.got_x.at[group], 8 + step))
        for step, group in enumerate(self.order):
            self.core_copies[4 + step].wait_recv()
            block = self.near + group
            self.part[block] = self.src[block, me.core] + self.got_core[block]

    def finish(self, then=None):
        for step, group in enumerate(self.order):
            self.over_x[step].wait_recv()
            self.total[group] = self.part[self.near + group] + self.got_x[group]
            if then is not None and step < 3:
                then.send(step)

    def end(self):
        for copy in self.done:
            copy.wait_send()


class Owners:
    def __init__(self, me, total, out, send_sem, recv_sem):
        self.me, self.total, self.out = me, total, out
        self.send_sem, self.recv_sem, self.copies = send_sem, recv_sem, []

    def send(self, step):
        me = self.me
        group, name = ((me.z_ab, "zab"), (me.z_a, "za"), (me.z_b, "zb"))[step]
        self.copies.append(
            me.send(
                name, self.total.at[group], self.out.at[me.z],
                self.send_sem.at[step], self.recv_sem.at[step],
            )
        )

    def arrive(self):
        self.out[self.me.z] = self.total[self.me.z]
        for copy in self.copies:
            copy.wait_recv()

    def end(self):
        for copy in self.copies:
            copy.wait_send()


def lane_mask(value, begin, end):
    lane = lax.broadcasted_iota(jnp.int32, value.shape, 1)
    return jnp.where(jnp.logical_and(lane >= begin, lane < end), value, jnp.zeros_like(value))


def cut_heads(value, after):
    groups = []
    for half in range(2):
        left = value[:, 384 * half : 384 * half + 256]
        right = value[:, 384 * half + 128 : 384 * half + 384]
        if after:
            groups += [lane_mask(left, 0, 192), lane_mask(pltpu.roll(right, 192, 1), 0, 192)]
        else:
            groups += [lane_mask(pltpu.roll(left, 64, 1), 64, 256), lane_mask(right, 64, 256)]
    return groups


def join_heads(groups, after):
    pieces = []
    for half in range(2):
        left, right = groups[2 * half], groups[2 * half + 1]
        if after:
            right = pltpu.roll(right, 64, 1)
        else:
            left = pltpu.roll(left, 192, 1)
        pieces += [left[:, :128], left[:, 128:] + right[:, :128], right[:, 128:]]
    return jnp.concatenate(pieces, axis=1)


def put_rows(ref, value, after):
    for group, part in enumerate(cut_heads(value, after)):
        ref[group] = part.astype(jnp.bfloat16)


def get_rows(ref, after):
    return join_heads([ref[group].astype(jnp.float32) for group in range(4)], after)


def put_pairs(ref, keys, values):
    for group, (left, right) in enumerate(zip(cut_heads(keys, True), cut_heads(values, False))):
        ref[group, :, 0:128] = left[:, :128].astype(jnp.bfloat16)
        ref[group, :, 128:256] = (left[:, 128:] + right[:, :128]).astype(jnp.bfloat16)
        ref[group, :, 256:384] = right[:, 128:].astype(jnp.bfloat16)


def get_pairs(ref):
    keys = [lane_mask(ref[group, :, 0:256].astype(jnp.float32), 0, 192) for group in range(4)]
    values = [lane_mask(ref[group, :, 128:384].astype(jnp.float32), 64, 256) for group in range(4)]
    return join_heads(keys, True), join_heads(values, False)


def scale_of(value):
    return lax.rsqrt(jnp.mean(value * value, axis=-1, keepdims=True) + EPSILON)


def norm_back(value, gain, grad):
    scale = scale_of(value)
    weighted = grad * gain
    middle = jnp.mean(value * weighted, axis=-1, keepdims=True)
    dgain = jnp.sum(grad * (value * scale), axis=0, keepdims=True)
    return scale * weighted - value * (scale * scale * scale) * middle, dgain


def open_kernel(
    layer_input, encoder, gain, *refs
):
    shards = refs[:11]
    q_out, kv_out, ckv_out, normed_out = refs[11:15]
    outs = refs[15:26]
    (q_mine, kv_mine, ckv_mine, q_send, q_recv, kv_send, kv_recv, ckv_send, ckv_recv,
     early_send, early_recv, late_send, late_recv, feed_send, feed_recv, held, held_sem) = refs[26:]
    me = Share()
    me.greet_all(extra=("ya", "yb", "xa", "xb"))
    early = make_groups(me, shards[:5], outs[:5], EARLY_PLAN, early_send, early_recv)
    late = make_groups(me, shards[5:8], outs[5:8], LATE_PLAN, late_send, late_recv)
    feed = make_groups(me, shards[8:], outs[8:], FEED_PLAN, feed_send, feed_recv)
    run_stage(early[0], 0)
    run_stage(early[1], 0)
    run_stage(late[0], 0)
    run_stage(late[1], 0)
    run_stage(early[0], 1)
    run_stage(early[1], 1)
    run_stage(feed[0], 0)
    run_stage(early[0], 2)
    run_stage(early[1], 2)
    residual = layer_input[...].astype(jnp.float32)
    normed = (residual * scale_of(residual) * gain[...]).astype(jnp.bfloat16)
    normed_out[...] = normed
    run_stage(late[0], 1)
    run_stage(late[1], 1)
    run_stage(early[0], 3)
    run_stage(early[1], 3)
    run_stage(late[0], 2)
    run_stage(late[1], 2)
    run_stage(early[0], 4)

    def fetch(index):
        fetched = []
        for y in range(4):
            for x in range(2):
                begin = 96 * (2 * y + x)
                fetched.append(
                    pltpu.make_async_copy(
                        outs[index].at[y, x],
                        held.at[index, pl.ds(begin, 96)],
                        held_sem.at[index, 2 * y + x],
                    )
                )
                fetched[-1].start()
        return fetched

    def wait_all(copies):
        for copy in copies:
            copy.wait()

    fetched = [fetch(index) for index in range(3)]
    run_stage(early[1], 4)
    fetched += [fetch(index) for index in range(3, 5)]
    wait_all(fetched[1])
    wait_all(fetched[2])
    put_pairs(kv_mine, dot_nn(normed, held[1]), dot_nn(normed, held[2]))
    self_kv = Pairs(me, kv_mine, kv_out, kv_send, kv_recv)
    self_kv.start()
    wait_all(fetched[0])
    put_rows(q_mine, dot_nn(normed, held[0]), True)
    rows = Rows(me, q_mine, q_out, q_send, q_recv, False)
    rows.start()
    wait_all(fetched[3])
    wait_all(fetched[4])
    put_pairs(ckv_mine, dot_nn(encoder[...], held[3]), dot_nn(encoder[...], held[4]))
    cross_kv = Pairs(me, ckv_mine, ckv_out, ckv_send, ckv_recv)
    cross_kv.start()
    run_stage(late[0], 3)
    self_kv.second()
    cross_kv.second()
    run_stage(late[1], 3)
    run_stage(late[0], 4)
    run_stage(feed[0], 1)
    self_kv.third()
    run_stage(late[1], 4)
    run_stage(late[0], 5)
    cross_kv.third()
    rows.arrive()
    self_kv.arrive()
    cross_kv.arrive()
    for chain in feed[0]:
        chain.second_copy.wait_recv()
        chain.third_copy.wait_recv()
        chain.own_copy.wait_recv()
    for chains in early + late + feed:
        for chain in chains:
            wait_sent(chain.copies)
    rows.end()
    self_kv.end()
    cross_kv.end()


def wait_sent(copies):
    for copy in copies:
        copy.wait_send()


def open_layer(layer_input, encoder, gain, shards, collective_id):
    bf = jnp.bfloat16
    early, late = chain_count(EARLY_PLAN), chain_count(LATE_PLAN)
    outs = pl.pallas_call(
        open_kernel,
        out_shape=[
            jax.ShapeDtypeStruct((4, 128, 256), bf),
            jax.ShapeDtypeStruct((16, 128, 384), bf),
            jax.ShapeDtypeStruct((16, 128, 384), bf),
            jax.ShapeDtypeStruct((128, 768), bf),
        ]
        + [jax.ShapeDtypeStruct((4, 2) + shard.shape, bf) for shard in shards],
        in_specs=[VMEM] * 3 + [ANY] * 11,
        out_specs=[VMEM] * 4 + [ANY] * 11,
        scratch_shapes=[
            pltpu.VMEM((4, 128, 256), bf),
            pltpu.VMEM((4, 128, 384), bf),
            pltpu.VMEM((4, 128, 384), bf),
            pltpu.SemaphoreType.DMA((4,)),
            pltpu.SemaphoreType.DMA((4,)),
            pltpu.SemaphoreType.DMA((15,)),
            pltpu.SemaphoreType.DMA((15,)),
            pltpu.SemaphoreType.DMA((15,)),
            pltpu.SemaphoreType.DMA((15,)),
            pltpu.SemaphoreType.DMA((early, 7)),
            pltpu.SemaphoreType.DMA((early, 7)),
            pltpu.SemaphoreType.DMA((late, 7)),
            pltpu.SemaphoreType.DMA((late, 7)),
            pltpu.SemaphoreType.DMA((4, 7)),
            pltpu.SemaphoreType.DMA((4, 7)),
            pltpu.VMEM((5, 768, 768), bf),
            pltpu.SemaphoreType.DMA((5, 8)),
        ],
        compiler_params=pltpu.CompilerParams(
            collective_id=collective_id, has_side_effects=True, vmem_limit_bytes=VMEM_BYTES
        ),
        name="open_layer",
    )(layer_input, encoder, gain, *shards)
    return outs[:4], [whole(out) for out in outs[4:12]], outs[12:]


def whole(gathered):
    return gathered.reshape(8 * gathered.shape[2], gathered.shape[3])


def row_scratch():
    return [
        pltpu.VMEM((4, 128, 256), jnp.bfloat16),
        pltpu.SemaphoreType.DMA((4,)),
        pltpu.SemaphoreType.DMA((4,)),
    ]


def sum_scratch():
    bf = jnp.bfloat16
    return [
        pltpu.SemaphoreType.DMA((12,)),
        pltpu.SemaphoreType.DMA((12,)),
        pltpu.VMEM((8, 128, 384), bf),
        pltpu.VMEM((8, 128, 384), bf),
        pltpu.VMEM((4, 128, 384), bf),
    ]


def owner_scratch():
    return [
        pltpu.VMEM((4, 128, 384), jnp.bfloat16),
        pltpu.SemaphoreType.DMA((3,)),
        pltpu.SemaphoreType.DMA((3,)),
    ]


def shared_call(kernel, name, args, shapes, scratch, collective_id, carry=(), hops=()):
    return staged_call(kernel, name, args, shapes, scratch, collective_id, "all", carry, hops)


def middle_kernel(
    o_in, layer_input, gain, w_out, w_query,
    q_out, attended_out, middle_out, normed_out,
    o_mine, o_send, o_recv, q_mine, q_send, q_recv,
):
    me = Share()
    back = Rows(me, o_in, o_mine, o_send, o_recv, True)
    back.start()
    back.arrive()
    attended = get_rows(o_mine, False).astype(jnp.bfloat16)
    middle = layer_input[...].astype(jnp.float32) + dot_nn(attended, w_out[...])
    normed = (middle * scale_of(middle) * gain[...]).astype(jnp.bfloat16)
    put_rows(q_mine, dot_nn(normed, w_query[...]), True)
    rows = Rows(me, q_mine, q_out, q_send, q_recv, False)
    rows.start()
    attended_out[...] = attended
    middle_out[...] = middle
    normed_out[...] = normed
    rows.arrive()
    back.end()
    rows.end()


def feed_kernel(
    o_in, middle, gain, w_out, w_gate, w_up, w_down, cotangent,
    g_out, final_out, crossed_out, normed_out, grad_gate, grad_up, mixed, branch_out, after_out,
    dgain_out,
    o_mine, o_send, o_recv, g_mine, g_send, g_recv, grad_mixed,
):
    low = jnp.bfloat16
    me = Share()
    back = Rows(me, o_in, o_mine, o_send, o_recv, True)
    back.start()
    grad_mixed[...] = dot_nt(cotangent[...], w_down[...])
    back.arrive()
    crossed = get_rows(o_mine, False).astype(low)
    crossed_out[...] = crossed
    after = middle[...] + dot_nn(crossed, w_out[...])
    normed = (after * scale_of(after) * gain[...]).astype(low)
    normed_out[...] = normed
    root = math.sqrt(2.0 / math.pi)
    for chunk in range(8):
        cols = slice(256 * chunk, 256 * chunk + 256)
        gate = dot_nn(normed, w_gate[:, cols])
        up = dot_nn(normed, w_up[:, cols])
        square = gate * gate
        curve = jnp.tanh(root * gate * (1.0 + 0.044715 * square))
        half = 0.5 * (1.0 + curve)
        gelu = gate * half
        slope = half + 0.5 * gate * (1.0 - curve * curve) * (
            root * (1.0 + 3 * 0.044715 * square)
        )
        incoming = grad_mixed[:, cols]
        mixed[:, cols] = (gelu * up).astype(low)
        grad_gate[:, cols] = (incoming * up * slope).astype(low)
        grad_up[:, cols] = (incoming * gelu).astype(low)
    grad_normed = dot_nt(grad_gate[...], w_gate[...]) + dot_nt(grad_up[...], w_up[...])
    grad_value, dgain = norm_back(after, gain[...], grad_normed)
    dgain_out[...] = dgain
    grad_after = cotangent[...].astype(jnp.float32) + grad_value
    branch = grad_after.astype(low)
    put_rows(g_mine, dot_nt(branch, w_out[...]), False)
    rows = Rows(me, g_mine, g_out, g_send, g_recv, False)
    rows.start()
    branch_out[...] = branch
    after_out[...] = grad_after
    final_out[...] = (after + dot_nn(mixed[...], w_down[...])).astype(low)
    rows.arrive()
    back.end()
    rows.end()


def turn_kernel(
    dq_in, dkv_in, middle, gain, grad_after, w_query, w_out,
    g_out, dq_out, total_out, branch_out, grad_out, dgain_out,
    dq_mine, dq_send, dq_recv, g_mine, g_send, g_recv, *sums,
):
    low = jnp.bfloat16
    me = Share()
    back = Rows(me, dq_in, dq_mine, dq_send, dq_recv, True)
    back.start()
    pairs = Sums(me, dkv_in, total_out, *sums)
    pairs.start()
    back.arrive()
    grad_query = get_rows(dq_mine, True).astype(low)
    dq_out[...] = grad_query
    grad_value, dgain = norm_back(middle[...], gain[...], dot_nt(grad_query, w_query[...]))
    dgain_out[...] = dgain
    grad_middle = grad_after[...] + grad_value
    branch = grad_middle.astype(low)
    put_rows(g_mine, dot_nt(branch, w_out[...]), False)
    rows = Rows(me, g_mine, g_out, g_send, g_recv, False)
    rows.start()
    pairs.over()
    grad_out[...] = grad_middle
    branch_out[...] = branch
    pairs.finish()
    rows.arrive()
    back.end()
    rows.end()
    pairs.end()


def close_kernel(
    dq_in, dkv_in, layer_input, gain, grad_middle, w_query, w_key, w_value,
    cross_total, w_ckey, w_cvalue,
    grad_out, encoder_out, dq_out, dk_out, dv_out, cross_dk, cross_dv, dgain_out,
    dq_mine, dq_send, dq_recv, total, *scratch,
):
    low = jnp.bfloat16
    me = Share()
    sums, self_own, cross_own = scratch[:5], scratch[5:8], scratch[8:11]
    pairs = Sums(me, dkv_in, total, *sums)
    pairs.start()
    back = Rows(me, dq_in, dq_mine, dq_send, dq_recv, True)
    back.start()
    cross = Owners(me, cross_total(), *cross_own)
    for step in range(3):
        cross.send(step)
    pairs.over()
    cross.arrive()
    keys, values = get_pairs(cross_own[0])
    keys, values = keys.astype(low), values.astype(low)
    cross_dk[...] = keys
    cross_dv[...] = values
    encoder_out[...] = dot_nt(keys, w_ckey[...]) + dot_nt(values, w_cvalue[...])
    back.arrive()
    grad_query = get_rows(dq_mine, True).astype(low)
    dq_out[...] = grad_query
    grad_normed = dot_nt(grad_query, w_query[...])
    owners = Owners(me, total, *self_own)
    pairs.finish(owners)
    owners.arrive()
    keys, values = get_pairs(self_own[0])
    keys, values = keys.astype(low), values.astype(low)
    dk_out[...] = keys
    dv_out[...] = values
    grad_normed = grad_normed + dot_nt(keys, w_key[...]) + dot_nt(values, w_value[...])
    residual = layer_input[...].astype(jnp.float32)
    grad_value, dgain = norm_back(residual, gain[...], grad_normed)
    dgain_out[...] = dgain
    grad_out[...] = grad_middle[...] + grad_value
    back.end()
    pairs.end()
    cross.end()
    owners.end()


def dot_nn(left, right):
    return jnp.dot(left, right, preferred_element_type=jnp.float32)


def dot_nt(left, right):
    return lax.dot_general(
        left, right, (((1,), (1,)), ((), ())), preferred_element_type=jnp.float32
    )


def head_lanes(value, head):
    lane = lax.broadcasted_iota(jnp.int32, value.shape, 1)
    return jnp.where(lane // 64 == head, value, jnp.zeros_like(value))


def head_rows(value, head):
    row = lax.broadcasted_iota(jnp.int32, value.shape, 0)
    return jnp.where(row // 64 == head, value, jnp.zeros_like(value))


def bias_offset(pair, side, chunk):
    c = lax.axis_index("ctx")
    mine = (c // 8) * 2 + c % 2
    block = 8 * pair + (mine if side == 0 else 7 - mine)
    return pl.multiple_of((15 - block) * 128 + chunk * 256, 128)


def bias_at(wide, head, pair, chunk):
    return jnp.concatenate(
        [wide[head, pl.ds(bias_offset(pair, side, chunk), 256), :] for side in range(2)], axis=1
    )


def forward_kernel(causal, *refs):
    if causal:
        q, kv, waves, o_low, o_full, lse, wide, values_t, score, total = refs
        def build(head, carry):
            for tile in range(USED):
                row = jnp.broadcast_to(waves[head, tile : tile + 1, :], (128, 256))
                turned = pltpu.roll(row, 129, 1, stride=1, stride_axis=0)
                wide[head, tile * 128 : tile * 128 + 128, :] = turned[:, :128]
            wide[head, USED * 128 :, :] = jnp.full(
                ((TILES - USED) * 128, 128), NEGATIVE, jnp.float32
            )
            return carry

        lax.fori_loop(0, 3, build, 0)
    else:
        q, kv, o_low, o_full, lse, values_t, score, total = refs

    for chunk in range(8):
        values_t[chunk] = kv[2 * chunk : 2 * chunk + 2, :, 128:384].reshape(256, 256).T
    for pair in range(2):
        chunks = 4 if causal and pair == 0 else 8
        rows = q[2 * pair : 2 * pair + 2].reshape(256, 256)
        total[...] = jnp.zeros_like(total)

        def one_head(head, carry):
            masked = head_lanes(rows, head)

            top = jnp.full((8, 256), NEGATIVE, jnp.float32)
            for chunk in range(chunks):
                keys = kv[2 * chunk : 2 * chunk + 2, :, 0:256].reshape(256, 256)
                block = dot_nt(keys, masked)
                if causal:
                    block = block + bias_at(wide, head, pair, chunk)
                score[chunk] = block
                top = jnp.maximum(top, jnp.max(block.reshape(32, 8, 256), axis=0))
            top = jnp.max(top, axis=0, keepdims=True)
            summed = jnp.zeros((8, 256), jnp.float32)
            held = jnp.zeros((256, 256), jnp.float32)
            for chunk in range(chunks):
                expo = jnp.exp(score[chunk] - top)
                summed = summed + jnp.sum(expo.reshape(32, 8, 256), axis=0)
                held = held + dot_nn(values_t[chunk], expo.astype(jnp.bfloat16))
            summed = jnp.sum(summed, axis=0, keepdims=True)
            total[...] += head_rows(held * (1.0 / summed), head + 1)
            lse[head, pair] = top + jnp.log(summed)
            return carry

        lax.fori_loop(0, 3, one_head, 0)
        final = total[...].T.reshape(2, 128, 256)
        o_full[2 * pair : 2 * pair + 2] = final
        o_low[2 * pair : 2 * pair + 2] = final.astype(jnp.bfloat16)


def attend(q, kv, waves, collective_id, greet, carry, hops):
    causal = waves is not None
    shapes = [
        ((4, 128, 256), jnp.bfloat16),
        ((4, 128, 256), jnp.float32),
        ((3, 2, 1, 256), jnp.float32),
    ]
    args = [q, kv]
    if causal:
        shapes.append(((3, TILES * 128, 128), jnp.float32))
        args.append(waves)
    return staged_call(
        functools.partial(forward_kernel, causal),
        "attend_self" if causal else "attend_cross",
        args,
        shapes,
        [
            pltpu.VMEM((8, 256, 256), jnp.bfloat16),
            pltpu.VMEM((8, 256, 256), jnp.float32),
            pltpu.VMEM((256, 256), jnp.float32),
        ],
        collective_id,
        greet,
        carry,
        hops,
    )


def backward_kernel(causal, *refs):
    if causal:
        (q, kv, grad, o_full, lse, wide, dq, dkv, waves,
         keys_t, dk, dv, dq_t, turned, along) = refs
        along[...] = jnp.zeros_like(along)
    else:
        q, kv, grad, o_full, lse, dq, dkv, keys_t, dk, dv, dq_t, turned = refs
    dk[...] = jnp.zeros_like(dk)
    dv[...] = jnp.zeros_like(dv)

    for chunk in range(8):
        keys_t[chunk] = kv[2 * chunk : 2 * chunk + 2, :, 0:256].reshape(256, 256).T
    for pair in range(2):
        chunks = 4 if causal and pair == 0 else 8
        both = slice(2 * pair, 2 * pair + 2)
        rows = q[both].reshape(256, 256)
        grads = grad[both].reshape(256, 256)
        turned[...] = (grads.astype(jnp.float32) * o_full[both].reshape(256, 256)).T
        dq_t[...] = jnp.zeros_like(dq_t)

        def one_head(head, carry):
            masked = head_lanes(rows, head)
            masked_grads = head_lanes(grads, head + 1)
            delta = jnp.sum(head_rows(turned[...], head + 1), axis=0, keepdims=True)
            row_lse = lse[head, pair]

            held = jnp.zeros((256, 256), jnp.float32)
            for chunk in range(chunks):
                block = kv[2 * chunk : 2 * chunk + 2].reshape(256, 384)
                scores = dot_nt(block[:, 0:256], masked)
                if causal:
                    scores = scores + bias_at(wide, head, pair, chunk)
                probs = jnp.exp(scores - row_lse)
                grad_probs = dot_nt(block[:, 128:384], masked_grads)
                grad_scores = probs * (grad_probs - delta)
                low = grad_scores.astype(jnp.bfloat16)
                spot = slice(chunk * 256, chunk * 256 + 256)
                dk[spot] += dot_nn(low, masked)
                dv[spot] += dot_nn(probs.astype(jnp.bfloat16), masked_grads)
                if causal:
                    for side in range(2):
                        where = pl.ds(bias_offset(pair, side, chunk), 256)
                        along[head, where, :] += grad_scores[:, 128 * side : 128 * side + 128]
                held = held + dot_nn(keys_t[chunk], low)
            dq_t[...] += head_rows(held, head)
            return carry

        lax.fori_loop(0, 3, one_head, 0)
        dq[both] = dq_t[...].T.reshape(2, 128, 256).astype(jnp.bfloat16)

    def pack(block, carry):
        spot = pl.ds(pl.multiple_of(block * 128, 128), 128)
        key_part, value_part = dk[spot], dv[spot]
        dkv[block, :, 0:128] = key_part[:, 0:128].astype(jnp.bfloat16)
        dkv[block, :, 128:256] = (key_part[:, 128:256] + value_part[:, 0:128]).astype(jnp.bfloat16)
        dkv[block, :, 256:384] = value_part[:, 128:256].astype(jnp.bfloat16)
        return carry

    lax.fori_loop(0, 16, pack, 0)
    if causal:
        waves[...] = jnp.zeros_like(waves)

        def fold(head, carry):
            for tile in range(USED):
                value = along[head, tile * 128 : tile * 128 + 128, :]
                value = jnp.concatenate([value, jnp.zeros_like(value)], axis=1)
                count = 64
                while count >= 1:
                    value = pltpu.roll(value[:count], count, 1) + value[count:]
                    count //= 2
                waves[head, tile : tile + 1, :] = value
            return carry

        lax.fori_loop(0, 3, fold, 0)


def attend_back(q, kv, grad, o_full, lse, wide):
    causal = wide is not None
    shapes = [((4, 128, 256), jnp.bfloat16), ((16, 128, 384), jnp.bfloat16)]
    args = [q, kv, grad, o_full, lse]
    scratch = [
        pltpu.VMEM((8, 256, 256), jnp.bfloat16),
        pltpu.VMEM((2048, 256), jnp.float32),
        pltpu.VMEM((2048, 256), jnp.float32),
        pltpu.VMEM((256, 256), jnp.float32),
        pltpu.VMEM((256, 256), jnp.float32),
    ]
    if causal:
        shapes.append(((3, TILES, 256), jnp.float32))
        args.append(wide)
        scratch.append(pltpu.VMEM((3, TILES * 128, 128), jnp.float32))
    return staged_call(
        functools.partial(backward_kernel, causal),
        "attend_back_self" if causal else "attend_back_cross",
        args,
        shapes,
        scratch,
    )


PRECISE = lax.Precision.HIGHEST


def body(
    layer_input,
    encoder_states,
    cotangent,
    bucket_ids,
    bias_table,
    gain_first,
    gain_second,
    gain_third,
    self_query,
    self_key,
    self_value,
    self_output,
    cross_query,
    cross_key,
    cross_value,
    cross_output,
    gate_weight,
    up_weight,
    down_weight,
):
    bucket_count, head_count = bias_table.shape
    width = layer_input.shape[-1]
    layer_input, encoder_states, cotangent = layer_input[0], encoder_states[0], cotangent[0]
    gain_first, gain_second, gain_third = (
        gain.reshape(1, width) for gain in (gain_first, gain_second, gain_third)
    )
    low, full = jnp.bfloat16, jnp.float32
    grouped, rows, wide_rows, line = (4, 128, 256), (128, 768), (128, 2048), (1, 768)
    first_head = 3 * ((lax.axis_index("ctx") // 2) % 4)
    padded = jnp.pad(bucket_ids, (TILES * 128 - bucket_ids.shape[0] + 128, 0), constant_values=-1)
    last = padded.shape[0]
    ids = jnp.stack([padded[last - 255 - 128 * k : last - 128 * k] for k in range(TILES)])
    ids = jnp.pad(ids, ((0, 0), (0, 1)), constant_values=-1)
    hot = (ids[:, :, None] == jnp.arange(bucket_count, dtype=jnp.int32)).astype(jnp.float32)
    own_table = lax.dynamic_slice_in_dim(bias_table, first_head, 3, 1)
    waves = jnp.einsum("kxb,bh->hkx", hot, own_table, precision=PRECISE)
    waves = jnp.where((ids >= 0)[None], waves, NEGATIVE)

    (self_q, self_kv, cross_kv, normed_one), weights, feed = open_layer(
        layer_input,
        encoder_states,
        gain_first,
        (
            self_query, self_key, self_value, cross_key, cross_value,
            self_output, cross_query, cross_output, gate_weight, up_weight, down_weight,
        ),
        2,
    )
    w_query, w_key, w_value, w_ckey, w_cvalue, w_out, w_cquery, w_cout = weights
    (self_low, self_full, self_lse, wide), feed = attend(
        self_q, self_kv, waves, 7, ("xa", "xb"), feed, ("side",) * 4
    )
    (cross_q, attended, middle, normed_two), feed = shared_call(
        middle_kernel,
        "middle",
        (self_low, layer_input, gain_second, w_out, w_cquery),
        ((grouped, low), (rows, low), (rows, full), (rows, low)),
        row_scratch() + row_scratch(),
        3,
        feed,
        ("za", "zb", "core", "core"),
    )
    (cross_low, cross_full, cross_lse), feed = attend(
        cross_q, cross_kv, None, 8, ("core",), feed, ("core", "core", None, None)
    )
    w_gate, w_up, w_down = (whole(weight) for weight in feed)
    (
        cross_grads, layer_output, crossed, normed_three, grad_gate, grad_up, mixed,
        branch_after, grad_after, dgain_third,
    ) = shared_call(
        feed_kernel,
        "feed_forward",
        (cross_low, middle, gain_third, w_cout, w_gate, w_up, w_down, cotangent),
        (
            (grouped, low), (rows, low), (rows, low), (rows, low), (wide_rows, low),
            (wide_rows, low), (wide_rows, low), (rows, low), (rows, full), (line, full),
        ),
        row_scratch() + row_scratch() + [pltpu.VMEM(wide_rows, full)],
        4,
    )
    cross_dq, cross_dkv = attend_back(cross_q, cross_kv, cross_grads, cross_full, cross_lse, None)
    (
        self_grads, grad_cquery, cross_total, branch_middle, grad_middle, dgain_second,
    ) = shared_call(
        turn_kernel,
        "turn",
        (
            cross_dq, cross_dkv.reshape(8, 2, 128, 384), middle, gain_second, grad_after,
            w_cquery, w_out,
        ),
        (
            (grouped, low), (rows, low), ((4, 128, 384), low), (rows, low), (rows, full),
            (line, full),
        ),
        row_scratch() + row_scratch() + sum_scratch(),
        5,
    )
    self_dq, self_dkv, grad_waves = attend_back(
        self_q, self_kv, self_grads, self_full, self_lse, wide
    )
    (
        grad_input, grad_encoder, grad_queries, grad_keys, grad_values, grad_ckeys, grad_cvalues,
        dgain_first,
    ) = shared_call(
        close_kernel,
        "close",
        (
            self_dq, self_dkv.reshape(8, 2, 128, 384), layer_input, gain_first, grad_middle,
            w_query, w_key, w_value, cross_total, w_ckey, w_cvalue,
        ),
        ((rows, full), (rows, full)) + ((rows, low),) * 5 + ((line, full),),
        row_scratch()
        + [pltpu.VMEM((4, 128, 384), low)]
        + sum_scratch()
        + owner_scratch()
        + owner_scratch(),
        6,
    )
    own_grads = jnp.einsum("kxb,hkx->bh", hot, grad_waves, precision=PRECISE)
    local_table = lax.dynamic_update_slice_in_dim(
        jnp.zeros_like(bias_table), own_grads, first_head, 1
    )
    small = jnp.concatenate(
        [dgain_first[0], dgain_second[0], dgain_third[0], local_table.reshape(-1)]
    )
    small = jnp.pad(small, (0, 24 * 128 - small.shape[0])).reshape(24, 128)
    partials = outer_products(
        (
            normed_one, normed_one, normed_one, attended,
            normed_two, encoder_states, encoder_states, crossed,
        ),
        (
            grad_queries, grad_keys, grad_values, branch_middle,
            grad_cquery, grad_ckeys, grad_cvalues, branch_after,
        ),
        normed_three,
        grad_gate,
        grad_up,
        mixed,
        cotangent,
    )
    *shards, sums = reduce_weights(partials, small, 1)
    sums = sums.reshape(-1)
    return (
        layer_output[None],
        grad_input[None],
        grad_encoder[None],
        sums[3 * width : 3 * width + bucket_count * head_count].reshape(bucket_count, head_count),
        sums[:width],
        sums[width : 2 * width],
        sums[2 * width : 3 * width],
    ) + tuple(shard.astype(jnp.float32) for shard in shards)


def solution(mesh):
    placed = (
        P("dp", "ctx", None),
        P("dp", "ctx", None),
        P("dp", "ctx", None),
        P(),
        P(),
        P(),
        P(),
        P(),
        P("dp", None),
        P("dp", None),
        P("dp", None),
        P("dp", None),
        P("dp", None),
        P("dp", None),
        P("dp", None),
        P("dp", None),
        P("dp", None),
        P("dp", None),
        P("dp", None),
    )
    return jax.shard_map(
        body,
        mesh=mesh,
        in_specs=placed,
        out_specs=(
            P("dp", "ctx", None),
            P("dp", "ctx", None),
            P("dp", "ctx", None),
            P(),
            P(),
            P(),
            P(),
            P("dp", None),
            P("dp", None),
            P("dp", None),
            P("dp", None),
            P("dp", None),
            P("dp", None),
            P("dp", None),
            P("dp", None),
            P("dp", None),
            P("dp", None),
            P("dp", None),
        ),
        check_vma=False,
    )
```

```python
import functools
import math
import jax
import jax.numpy as jnp
from jax import lax
from jax.experimental import pallas as pl
from jax.experimental.pallas import tpu as pltpu
from jax.sharding import PartitionSpec as P

MESH = pl.DeviceIdType.MESH
VMEM_BYTES = 62 * 2**20
ANY = pl.BlockSpec(memory_space=pl.ANY)
HBM = pl.BlockSpec(memory_space=pltpu.HBM)
VMEM = pl.BlockSpec(memory_space=pltpu.VMEM)


class Place:
    def __init__(self):
        c = lax.axis_index("ctx")
        d = lax.axis_index("dp")
        self.c, self.d = c, d
        self.x_hi = c // 8
        self.z = (c // 2) % 4
        self.core = c % 2
        self.y = d // 2
        self.x_lo = d % 2
        self.y_a = self.y + 1 - 2 * (self.y % 2)
        self.y_b = 3 - self.y
        self.y_ab = 3 - self.y_a
        self.z_a = self.z + 1 - 2 * (self.z % 2)
        self.z_b = 3 - self.z
        self.z_ab = 3 - self.z_a
        far_lo, far_hi = 1 - self.x_lo, 1 - self.x_hi
        self.x = self.x_lo * 2 + self.x_hi
        self.x_a = far_lo * 2 + self.x_hi
        self.x_b = far_lo * 2 + far_hi
        self.x_ab = self.x_lo * 2 + far_hi
        same = self.x_hi * 8 + self.z * 2 + self.core
        self.dev = {
            "core": (self.x_hi * 8 + self.z * 2 + 1 - self.core, d),
            "ya": (same, self.y_a * 2 + self.x_lo),
            "yb": (same, self.y_b * 2 + self.x_lo),
            "za": (self.x_hi * 8 + self.z_a * 2 + self.core, d),
            "zb": (self.x_hi * 8 + self.z_b * 2 + self.core, d),
            "xa": (same, self.y * 2 + far_lo),
            "xb": (far_hi * 8 + self.z * 2 + self.core, self.y * 2 + far_lo),
            "xab": (far_hi * 8 + self.z * 2 + self.core, d),
        }

    def greet(self, names):
        barrier = pltpu.get_barrier_semaphore()
        for name in names:
            pl.semaphore_signal(
                barrier, inc=1, device_id=self.dev[name], device_id_type=MESH
            )
        pl.semaphore_wait(barrier, len(names))

    def send(self, name, src, dst, send_sem, recv_sem):
        copy = pltpu.make_async_remote_copy(
            src_ref=src,
            dst_ref=dst,
            send_sem=send_sem,
            recv_sem=recv_sem,
            device_id=self.dev[name],
            device_id_type=MESH,
        )
        copy.start()
        return copy


EARLY_PLAN = (
    ((0, "pair", 0), (1, "pair", 0), (2, "pair", 0)),
    ((3, "pair", 0), (4, "pair", 0)),
)
LATE_PLAN = (((0, "zb", 0), (1, "za", 0)), ((2, "pair", 0),))
FEED_PLAN = (((0, "za", 0), (1, "zb", 0), (2, "pair", 0)),)


class Chain:
    def __init__(self, me, source, target, kind, half, piece, pieces, sems):
        rows, cols = source.shape[-2:]
        width = cols // 2 // pieces
        self.me, self.source, self.target, self.kind = me, source, target, kind
        self.sems, self.slot, self.copies = sems, 0, []
        self.all_rows = pl.ds(0, rows)
        if kind == "pair":
            self.rows = pl.ds(half * (rows // 2), rows // 2)
            self.all_rows = self.rows
            flip = half == 1
        else:
            bit = me.z % 2 if kind == "za" else me.z // 2
            self.rows = pl.ds(pl.multiple_of(bit * (rows // 2), 16), rows // 2)
            flip = kind == "zb"
        self.cols = pl.ds(pl.multiple_of(me.core * (cols // 2) + piece * width, 128), width)
        self.other = pl.ds(pl.multiple_of((1 - me.core) * (cols // 2) + piece * width, 128), width)
        self.first, self.second = ("yb", "ya") if flip else ("ya", "yb")
        self.near = me.y_b if flip else me.y_a
        self.side = "xb" if flip else "xa"
        self.stages = 4 if kind == "pair" else 5

    def go(self, name, src, dst):
        send_sem, recv_sem, index = self.sems
        copy = self.me.send(
            name, src, dst, send_sem.at[index, self.slot], recv_sem.at[index, self.slot]
        )
        self.slot += 1
        self.copies.append(copy)
        return copy

    def hop(self, name):
        me, out = self.me, self.target
        if name == "side":
            got = out.at[:, me.x_lo, self.rows, self.cols]
            return self.go(self.side, got, got)
        if name == "core":
            got = out.at[:, :, self.all_rows, self.cols]
            return self.go("core", got, got)
        got = out.at[:, :, self.rows, self.cols]
        return self.go(self.kind, got, got)

    def run(self, stage):
        me, out = self.me, self.target
        if stage == 0:
            mine = self.source.at[self.rows, self.cols]
            spot = out.at[me.y, me.x_lo, self.rows, self.cols]
            self.first_copy = self.go(self.first, mine, spot)
            self.second_copy = self.go(self.second, mine, spot)
            self.own_copy = self.go(
                "core",
                self.source.at[self.rows, self.other],
                out.at[me.y, me.x_lo, self.rows, self.other],
            )
        elif stage == 1:
            self.first_copy.wait_recv()
            got = out.at[self.near, me.x_lo, self.rows, self.cols]
            self.third_copy = self.go(self.second, got, got)
        elif stage == 2:
            self.second_copy.wait_recv()
            self.own_copy.wait_recv()
            self.third_copy.wait_recv()
            got = out.at[:, me.x_lo, self.rows, self.cols]
            self.last = self.go(self.side, got, got)
        elif stage == 3 and self.kind != "pair":
            self.last.wait_recv()
            got = out.at[:, :, self.rows, self.cols]
            self.last = self.go(self.kind, got, got)
        elif stage == self.stages - 1:
            self.last.wait_recv()
            got = out.at[:, :, self.all_rows, self.cols]
            self.last = self.go("core", got, got)
        elif stage == self.stages:
            self.last.wait_recv()


def make_groups(me, ins, outs, plan, send_sem, recv_sem):
    pieces = {}
    for group in plan:
        for array, kind, piece in group:
            pieces[array] = max(pieces.get(array, 0), piece + 1)
    groups = []
    index = 0
    for group in plan:
        chains = []
        for array, kind, piece in group:
            for half in range(2 if kind == "pair" else 1):
                chains.append(
                    Chain(
                        me, ins[array], outs[array], kind, half, piece, pieces[array],
                        (send_sem, recv_sem, index),
                    )
                )
                index += 1
        groups.append(chains)
    return groups


def run_stage(chains, stage):
    for chain in chains:
        chain.run(stage)


def chain_count(plan):
    return sum(2 if kind == "pair" else 1 for group in plan for _, kind, _ in group)


class Staged:
    def __init__(self, source, target, sem):
        self.copy = pltpu.make_async_copy(source, target, sem)
        self.copy.start()
        self.target, self.here = target, False

    def __call__(self):
        if not self.here:
            self.copy.wait()
            self.here = True
        return self.target

    def __getitem__(self, index):
        return self()[index]

    @property
    def at(self):
        return self().at


class Shared:
    def __init__(self, ref, peer, send_sem, recv_sem):
        self.ref, self.peer, self.sems = ref, peer, (send_sem, recv_sem)

    def __getitem__(self, index):
        return self.ref[index]

    def __setitem__(self, index, value):
        self.ref[index] = value
        if index is Ellipsis:
            self.tell()

    def tell(self):
        self.copy = Place().send("core", self.ref, self.peer, *self.sems)


def staged_kernel(kernel, n_in, n_out, greet, hops, share, *refs):
    refs = list(refs)

    def take(count):
        taken = refs[:count]
        del refs[:count]
        return taken

    n_carry = 3 if hops else 0
    ins, _, outs, peers, carried, targets = (
        take(n_in), take(n_carry), take(n_out), take(len(share)), take(n_carry), take(n_in)
    )
    (sem,) = take(1)
    staged = [Staged(ref, target, sem.at[i]) for i, (ref, target) in enumerate(zip(ins, targets))]
    moved = []
    if hops:
        send_sem, recv_sem = take(2)
    if share:
        share_send, share_recv = take(2)
        for slot, index in enumerate(share):
            outs[index] = Shared(
                outs[index], peers[slot], share_send.at[slot], share_recv.at[slot]
            )
    if greet is not None:
        me = Share()
        if greet == "all":
            me.greet_all()
        else:
            me.greet(greet)
    if hops:
        (chains,) = make_groups(me, carried, carried, FEED_PLAN, send_sem, recv_sem)
        for chain, hop in zip(chains, hops):
            if hop is not None:
                moved.append(chain.hop(hop))
    if greet != "all":
        staged = [ref() for ref in staged]
    kernel(*staged, *outs, *refs)
    if greet == "all":
        for ref in staged:
            ref()
    for copy in moved:
        copy.wait()
    for index in share:
        outs[index].copy.wait()


def staged_call(
    kernel, name, args, shapes, scratch, collective_id=None, greet=None, carry=(), hops=(), share=()
):
    carry = tuple(carry)
    shapes = tuple(shapes)
    n_out = len(shapes)
    shapes = shapes + tuple(shapes[index] for index in share)
    outs = pl.pallas_call(
        functools.partial(staged_kernel, kernel, len(args), n_out, greet, hops, tuple(share)),
        out_shape=[jax.ShapeDtypeStruct(shape, kind) for shape, kind in shapes]
        + [jax.ShapeDtypeStruct(array.shape, array.dtype) for array in carry],
        in_specs=[HBM] * len(args) + [ANY] * len(carry),
        out_specs=[VMEM] * len(shapes) + [ANY] * len(carry),
        scratch_shapes=[pltpu.VMEM(arg.shape, arg.dtype) for arg in args]
        + [pltpu.SemaphoreType.DMA((len(args),))]
        + ([pltpu.SemaphoreType.DMA((4, 7))] * 2 if hops else [])
        + ([pltpu.SemaphoreType.DMA((len(share),))] * 2 if share else [])
        + scratch,
        input_output_aliases={len(args) + i: len(shapes) + i for i in range(len(carry))},
        compiler_params=pltpu.CompilerParams(
            collective_id=collective_id,
            has_side_effects=greet is not None,
            vmem_limit_bytes=VMEM_BYTES,
        ),
        name=name,
    )(*args, *carry)
    return (outs[: len(shapes)], outs[len(shapes) :]) if carry else outs

AXES = ("y", "x", "z")


ACT_OF = (0, 0, 0, 1, 2, 3, 3, 4)


class Outer:
    def __init__(self, me, ins, acc, acts, grads, feeds, cots, turned, mixed_t, sem):
        self.me, self.acc = me, acc
        self.acts, self.grads, self.feeds, self.cots = acts, grads, feeds, cots
        self.turned, self.mixed_t = turned, mixed_t
        self.copies = []
        half = pl.ds(pl.multiple_of(me.core * 384, 128), 384)
        for side in range(2):
            begin = pl.ds(128 * side, 128)
            own = ins[18 * side : 18 * side + 18]
            for index in range(6):
                self.fetch(own[index], acts.at[index, begin], sem)
            for index in range(8):
                self.fetch(own[6 + index].at[:, half], grads.at[index, begin], sem)
            for index in range(3):
                self.fetch(own[14 + index], feeds.at[index, begin], sem)
            self.fetch(own[17], cots.at[begin], sem)

    def fetch(self, src, dst, sem):
        copy = pltpu.make_async_copy(src, dst, sem.at[len(self.copies)])
        copy.start()
        self.copies.append(copy)

    def ready(self):
        for copy in self.copies:
            copy.wait()
        for index in range(6):
            self.turned[index] = self.acts[index].T.reshape(8, 6, 16, 256)
        self.mixed_t[...] = self.feeds[2].T.reshape(8, 8, 2, 16, 256)

    def put(self, part, block, cols, value):
        width = value.shape[1]
        value = value.astype(jnp.bfloat16).reshape(4, 2, 16, width)
        for x_lo in range(2):
            self.acc[part, :, 2 * x_lo + block // 4, block % 4, :, cols] = value[:, x_lo]

    def compute(self, part):
        def dot(left, right):
            return jnp.dot(left, right, preferred_element_type=jnp.float32)

        for index in range(8):
            left = self.turned[ACT_OF[index], :, part].reshape(128, 256)
            self.put(part, index, slice(0, 384), dot(left, self.grads[index]))
        left = self.turned[5, :, part].reshape(128, 256)
        for block in range(8):
            cols = pl.ds(pl.multiple_of((2 * block + self.me.core) * 128, 128), 128)
            right = jnp.concatenate([self.feeds[0, :, cols], self.feeds[1, :, cols]], axis=1)
            self.put(part, block, slice(384, 640), dot(left, right))
        left = self.mixed_t[:, :, self.me.core].reshape(1024, 256)
        down = dot(left, self.cots[:, 128 * part : 128 * part + 128])
        down = down.astype(jnp.bfloat16).reshape(4, 2, 2, 4, 16, 128)
        for x_lo in range(2):
            for x_hi in range(2):
                self.acc[part, :, 2 * x_lo + x_hi, :, :, 640:768] = down[:, x_lo, x_hi]


def reduce_kernel(*refs):
    ins, small = refs[:36], refs[36]
    full, small_out = refs[37:39]
    (acc, r1, r2, r3, r4, r5, r6, sm_in,
     send_sem, recv_sem, sm_send, sm_recv, ag_send, ag_recv, *outer) = refs[39:]
    recvs = (r1, r2, r3, r4, r5, r6)
    me = Place()
    outer = Outer(me, ins, acc, *outer)
    me.greet(("core", "ya", "yb", "xa", "xb", "za", "zb", "xab"))
    spots = {
        "y": (me.y, me.y_a, me.y_b, me.y_ab),
        "x": (me.x, me.x_a, me.x_b, me.x_ab),
        "z": (me.z, me.z_a, me.z_b, me.z_ab),
    }
    parts = range(6)
    started = []

    def go(name, src, dst, send, recv):
        copy = me.send(name, src, dst, send, recv)
        started.append(copy)
        return copy

    small_out[...] = small[...]
    small_steps = ("core", "ya", "yb", "xa", "xb", "za", "zb")
    small_copies = []

    def small_start(step):
        small_copies.append(
            me.send(small_steps[step], small_out, sm_in.at[step], sm_send.at[step], sm_recv.at[step])
        )

    def small_end(step):
        small_copies[step].wait()
        small_out[...] = small_out[...] + sm_in[step]

    small_start(0)

    def order(part):
        first = (part // 2) % 3
        return [AXES[(first + k) % 3] for k in range(3)]

    def region(part, picks):
        return (part,) + tuple(picks.get(axis, slice(None)) for axis in AXES)

    def at(ref, index):
        return ref.at[index]

    def add(index, source, source_index):
        acc[index] = acc[index] + source[source_index]

    def dims(part):
        return ("a", "b") if part % 2 == 0 else ("b", "a")

    outer.ready()
    pending = {}
    for part in parts:
        axis = order(part)[0]
        me_at, a_at, b_at, ab_at = spots[axis]
        first, second = dims(part)
        sent = (a_at, ab_at) if first == "a" else (b_at, ab_at)
        outer.compute(part)
        pending[part] = []
        for slot, spot in enumerate(sent):
            pending[part].append(
                go(
                    axis + first,
                    at(acc, region(part, {axis: spot})),
                    r1.at[part, slot],
                    send_sem.at[part, 1 + slot],
                    recv_sem.at[part, 1 + slot],
                )
            )
    small_end(0)
    small_start(1)
    sem_at = {part: 3 for part in parts}

    def next_sem(part):
        sem_at[part] += 1
        return send_sem.at[part, sem_at[part] - 1], recv_sem.at[part, sem_at[part] - 1]

    for level in range(3):
        one, two = recvs[2 * level], recvs[2 * level + 1]
        for part in parts:
            axes = order(part)
            axis = axes[level]
            first, second = dims(part)
            me_at, a_at, b_at, ab_at = spots[axis]
            kept = b_at if first == "a" else a_at
            fixed = {name: spots[name][0] for name in axes[:level]}
            for copy in pending[part]:
                copy.wait_recv()
            add(region(part, {**fixed, axis: kept}), one, (part, 1))
            send, recv = next_sem(part)
            pending[part] = [
                go(axis + second, at(acc, region(part, {**fixed, axis: kept})), two.at[part], send, recv)
            ]
        for part in parts:
            axes = order(part)
            fixed = {name: spots[name][0] for name in axes[: level + 1]}
            add(region(part, fixed), one, (part, 0))
        small_end(2 * level + 1)
        small_start(2 * level + 2)
        for part in parts:
            axes = order(part)
            fixed = {name: spots[name][0] for name in axes[: level + 1]}
            for copy in pending[part]:
                copy.wait_recv()
            add(region(part, fixed), two, (part,))
            if level == 2:
                continue
            axis = axes[level + 1]
            first, second = dims(part)
            me_at, a_at, b_at, ab_at = spots[axis]
            sent = (a_at, ab_at) if first == "a" else (b_at, ab_at)
            pending[part] = []
            for slot, spot in enumerate(sent):
                send, recv = next_sem(part)
                pending[part].append(
                    go(
                        axis + first,
                        at(acc, region(part, {**fixed, axis: spot})),
                        recvs[2 * level + 2].at[part, slot],
                        send,
                        recv,
                    )
                )
        small_end(2 * level + 2)
        if level < 2:
            small_start(2 * level + 3)

    here = me.x_hi * 4 + me.z
    there = (1 - me.x_hi) * 4 + me.z
    for part in parts:
        full[here, me.core, part] = acc[part, me.y, me.x, me.z]
    used = [0]

    def pass_on(name, group, half):
        index = used[0]
        used[0] += 1
        src = full.at[group, me.core, pl.ds(3 * half, 3)]
        return go(name, src, src, ag_send.at[index], ag_recv.at[index])

    early = [pass_on("xab", here, half) for half in range(2)]
    near = [pass_on("za", here, 0), pass_on("zb", here, 1)]
    far = []
    for half in range(2):
        early[half].wait_recv()
        far.append(pass_on(("za", "zb")[half], there, half))
    base, base_far = me.x_hi * 4, (1 - me.x_hi) * 4
    ends = [pass_on("zb", here, 0), pass_on("za", here, 1)]
    ends += [pass_on("zb", there, 0), pass_on("za", there, 1)]
    for half in range(2):
        got = (me.z_a, me.z_b)[half]
        near[half].wait_recv()
        ends.append(pass_on(("zb", "za")[half], base + got, half))
    for half in range(2):
        got = (me.z_a, me.z_b)[half]
        far[half].wait_recv()
        ends.append(pass_on(("zb", "za")[half], base_far + got, half))
    for copy in ends:
        copy.wait_recv()
    last = go("core", full.at[:, me.core], full.at[:, me.core], ag_send.at[used[0]], ag_recv.at[used[0]])

    last.wait_recv()
    for copy in started:
        copy.wait_send()


def reduce_weights(own, peer, small, collective_id):
    bf = jnp.bfloat16
    return pl.pallas_call(
        reduce_kernel,
        out_shape=[
            jax.ShapeDtypeStruct((8, 2, 6, 16, 768), bf),
            jax.ShapeDtypeStruct(small.shape, small.dtype),
        ],
        in_specs=[HBM] * 36 + [VMEM],
        out_specs=[VMEM] * 2,
        scratch_shapes=[
            pltpu.VMEM((6, 4, 4, 4, 16, 768), bf),
            pltpu.VMEM((6, 2, 4, 4, 16, 768), bf),
            pltpu.VMEM((6, 4, 4, 16, 768), bf),
            pltpu.VMEM((6, 2, 4, 16, 768), bf),
            pltpu.VMEM((6, 4, 16, 768), bf),
            pltpu.VMEM((6, 2, 16, 768), bf),
            pltpu.VMEM((6, 16, 768), bf),
            pltpu.VMEM((7,) + small.shape, small.dtype),
            pltpu.SemaphoreType.DMA((6, 10)),
            pltpu.SemaphoreType.DMA((6, 10)),
            pltpu.SemaphoreType.DMA((7,)),
            pltpu.SemaphoreType.DMA((7,)),
            pltpu.SemaphoreType.DMA((16,)),
            pltpu.SemaphoreType.DMA((16,)),
            pltpu.VMEM((6, 256, 768), bf),
            pltpu.VMEM((8, 256, 384), bf),
            pltpu.VMEM((3, 256, 2048), bf),
            pltpu.VMEM((256, 768), bf),
            pltpu.VMEM((6, 8, 6, 16, 256), bf),
            pltpu.VMEM((8, 8, 2, 16, 256), bf),
            pltpu.SemaphoreType.DMA((36,)),
        ],
        compiler_params=pltpu.CompilerParams(
            collective_id=collective_id, has_side_effects=True, vmem_limit_bytes=VMEM_BYTES
        ),
        name="reduce_weights",
    )(*own, *peer, small)


def place_kernel(full, *refs):
    passed, outs = refs[:3], refs[3:]
    wide = jnp.float32
    for o in range(16):
        group, core = o // 2, o % 2
        for part in range(6):
            rows = slice(16 * part, 16 * part + 16)
            block = full[group, core, part]
            outs[group][rows, core * 384 : core * 384 + 384] = block[:, 0:384].astype(wide)
            outs[8][rows, 128 * o : 128 * o + 128] = block[:, 384:512].astype(wide)
            outs[9][rows, 128 * o : 128 * o + 128] = block[:, 512:640].astype(wide)
            outs[10][16 * o : 16 * o + 16, 128 * part : 128 * part + 128] = block[
                :, 640:768
            ].astype(wide)
    for source, target in zip(passed, outs[11:]):
        target[...] = source[...]


def place_all(full, passed):
    wide = jnp.float32
    shapes = [((96, 768), wide)] * 8 + [((96, 2048), wide)] * 2 + [((256, 768), wide)]
    shapes += [(array.shape, array.dtype) for array in passed]
    return staged_call(place_kernel, "place", (full,) + tuple(passed), shapes, [])

NEGATIVE = -1e30
EPSILON = 1e-06
TILES = 23
USED = 16


class Share(Place):
    def __init__(self):
        super().__init__()
        self.dev["zab"] = (self.x_hi * 8 + self.z_ab * 2 + self.core, self.d)
        self.mine = self.x_hi * 2 + self.core
        self.slot = self.c // 4
        rest = self.c % 4
        self.owner = rest + (self.slot % 2) * (3 - 2 * rest)
        self.at_home = self.owner == self.mine

    def block(self, slot):
        return 4 * slot + (self.mine if slot % 2 == 0 else 3 - self.mine)

    def worker(self, group):
        return (self.owner // 2) * 8 + group * 2 + self.owner % 2

    def greet_all(self, extra=()):
        barrier = pltpu.get_barrier_semaphore()
        for name in extra:
            pl.semaphore_signal(
                barrier, inc=1, device_id=self.dev[name], device_id_type=MESH
            )
        for step in range(1, 16):
            pl.semaphore_signal(
                barrier, inc=1, device_id=((self.c + step) % 16, self.d), device_id_type=MESH
            )
        pl.semaphore_wait(barrier, 15 + len(extra))

    def copy_to(self, ctx, src, dst, send_sem, recv_sem):
        return pltpu.make_async_remote_copy(
            src_ref=src,
            dst_ref=dst,
            send_sem=send_sem,
            recv_sem=recv_sem,
            device_id=(ctx, self.d),
            device_id_type=MESH,
        )


class Rows:
    def __init__(self, me, src, dst, send_sem, recv_sem, back):
        self.me, self.src, self.dst = me, src, dst
        self.send_sem, self.recv_sem, self.back = send_sem, recv_sem, back

    def to_worker(self, group, ours):
        me = self.me
        away = jnp.logical_not(jnp.logical_and(me.at_home, me.z == group))
        if self.back:
            copy = me.copy_to(
                me.worker(group), self.src.at[0], self.dst.at[group],
                self.send_sem.at[0], self.recv_sem.at[group],
            )
        else:
            copy = me.copy_to(
                me.worker(group), self.src.at[group], self.dst.at[me.slot],
                self.send_sem.at[group], self.recv_sem.at[me.slot],
            )
        return away, copy

    def to_home(self, slot):
        me = self.me
        away = me.block(slot) != me.c
        if self.back:
            copy = me.copy_to(
                me.block(slot), self.src.at[slot], self.dst.at[me.z],
                self.send_sem.at[slot], self.recv_sem.at[me.z],
            )
        else:
            copy = me.copy_to(
                me.block(slot), self.src.at[0], self.dst.at[slot],
                self.send_sem.at[0], self.recv_sem.at[slot],
            )
        return away, copy

    def each(self, sending, action):
        for index in range(4):
            if sending != self.back:
                away, copy = self.to_worker(index, sending)
            else:
                away, copy = self.to_home(index)

            @pl.when(away)
            def _():
                action(copy)

    def start(self):
        me = self.me
        self.each(True, lambda copy: copy.start())

        @pl.when(me.at_home)
        def _():
            if self.back:
                self.dst[me.z] = self.src[me.slot]
            else:
                self.dst[me.slot] = self.src[me.z]

    def arrive(self):
        self.each(False, lambda copy: copy.wait_recv())

    def end(self):
        self.each(True, lambda copy: copy.wait_send())


class Pairs:
    def __init__(self, me, src, out, send_sem, recv_sem):
        self.me, self.src, self.out = me, src, out
        self.send_sem, self.recv_sem, self.done = send_sem, recv_sem, []
        self.groups = (me.z_a, me.z_b, me.z_ab)

    def go(self, name, src, dst, slot):
        copy = self.me.send(name, src, dst, self.send_sem.at[slot], self.recv_sem.at[slot])
        self.done.append(copy)
        return copy

    def start(self):
        me = self.me
        self.out[me.c] = self.src[me.z]
        self.first = [
            self.go(name, self.src.at[group], self.out.at[me.c], slot)
            for slot, (name, group) in enumerate(zip(("za", "zb", "zab"), self.groups))
        ]
        self.over_x, self.over_core = [], []
        self.pass_on(0)

    def pass_on(self, step):
        me = self.me
        block = me.x_hi * 8 + ((me.z,) + self.groups)[step] * 2 + me.core
        spot = self.out.at[block]
        self.over_x.append(self.go("xab", spot, spot, 3 + step))
        self.over_core.append(self.go("core", spot, spot, 7 + step))

    def second(self):
        for step in range(1, 4):
            self.first[step - 1].wait_recv()
            self.pass_on(step)

    def third(self):
        me = self.me
        for step, group in enumerate((me.z,) + self.groups):
            self.over_x[step].wait_recv()
            spot = self.out.at[(1 - me.x_hi) * 8 + group * 2 + me.core]
            self.over_core.append(self.go("core", spot, spot, 11 + step))

    def arrive(self):
        for copy in self.over_core:
            copy.wait_recv()

    def end(self):
        for copy in self.done:
            copy.wait_send()


class Sums:
    def __init__(self, me, src, total, send_sem, recv_sem, got_core, part, got_x):
        self.me, self.src, self.total = me, src, total
        self.send_sem, self.recv_sem, self.done = send_sem, recv_sem, []
        self.got_core, self.part, self.got_x = got_core, part, got_x
        self.order = (me.z_ab, me.z_a, me.z_b, me.z)

    def go(self, name, src, dst, slot):
        copy = self.me.send(name, src, dst, self.send_sem.at[slot], self.recv_sem.at[slot])
        self.done.append(copy)
        return copy

    def start(self):
        me = self.me
        self.near, self.far = me.x_hi * 4, (1 - me.x_hi) * 4
        self.core_copies = [
            self.go(
                "core",
                self.src.at[side + group, 1 - me.core],
                self.got_core.at[side + group],
                4 * index + step,
            )
            for index, side in enumerate((self.far, self.near))
            for step, group in enumerate(self.order)
        ]

    def over(self):
        me = self.me
        self.over_x = []
        for step, group in enumerate(self.order):
            self.core_copies[step].wait_recv()
            block = self.far + group
            self.part[block] = self.src[block, me.core] + self.got_core[block]
            self.over_x.append(self.go("xab", self.part.at[block], self.got_x.at[group], 8 + step))
        for step, group in enumerate(self.order):
            self.core_copies[4 + step].wait_recv()
            block = self.near + group
            self.part[block] = self.src[block, me.core] + self.got_core[block]

    def finish(self, then=None):
        for step, group in enumerate(self.order):
            self.over_x[step].wait_recv()
            self.total[group] = self.part[self.near + group] + self.got_x[group]
            if then is not None and step < 3:
                then.send(step)

    def end(self):
        for copy in self.done:
            copy.wait_send()


class Owners:
    def __init__(self, me, total, out, send_sem, recv_sem):
        self.me, self.total, self.out = me, total, out
        self.send_sem, self.recv_sem, self.copies = send_sem, recv_sem, []

    def send(self, step):
        me = self.me
        group, name = ((me.z_ab, "zab"), (me.z_a, "za"), (me.z_b, "zb"))[step]
        self.copies.append(
            me.send(
                name, self.total.at[group], self.out.at[me.z],
                self.send_sem.at[step], self.recv_sem.at[step],
            )
        )

    def arrive(self):
        self.out[self.me.z] = self.total[self.me.z]
        for copy in self.copies:
            copy.wait_recv()

    def end(self):
        for copy in self.copies:
            copy.wait_send()


def lane_mask(value, begin, end):
    lane = lax.broadcasted_iota(jnp.int32, value.shape, 1)
    return jnp.where(jnp.logical_and(lane >= begin, lane < end), value, jnp.zeros_like(value))


def cut_heads(value, after):
    groups = []
    for half in range(2):
        left = value[:, 384 * half : 384 * half + 256]
        right = value[:, 384 * half + 128 : 384 * half + 384]
        if after:
            groups += [lane_mask(left, 0, 192), lane_mask(pltpu.roll(right, 192, 1), 0, 192)]
        else:
            groups += [lane_mask(pltpu.roll(left, 64, 1), 64, 256), lane_mask(right, 64, 256)]
    return groups


def join_heads(groups, after):
    pieces = []
    for half in range(2):
        left, right = groups[2 * half], groups[2 * half + 1]
        if after:
            right = pltpu.roll(right, 64, 1)
        else:
            left = pltpu.roll(left, 192, 1)
        pieces += [left[:, :128], left[:, 128:] + right[:, :128], right[:, 128:]]
    return jnp.concatenate(pieces, axis=1)


def put_rows(ref, value, after):
    for group, part in enumerate(cut_heads(value, after)):
        ref[group] = part.astype(jnp.bfloat16)


def get_rows(ref, after):
    return join_heads([ref[group].astype(jnp.float32) for group in range(4)], after)


def put_pairs(ref, keys, values):
    for group, (left, right) in enumerate(zip(cut_heads(keys, True), cut_heads(values, False))):
        ref[group, :, 0:128] = left[:, :128].astype(jnp.bfloat16)
        ref[group, :, 128:256] = (left[:, 128:] + right[:, :128]).astype(jnp.bfloat16)
        ref[group, :, 256:384] = right[:, 128:].astype(jnp.bfloat16)


def get_pairs(ref):
    keys = [lane_mask(ref[group, :, 0:256].astype(jnp.float32), 0, 192) for group in range(4)]
    values = [lane_mask(ref[group, :, 128:384].astype(jnp.float32), 64, 256) for group in range(4)]
    return join_heads(keys, True), join_heads(values, False)


def scale_of(value):
    return lax.rsqrt(jnp.mean(value * value, axis=-1, keepdims=True) + EPSILON)


def norm_back(value, gain, grad):
    scale = scale_of(value)
    weighted = grad * gain
    middle = jnp.mean(value * weighted, axis=-1, keepdims=True)
    dgain = jnp.sum(grad * (value * scale), axis=0, keepdims=True)
    return scale * weighted - value * (scale * scale * scale) * middle, dgain


def open_kernel(
    layer_input, encoder, gain, cotangent, *refs
):
    shards = refs[:11]
    q_out, kv_out, ckv_out, normed_out, normed_peer, encoder_peer, cotangent_peer = refs[11:18]
    outs = refs[18:29]
    (q_mine, kv_mine, ckv_mine, q_send, q_recv, kv_send, kv_recv, ckv_send, ckv_recv,
     early_send, early_recv, late_send, late_recv, feed_send, feed_recv, held, held_sem,
     share_send, share_recv) = refs[29:]
    me = Share()
    me.greet_all(extra=("ya", "yb", "xa", "xb"))
    early = make_groups(me, shards[:5], outs[:5], EARLY_PLAN, early_send, early_recv)
    late = make_groups(me, shards[5:8], outs[5:8], LATE_PLAN, late_send, late_recv)
    feed = make_groups(me, shards[8:], outs[8:], FEED_PLAN, feed_send, feed_recv)
    run_stage(early[0], 0)
    run_stage(early[1], 0)
    run_stage(late[0], 0)
    run_stage(late[1], 0)
    run_stage(early[0], 1)
    run_stage(early[1], 1)
    run_stage(feed[0], 0)
    run_stage(early[0], 2)
    run_stage(early[1], 2)
    residual = layer_input[...].astype(jnp.float32)
    normed = (residual * scale_of(residual) * gain[...]).astype(jnp.bfloat16)
    normed_out[...] = normed
    shared = [
        me.send("core", src, dst, share_send.at[slot], share_recv.at[slot])
        for slot, (src, dst) in enumerate(
            ((normed_out, normed_peer), (encoder, encoder_peer), (cotangent, cotangent_peer))
        )
    ]
    run_stage(late[0], 1)
    run_stage(late[1], 1)
    run_stage(early[0], 3)
    run_stage(early[1], 3)
    run_stage(late[0], 2)
    run_stage(late[1], 2)
    run_stage(early[0], 4)

    def fetch(index):
        fetched = []
        for y in range(4):
            for x in range(2):
                begin = 96 * (2 * y + x)
                fetched.append(
                    pltpu.make_async_copy(
                        outs[index].at[y, x],
                        held.at[index, pl.ds(begin, 96)],
                        held_sem.at[index, 2 * y + x],
                    )
                )
                fetched[-1].start()
        return fetched

    def wait_all(copies):
        for copy in copies:
            copy.wait()

    fetched = [fetch(index) for index in range(3)]
    run_stage(early[1], 4)
    fetched += [fetch(index) for index in range(3, 5)]
    wait_all(fetched[1])
    wait_all(fetched[2])
    put_pairs(kv_mine, dot_nn(normed, held[1]), dot_nn(normed, held[2]))
    self_kv = Pairs(me, kv_mine, kv_out, kv_send, kv_recv)
    self_kv.start()
    wait_all(fetched[0])
    put_rows(q_mine, dot_nn(normed, held[0]), True)
    rows = Rows(me, q_mine, q_out, q_send, q_recv, False)
    rows.start()
    wait_all(fetched[3])
    wait_all(fetched[4])
    put_pairs(ckv_mine, dot_nn(encoder[...], held[3]), dot_nn(encoder[...], held[4]))
    cross_kv = Pairs(me, ckv_mine, ckv_out, ckv_send, ckv_recv)
    cross_kv.start()
    run_stage(late[0], 3)
    self_kv.second()
    cross_kv.second()
    run_stage(late[1], 3)
    run_stage(late[0], 4)
    run_stage(feed[0], 1)
    self_kv.third()
    run_stage(late[1], 4)
    run_stage(late[0], 5)
    cross_kv.third()
    rows.arrive()
    self_kv.arrive()
    cross_kv.arrive()
    for chain in feed[0]:
        chain.second_copy.wait_recv()
        chain.third_copy.wait_recv()
        chain.own_copy.wait_recv()
    for chains in early + late + feed:
        for chain in chains:
            wait_sent(chain.copies)
    rows.end()
    self_kv.end()
    cross_kv.end()
    for copy in shared:
        copy.wait()


def wait_sent(copies):
    for copy in copies:
        copy.wait_send()


def open_layer(layer_input, encoder, gain, cotangent, shards, collective_id):
    bf = jnp.bfloat16
    early, late = chain_count(EARLY_PLAN), chain_count(LATE_PLAN)
    outs = pl.pallas_call(
        open_kernel,
        out_shape=[
            jax.ShapeDtypeStruct((4, 128, 256), bf),
            jax.ShapeDtypeStruct((16, 128, 384), bf),
            jax.ShapeDtypeStruct((16, 128, 384), bf),
        ]
        + [jax.ShapeDtypeStruct((128, 768), bf)] * 4
        + [jax.ShapeDtypeStruct((4, 2) + shard.shape, bf) for shard in shards],
        in_specs=[VMEM] * 3 + [ANY] * 12,
        out_specs=[VMEM] * 6 + [ANY] * 12,
        scratch_shapes=[
            pltpu.VMEM((4, 128, 256), bf),
            pltpu.VMEM((4, 128, 384), bf),
            pltpu.VMEM((4, 128, 384), bf),
            pltpu.SemaphoreType.DMA((4,)),
            pltpu.SemaphoreType.DMA((4,)),
            pltpu.SemaphoreType.DMA((15,)),
            pltpu.SemaphoreType.DMA((15,)),
            pltpu.SemaphoreType.DMA((15,)),
            pltpu.SemaphoreType.DMA((15,)),
            pltpu.SemaphoreType.DMA((early, 7)),
            pltpu.SemaphoreType.DMA((early, 7)),
            pltpu.SemaphoreType.DMA((late, 7)),
            pltpu.SemaphoreType.DMA((late, 7)),
            pltpu.SemaphoreType.DMA((4, 7)),
            pltpu.SemaphoreType.DMA((4, 7)),
            pltpu.VMEM((5, 768, 768), bf),
            pltpu.SemaphoreType.DMA((5, 8)),
            pltpu.SemaphoreType.DMA((3,)),
            pltpu.SemaphoreType.DMA((3,)),
        ],
        compiler_params=pltpu.CompilerParams(
            collective_id=collective_id, has_side_effects=True, vmem_limit_bytes=VMEM_BYTES
        ),
        name="open_layer",
    )(layer_input, encoder, gain, cotangent, *shards)
    return outs[:7], [whole(out) for out in outs[7:15]], outs[15:]


def whole(gathered):
    return gathered.reshape(8 * gathered.shape[2], gathered.shape[3])


def row_scratch():
    return [
        pltpu.VMEM((4, 128, 256), jnp.bfloat16),
        pltpu.SemaphoreType.DMA((4,)),
        pltpu.SemaphoreType.DMA((4,)),
    ]


def sum_scratch():
    bf = jnp.bfloat16
    return [
        pltpu.SemaphoreType.DMA((12,)),
        pltpu.SemaphoreType.DMA((12,)),
        pltpu.VMEM((8, 128, 384), bf),
        pltpu.VMEM((8, 128, 384), bf),
        pltpu.VMEM((4, 128, 384), bf),
    ]


def owner_scratch():
    return [
        pltpu.VMEM((4, 128, 384), jnp.bfloat16),
        pltpu.SemaphoreType.DMA((3,)),
        pltpu.SemaphoreType.DMA((3,)),
    ]


def shared_call(
    kernel, name, args, shapes, scratch, collective_id, carry=(), hops=(), share=()
):
    return staged_call(
        kernel, name, args, shapes, scratch, collective_id, "all", carry, hops, share
    )


def middle_kernel(
    o_in, layer_input, gain, w_out, w_query,
    q_out, attended_out, middle_out, normed_out,
    o_mine, o_send, o_recv, q_mine, q_send, q_recv,
):
    me = Share()
    back = Rows(me, o_in, o_mine, o_send, o_recv, True)
    back.start()
    back.arrive()
    attended = get_rows(o_mine, False).astype(jnp.bfloat16)
    middle = layer_input[...].astype(jnp.float32) + dot_nn(attended, w_out[...])
    normed = (middle * scale_of(middle) * gain[...]).astype(jnp.bfloat16)
    put_rows(q_mine, dot_nn(normed, w_query[...]), True)
    rows = Rows(me, q_mine, q_out, q_send, q_recv, False)
    rows.start()
    attended_out[...] = attended
    middle_out[...] = middle
    normed_out[...] = normed
    rows.arrive()
    back.end()
    rows.end()


def feed_kernel(
    o_in, middle, gain, w_out, w_gate, w_up, w_down, cotangent,
    g_out, final_out, crossed_out, normed_out, grad_gate, grad_up, mixed, branch_out, after_out,
    dgain_out,
    o_mine, o_send, o_recv, g_mine, g_send, g_recv, grad_mixed,
):
    low = jnp.bfloat16
    me = Share()
    back = Rows(me, o_in, o_mine, o_send, o_recv, True)
    back.start()
    grad_mixed[...] = dot_nt(cotangent[...], w_down[...])
    back.arrive()
    crossed = get_rows(o_mine, False).astype(low)
    crossed_out[...] = crossed
    after = middle[...] + dot_nn(crossed, w_out[...])
    normed = (after * scale_of(after) * gain[...]).astype(low)
    normed_out[...] = normed
    root = math.sqrt(2.0 / math.pi)
    for chunk in range(8):
        cols = slice(256 * chunk, 256 * chunk + 256)
        gate = dot_nn(normed, w_gate[:, cols])
        up = dot_nn(normed, w_up[:, cols])
        square = gate * gate
        curve = jnp.tanh(root * gate * (1.0 + 0.044715 * square))
        half = 0.5 * (1.0 + curve)
        gelu = gate * half
        slope = half + 0.5 * gate * (1.0 - curve * curve) * (
            root * (1.0 + 3 * 0.044715 * square)
        )
        incoming = grad_mixed[:, cols]
        mixed[:, cols] = (gelu * up).astype(low)
        grad_gate[:, cols] = (incoming * up * slope).astype(low)
        grad_up[:, cols] = (incoming * gelu).astype(low)
    for ref in (mixed, grad_gate, grad_up):
        ref.tell()
    grad_normed = dot_nt(grad_gate[...], w_gate[...]) + dot_nt(grad_up[...], w_up[...])
    grad_value, dgain = norm_back(after, gain[...], grad_normed)
    dgain_out[...] = dgain
    grad_after = cotangent[...].astype(jnp.float32) + grad_value
    branch = grad_after.astype(low)
    put_rows(g_mine, dot_nt(branch, w_out[...]), False)
    rows = Rows(me, g_mine, g_out, g_send, g_recv, False)
    rows.start()
    branch_out[...] = branch
    after_out[...] = grad_after
    final_out[...] = (after + dot_nn(mixed[...], w_down[...])).astype(low)
    rows.arrive()
    back.end()
    rows.end()


def turn_kernel(
    dq_in, dkv_in, middle, gain, grad_after, w_query, w_out,
    g_out, dq_out, total_out, branch_out, grad_out, dgain_out,
    dq_mine, dq_send, dq_recv, g_mine, g_send, g_recv, *sums,
):
    low = jnp.bfloat16
    me = Share()
    back = Rows(me, dq_in, dq_mine, dq_send, dq_recv, True)
    back.start()
    pairs = Sums(me, dkv_in, total_out, *sums)
    pairs.start()
    back.arrive()
    grad_query = get_rows(dq_mine, True).astype(low)
    dq_out[...] = grad_query
    grad_value, dgain = norm_back(middle[...], gain[...], dot_nt(grad_query, w_query[...]))
    dgain_out[...] = dgain
    grad_middle = grad_after[...] + grad_value
    branch = grad_middle.astype(low)
    put_rows(g_mine, dot_nt(branch, w_out[...]), False)
    rows = Rows(me, g_mine, g_out, g_send, g_recv, False)
    rows.start()
    pairs.over()
    grad_out[...] = grad_middle
    branch_out[...] = branch
    pairs.finish()
    rows.arrive()
    back.end()
    rows.end()
    pairs.end()


def close_kernel(
    dq_in, dkv_in, layer_input, gain, grad_middle, w_query, w_key, w_value,
    cross_total, w_ckey, w_cvalue,
    grad_out, encoder_out, dq_out, dk_out, dv_out, cross_dk, cross_dv, dgain_out,
    dq_mine, dq_send, dq_recv, total, *scratch,
):
    low = jnp.bfloat16
    me = Share()
    sums, self_own, cross_own = scratch[:5], scratch[5:8], scratch[8:11]
    pairs = Sums(me, dkv_in, total, *sums)
    pairs.start()
    back = Rows(me, dq_in, dq_mine, dq_send, dq_recv, True)
    back.start()
    cross = Owners(me, cross_total(), *cross_own)
    for step in range(3):
        cross.send(step)
    pairs.over()
    cross.arrive()
    keys, values = get_pairs(cross_own[0])
    keys, values = keys.astype(low), values.astype(low)
    cross_dk[...] = keys
    cross_dv[...] = values
    encoder_out[...] = dot_nt(keys, w_ckey[...]) + dot_nt(values, w_cvalue[...])
    back.arrive()
    grad_query = get_rows(dq_mine, True).astype(low)
    dq_out[...] = grad_query
    grad_normed = dot_nt(grad_query, w_query[...])
    owners = Owners(me, total, *self_own)
    pairs.finish(owners)
    owners.arrive()
    keys, values = get_pairs(self_own[0])
    keys, values = keys.astype(low), values.astype(low)
    dk_out[...] = keys
    dv_out[...] = values
    grad_normed = grad_normed + dot_nt(keys, w_key[...]) + dot_nt(values, w_value[...])
    residual = layer_input[...].astype(jnp.float32)
    grad_value, dgain = norm_back(residual, gain[...], grad_normed)
    dgain_out[...] = dgain
    grad_out[...] = grad_middle[...] + grad_value
    back.end()
    pairs.end()
    cross.end()
    owners.end()


def dot_nn(left, right):
    return jnp.dot(left, right, preferred_element_type=jnp.float32)


def dot_nt(left, right):
    return lax.dot_general(
        left, right, (((1,), (1,)), ((), ())), preferred_element_type=jnp.float32
    )


def head_lanes(value, head):
    lane = lax.broadcasted_iota(jnp.int32, value.shape, 1)
    return jnp.where(lane // 64 == head, value, jnp.zeros_like(value))


def head_rows(value, head):
    row = lax.broadcasted_iota(jnp.int32, value.shape, 0)
    return jnp.where(row // 64 == head, value, jnp.zeros_like(value))


def bias_offset(pair, side, chunk):
    c = lax.axis_index("ctx")
    mine = (c // 8) * 2 + c % 2
    block = 8 * pair + (mine if side == 0 else 7 - mine)
    return pl.multiple_of((15 - block) * 128 + chunk * 256, 128)


def bias_at(wide, head, pair, chunk):
    return jnp.concatenate(
        [wide[head, pl.ds(bias_offset(pair, side, chunk), 256), :] for side in range(2)], axis=1
    )


def forward_kernel(causal, *refs):
    if causal:
        q, kv, waves, o_low, o_full, lse, wide, values_t, score, total = refs
        def build(head, carry):
            for tile in range(USED):
                row = jnp.broadcast_to(waves[head, tile : tile + 1, :], (128, 256))
                turned = pltpu.roll(row, 129, 1, stride=1, stride_axis=0)
                wide[head, tile * 128 : tile * 128 + 128, :] = turned[:, :128]
            wide[head, USED * 128 :, :] = jnp.full(
                ((TILES - USED) * 128, 128), NEGATIVE, jnp.float32
            )
            return carry

        lax.fori_loop(0, 3, build, 0)
    else:
        q, kv, o_low, o_full, lse, values_t, score, total = refs

    for chunk in range(8):
        values_t[chunk] = kv[2 * chunk : 2 * chunk + 2, :, 128:384].reshape(256, 256).T
    for pair in range(2):
        chunks = 4 if causal and pair == 0 else 8
        rows = q[2 * pair : 2 * pair + 2].reshape(256, 256)
        total[...] = jnp.zeros_like(total)

        def one_head(head, carry):
            masked = head_lanes(rows, head)

            top = jnp.full((8, 256), NEGATIVE, jnp.float32)
            for chunk in range(chunks):
                keys = kv[2 * chunk : 2 * chunk + 2, :, 0:256].reshape(256, 256)
                block = dot_nt(keys, masked)
                if causal:
                    block = block + bias_at(wide, head, pair, chunk)
                score[chunk] = block
                top = jnp.maximum(top, jnp.max(block.reshape(32, 8, 256), axis=0))
            top = jnp.max(top, axis=0, keepdims=True)
            summed = jnp.zeros((8, 256), jnp.float32)
            held = jnp.zeros((256, 256), jnp.float32)
            for chunk in range(chunks):
                expo = jnp.exp(score[chunk] - top)
                summed = summed + jnp.sum(expo.reshape(32, 8, 256), axis=0)
                held = held + dot_nn(values_t[chunk], expo.astype(jnp.bfloat16))
            summed = jnp.sum(summed, axis=0, keepdims=True)
            total[...] += head_rows(held * (1.0 / summed), head + 1)
            lse[head, pair] = top + jnp.log(summed)
            return carry

        lax.fori_loop(0, 3, one_head, 0)
        final = total[...].T.reshape(2, 128, 256)
        o_full[2 * pair : 2 * pair + 2] = final
        o_low[2 * pair : 2 * pair + 2] = final.astype(jnp.bfloat16)


def attend(q, kv, waves, collective_id, greet, carry, hops):
    causal = waves is not None
    shapes = [
        ((4, 128, 256), jnp.bfloat16),
        ((4, 128, 256), jnp.float32),
        ((3, 2, 1, 256), jnp.float32),
    ]
    args = [q, kv]
    if causal:
        shapes.append(((3, TILES * 128, 128), jnp.float32))
        args.append(waves)
    return staged_call(
        functools.partial(forward_kernel, causal),
        "attend_self" if causal else "attend_cross",
        args,
        shapes,
        [
            pltpu.VMEM((8, 256, 256), jnp.bfloat16),
            pltpu.VMEM((8, 256, 256), jnp.float32),
            pltpu.VMEM((256, 256), jnp.float32),
        ],
        collective_id,
        greet,
        carry,
        hops,
    )


def backward_kernel(causal, *refs):
    if causal:
        (q, kv, grad, o_full, lse, wide, dq, dkv, waves,
         keys_t, dk, dv, dq_t, turned, along) = refs
        along[...] = jnp.zeros_like(along)
    else:
        q, kv, grad, o_full, lse, dq, dkv, keys_t, dk, dv, dq_t, turned = refs
    dk[...] = jnp.zeros_like(dk)
    dv[...] = jnp.zeros_like(dv)

    for chunk in range(8):
        keys_t[chunk] = kv[2 * chunk : 2 * chunk + 2, :, 0:256].reshape(256, 256).T
    for pair in range(2):
        chunks = 4 if causal and pair == 0 else 8
        both = slice(2 * pair, 2 * pair + 2)
        rows = q[both].reshape(256, 256)
        grads = grad[both].reshape(256, 256)
        turned[...] = (grads.astype(jnp.float32) * o_full[both].reshape(256, 256)).T
        dq_t[...] = jnp.zeros_like(dq_t)

        def one_head(head, carry):
            masked = head_lanes(rows, head)
            masked_grads = head_lanes(grads, head + 1)
            delta = jnp.sum(head_rows(turned[...], head + 1), axis=0, keepdims=True)
            row_lse = lse[head, pair]

            held = jnp.zeros((256, 256), jnp.float32)
            for chunk in range(chunks):
                block = kv[2 * chunk : 2 * chunk + 2].reshape(256, 384)
                scores = dot_nt(block[:, 0:256], masked)
                if causal:
                    scores = scores + bias_at(wide, head, pair, chunk)
                probs = jnp.exp(scores - row_lse)
                grad_probs = dot_nt(block[:, 128:384], masked_grads)
                grad_scores = probs * (grad_probs - delta)
                low = grad_scores.astype(jnp.bfloat16)
                spot = slice(chunk * 256, chunk * 256 + 256)
                dk[spot] += dot_nn(low, masked)
                dv[spot] += dot_nn(probs.astype(jnp.bfloat16), masked_grads)
                if causal:
                    for side in range(2):
                        where = pl.ds(bias_offset(pair, side, chunk), 256)
                        along[head, where, :] += grad_scores[:, 128 * side : 128 * side + 128]
                held = held + dot_nn(keys_t[chunk], low)
            dq_t[...] += head_rows(held, head)
            return carry

        lax.fori_loop(0, 3, one_head, 0)
        dq[both] = dq_t[...].T.reshape(2, 128, 256).astype(jnp.bfloat16)

    def pack(block, carry):
        spot = pl.ds(pl.multiple_of(block * 128, 128), 128)
        key_part, value_part = dk[spot], dv[spot]
        dkv[block, :, 0:128] = key_part[:, 0:128].astype(jnp.bfloat16)
        dkv[block, :, 128:256] = (key_part[:, 128:256] + value_part[:, 0:128]).astype(jnp.bfloat16)
        dkv[block, :, 256:384] = value_part[:, 128:256].astype(jnp.bfloat16)
        return carry

    lax.fori_loop(0, 16, pack, 0)
    if causal:
        waves[...] = jnp.zeros_like(waves)

        def fold(head, carry):
            for tile in range(USED):
                value = along[head, tile * 128 : tile * 128 + 128, :]
                value = jnp.concatenate([value, jnp.zeros_like(value)], axis=1)
                count = 64
                while count >= 1:
                    value = pltpu.roll(value[:count], count, 1) + value[count:]
                    count //= 2
                waves[head, tile : tile + 1, :] = value
            return carry

        lax.fori_loop(0, 3, fold, 0)


def attend_back(q, kv, grad, o_full, lse, wide):
    causal = wide is not None
    shapes = [((4, 128, 256), jnp.bfloat16), ((16, 128, 384), jnp.bfloat16)]
    args = [q, kv, grad, o_full, lse]
    scratch = [
        pltpu.VMEM((8, 256, 256), jnp.bfloat16),
        pltpu.VMEM((2048, 256), jnp.float32),
        pltpu.VMEM((2048, 256), jnp.float32),
        pltpu.VMEM((256, 256), jnp.float32),
        pltpu.VMEM((256, 256), jnp.float32),
    ]
    if causal:
        shapes.append(((3, TILES, 256), jnp.float32))
        args.append(wide)
        scratch.append(pltpu.VMEM((3, TILES * 128, 128), jnp.float32))
    return staged_call(
        functools.partial(backward_kernel, causal),
        "attend_back_self" if causal else "attend_back_cross",
        args,
        shapes,
        scratch,
    )


PRECISE = lax.Precision.HIGHEST


def body(
    layer_input,
    encoder_states,
    cotangent,
    bucket_ids,
    bias_table,
    gain_first,
    gain_second,
    gain_third,
    self_query,
    self_key,
    self_value,
    self_output,
    cross_query,
    cross_key,
    cross_value,
    cross_output,
    gate_weight,
    up_weight,
    down_weight,
):
    bucket_count, head_count = bias_table.shape
    width = layer_input.shape[-1]
    layer_input, encoder_states, cotangent = layer_input[0], encoder_states[0], cotangent[0]
    gain_first, gain_second, gain_third = (
        gain.reshape(1, width) for gain in (gain_first, gain_second, gain_third)
    )
    low, full = jnp.bfloat16, jnp.float32
    grouped, rows, wide_rows, line = (4, 128, 256), (128, 768), (128, 2048), (1, 768)
    first_head = 3 * ((lax.axis_index("ctx") // 2) % 4)
    padded = jnp.pad(bucket_ids, (TILES * 128 - bucket_ids.shape[0] + 128, 0), constant_values=-1)
    last = padded.shape[0]
    ids = jnp.stack([padded[last - 255 - 128 * k : last - 128 * k] for k in range(TILES)])
    ids = jnp.pad(ids, ((0, 0), (0, 1)), constant_values=-1)
    hot = (ids[:, :, None] == jnp.arange(bucket_count, dtype=jnp.int32)).astype(jnp.float32)
    own_table = lax.dynamic_slice_in_dim(bias_table, first_head, 3, 1)
    waves = jnp.einsum("kxb,bh->hkx", hot, own_table, precision=PRECISE)
    waves = jnp.where((ids >= 0)[None], waves, NEGATIVE)

    (
        (self_q, self_kv, cross_kv, normed_one, normed_one_peer, encoder_peer, cotangent_peer),
        weights,
        feed,
    ) = open_layer(
        layer_input,
        encoder_states,
        gain_first,
        cotangent,
        (
            self_query, self_key, self_value, cross_key, cross_value,
            self_output, cross_query, cross_output, gate_weight, up_weight, down_weight,
        ),
        2,
    )
    w_query, w_key, w_value, w_ckey, w_cvalue, w_out, w_cquery, w_cout = weights
    (self_low, self_full, self_lse, wide), feed = attend(
        self_q, self_kv, waves, 7, ("xa", "xb"), feed, ("side",) * 4
    )
    (
        (cross_q, attended, middle, normed_two, attended_peer, normed_two_peer), feed
    ) = shared_call(
        middle_kernel,
        "middle",
        (self_low, layer_input, gain_second, w_out, w_cquery),
        ((grouped, low), (rows, low), (rows, full), (rows, low)),
        row_scratch() + row_scratch(),
        3,
        feed,
        ("za", "zb", "core", "core"),
        (1, 3),
    )
    (cross_low, cross_full, cross_lse), feed = attend(
        cross_q, cross_kv, None, 8, ("core",), feed, ("core", "core", None, None)
    )
    w_gate, w_up, w_down = (whole(weight) for weight in feed)
    (
        cross_grads, layer_output, crossed, normed_three, grad_gate, grad_up, mixed,
        branch_after, grad_after, dgain_third,
        *feed_peers,
    ) = shared_call(
        feed_kernel,
        "feed_forward",
        (cross_low, middle, gain_third, w_cout, w_gate, w_up, w_down, cotangent),
        (
            (grouped, low), (rows, low), (rows, low), (rows, low), (wide_rows, low),
            (wide_rows, low), (wide_rows, low), (rows, low), (rows, full), (line, full),
        ),
        row_scratch() + row_scratch() + [pltpu.VMEM(wide_rows, full)],
        4,
        share=(2, 3, 7, 4, 5, 6),
    )
    cross_dq, cross_dkv = attend_back(cross_q, cross_kv, cross_grads, cross_full, cross_lse, None)
    (
        self_grads, grad_cquery, cross_total, branch_middle, grad_middle, dgain_second,
        grad_cquery_peer, branch_middle_peer,
    ) = shared_call(
        turn_kernel,
        "turn",
        (
            cross_dq, cross_dkv.reshape(8, 2, 128, 384), middle, gain_second, grad_after,
            w_cquery, w_out,
        ),
        (
            (grouped, low), (rows, low), ((4, 128, 384), low), (rows, low), (rows, full),
            (line, full),
        ),
        row_scratch() + row_scratch() + sum_scratch(),
        5,
        share=(1, 3),
    )
    self_dq, self_dkv, grad_waves = attend_back(
        self_q, self_kv, self_grads, self_full, self_lse, wide
    )
    (
        grad_input, grad_encoder, grad_queries, grad_keys, grad_values, grad_ckeys, grad_cvalues,
        dgain_first, *close_peers,
    ) = shared_call(
        close_kernel,
        "close",
        (
            self_dq, self_dkv.reshape(8, 2, 128, 384), layer_input, gain_first, grad_middle,
            w_query, w_key, w_value, cross_total, w_ckey, w_cvalue,
        ),
        ((rows, full), (rows, full)) + ((rows, low),) * 5 + ((line, full),),
        row_scratch()
        + [pltpu.VMEM((4, 128, 384), low)]
        + sum_scratch()
        + owner_scratch()
        + owner_scratch(),
        6,
        share=(2, 3, 4, 5, 6),
    )
    own_grads = jnp.einsum("kxb,hkx->bh", hot, grad_waves, precision=PRECISE)
    local_table = lax.dynamic_update_slice_in_dim(
        jnp.zeros_like(bias_table), own_grads, first_head, 1
    )
    small = jnp.concatenate(
        [dgain_first[0], dgain_second[0], dgain_third[0], local_table.reshape(-1)]
    )
    small = jnp.pad(small, (0, 24 * 128 - small.shape[0])).reshape(24, 128)
    crossed_peer, normed_three_peer, branch_after_peer, *feed_peers = feed_peers
    full_sums, sums = reduce_weights(
        (
            normed_one, attended, normed_two, encoder_states, crossed, normed_three,
            grad_queries, grad_keys, grad_values, branch_middle,
            grad_cquery, grad_ckeys, grad_cvalues, branch_after,
            grad_gate, grad_up, mixed, cotangent,
        ),
        (
            normed_one_peer, attended_peer, normed_two_peer, encoder_peer, crossed_peer,
            normed_three_peer,
            *close_peers[:3], branch_middle_peer,
            grad_cquery_peer, *close_peers[3:], branch_after_peer,
            *feed_peers, cotangent_peer,
        ),
        small,
        1,
    )
    *shards, layer_output, grad_input, grad_encoder = place_all(
        full_sums, (layer_output, grad_input, grad_encoder)
    )
    sums = sums.reshape(-1)
    return (
        layer_output[None],
        grad_input[None],
        grad_encoder[None],
        sums[3 * width : 3 * width + bucket_count * head_count].reshape(bucket_count, head_count),
        sums[:width],
        sums[width : 2 * width],
        sums[2 * width : 3 * width],
    ) + tuple(shards)


def solution(mesh):
    placed = (
        P("dp", "ctx", None),
        P("dp", "ctx", None),
        P("dp", "ctx", None),
        P(),
        P(),
        P(),
        P(),
        P(),
        P("dp", None),
        P("dp", None),
        P("dp", None),
        P("dp", None),
        P("dp", None),
        P("dp", None),
        P("dp", None),
        P("dp", None),
        P("dp", None),
        P("dp", None),
        P("dp", None),
    )
    return jax.shard_map(
        body,
        mesh=mesh,
        in_specs=placed,
        out_specs=(
            P("dp", "ctx", None),
            P("dp", "ctx", None),
            P("dp", "ctx", None),
            P(),
            P(),
            P(),
            P(),
            P("dp", None),
            P("dp", None),
            P("dp", None),
            P("dp", None),
            P("dp", None),
            P("dp", None),
            P("dp", None),
            P("dp", None),
            P("dp", None),
            P("dp", None),
            P("dp", None),
        ),
        check_vma=False,
    )
```

```python
import functools
import math
import jax
import jax.numpy as jnp
from jax import lax
from jax.experimental import pallas as pl
from jax.experimental.pallas import tpu as pltpu
from jax.sharding import PartitionSpec as P

MESH = pl.DeviceIdType.MESH
VMEM_BYTES = 62 * 2**20
ANY = pl.BlockSpec(memory_space=pl.ANY)
HBM = pl.BlockSpec(memory_space=pltpu.HBM)
VMEM = pl.BlockSpec(memory_space=pltpu.VMEM)


class Place:
    def __init__(self):
        c = lax.axis_index("ctx")
        d = lax.axis_index("dp")
        self.c, self.d = c, d
        self.x_hi = c // 8
        self.z = (c // 2) % 4
        self.core = c % 2
        self.y = d // 2
        self.x_lo = d % 2
        self.y_a = self.y + 1 - 2 * (self.y % 2)
        self.y_b = 3 - self.y
        self.y_ab = 3 - self.y_a
        self.z_a = self.z + 1 - 2 * (self.z % 2)
        self.z_b = 3 - self.z
        self.z_ab = 3 - self.z_a
        far_lo, far_hi = 1 - self.x_lo, 1 - self.x_hi
        self.x = self.x_lo * 2 + self.x_hi
        self.x_a = far_lo * 2 + self.x_hi
        self.x_b = far_lo * 2 + far_hi
        self.x_ab = self.x_lo * 2 + far_hi
        same = self.x_hi * 8 + self.z * 2 + self.core
        self.dev = {
            "core": (self.x_hi * 8 + self.z * 2 + 1 - self.core, d),
            "ya": (same, self.y_a * 2 + self.x_lo),
            "yb": (same, self.y_b * 2 + self.x_lo),
            "za": (self.x_hi * 8 + self.z_a * 2 + self.core, d),
            "zb": (self.x_hi * 8 + self.z_b * 2 + self.core, d),
            "xa": (same, self.y * 2 + far_lo),
            "xb": (far_hi * 8 + self.z * 2 + self.core, self.y * 2 + far_lo),
            "xab": (far_hi * 8 + self.z * 2 + self.core, d),
        }

    def greet(self, names):
        barrier = pltpu.get_barrier_semaphore()
        for name in names:
            pl.semaphore_signal(
                barrier, inc=1, device_id=self.dev[name], device_id_type=MESH
            )
        pl.semaphore_wait(barrier, len(names))

    def send(self, name, src, dst, send_sem, recv_sem):
        copy = pltpu.make_async_remote_copy(
            src_ref=src,
            dst_ref=dst,
            send_sem=send_sem,
            recv_sem=recv_sem,
            device_id=self.dev[name],
            device_id_type=MESH,
        )
        copy.start()
        return copy


EARLY_PLAN = (
    ((0, "pair", 0), (1, "pair", 0), (2, "pair", 0)),
    ((3, "pair", 0), (4, "pair", 0)),
)
LATE_PLAN = (((0, "zb", 0), (1, "za", 0)), ((2, "pair", 0),))
FEED_PLAN = (((0, "za", 0), (1, "zb", 0), (0, "za", 1), (1, "zb", 1), (2, "pair", 0)),)


class Chain:
    def __init__(self, me, source, target, kind, half, piece, pieces, sems):
        rows, cols = source.shape[-2:]
        width = cols // 2 // pieces
        self.me, self.source, self.target, self.kind = me, source, target, kind
        self.sems, self.slot, self.copies = sems, 0, []
        self.all_rows = pl.ds(0, rows)
        if kind == "pair":
            self.rows = pl.ds(half * (rows // 2), rows // 2)
            self.all_rows = self.rows
            flip = half == 1
        else:
            bit = me.z % 2 if kind == "za" else me.z // 2
            self.rows = pl.ds(pl.multiple_of(bit * (rows // 2), 16), rows // 2)
            flip = kind == "zb"
        self.cols = pl.ds(pl.multiple_of(me.core * (cols // 2) + piece * width, 128), width)
        self.other = pl.ds(pl.multiple_of((1 - me.core) * (cols // 2) + piece * width, 128), width)
        self.first, self.second = ("yb", "ya") if flip else ("ya", "yb")
        self.near = me.y_b if flip else me.y_a
        self.side = "xb" if flip else "xa"
        if kind != "pair" and pieces == 2:
            self.side = ("xb", "xa")[piece]
        self.stages = 4 if kind == "pair" else 5

    def go(self, name, src, dst):
        send_sem, recv_sem, index = self.sems
        copy = self.me.send(
            name, src, dst, send_sem.at[index, self.slot], recv_sem.at[index, self.slot]
        )
        self.slot += 1
        self.copies.append(copy)
        return copy

    def hop(self, name):
        me, out = self.me, self.target
        if name == "side":
            got = out.at[:, me.x_lo, self.rows, self.cols]
            return self.go(self.side, got, got)
        if name == "core":
            got = out.at[:, :, self.all_rows, self.cols]
            return self.go("core", got, got)
        got = out.at[:, :, self.rows, self.cols]
        return self.go(self.kind, got, got)

    def run(self, stage):
        me, out = self.me, self.target
        if stage == 0:
            mine = self.source.at[self.rows, self.cols]
            spot = out.at[me.y, me.x_lo, self.rows, self.cols]
            self.first_copy = self.go(self.first, mine, spot)
            self.second_copy = self.go(self.second, mine, spot)
            self.own_copy = self.go(
                "core",
                self.source.at[self.rows, self.other],
                out.at[me.y, me.x_lo, self.rows, self.other],
            )
        elif stage == 1:
            self.first_copy.wait_recv()
            got = out.at[self.near, me.x_lo, self.rows, self.cols]
            self.third_copy = self.go(self.second, got, got)
        elif stage == 2:
            self.second_copy.wait_recv()
            self.own_copy.wait_recv()
            self.third_copy.wait_recv()
            got = out.at[:, me.x_lo, self.rows, self.cols]
            self.last = self.go(self.side, got, got)
        elif stage == 3 and self.kind != "pair":
            self.last.wait_recv()
            got = out.at[:, :, self.rows, self.cols]
            self.last = self.go(self.kind, got, got)
        elif stage == self.stages - 1:
            self.last.wait_recv()
            got = out.at[:, :, self.all_rows, self.cols]
            self.last = self.go("core", got, got)
        elif stage == self.stages:
            self.last.wait_recv()


def make_groups(me, ins, outs, plan, send_sem, recv_sem):
    pieces = {}
    for group in plan:
        for array, kind, piece in group:
            pieces[array] = max(pieces.get(array, 0), piece + 1)
    groups = []
    index = 0
    for group in plan:
        chains = []
        for array, kind, piece in group:
            for half in range(2 if kind == "pair" else 1):
                chains.append(
                    Chain(
                        me, ins[array], outs[array], kind, half, piece, pieces[array],
                        (send_sem, recv_sem, index),
                    )
                )
                index += 1
        groups.append(chains)
    return groups


def run_stage(chains, stage):
    for chain in chains:
        chain.run(stage)


def chain_count(plan):
    return sum(2 if kind == "pair" else 1 for group in plan for _, kind, _ in group)


class Staged:
    def __init__(self, source, target, sem):
        self.copy = pltpu.make_async_copy(source, target, sem)
        self.copy.start()
        self.target, self.here = target, False

    def __call__(self):
        if not self.here:
            self.copy.wait()
            self.here = True
        return self.target

    def __getitem__(self, index):
        return self()[index]

    @property
    def at(self):
        return self().at


class Shared:
    def __init__(self, ref, peer, send_sem, recv_sem):
        self.ref, self.peer, self.sems = ref, peer, (send_sem, recv_sem)

    def __getitem__(self, index):
        return self.ref[index]

    def __setitem__(self, index, value):
        self.ref[index] = value
        if index is Ellipsis:
            self.tell()

    def tell(self):
        self.copy = Place().send("core", self.ref, self.peer, *self.sems)


class Deferred:
    def __init__(self, copies, source, target, sem):
        self.copies, self.source, self.target, self.here = copies, source, target, False
        rows = source.shape[2]
        self.loads = [
            pltpu.make_async_copy(
                source.at[y, x], target.at[pl.ds((2 * y + x) * rows, rows)], sem.at[2 * y + x]
            )
            for y in range(4)
            for x in range(2)
        ]

    def prepare(self):
        for copy in self.copies:
            copy.wait_recv()
        for load in self.loads:
            load.start()

    def __getitem__(self, index):
        if not self.here:
            for load in self.loads:
                load.wait()
            self.here = True
        return self.target[index]


def staged_kernel(kernel, n_in, n_out, n_carry, greet, hops, share, load_carry, pair_hops, *refs):
    refs = list(refs)

    def take(count):
        taken = refs[:count]
        del refs[:count]
        return taken

    ins, _, outs, peers, carried, targets = (
        take(n_in), take(n_carry), take(n_out), take(len(share)), take(n_carry), take(n_in)
    )
    (sem,) = take(1)
    staged = [Staged(ref, target, sem.at[i]) for i, (ref, target) in enumerate(zip(ins, targets))]
    moved = []
    if hops:
        send_sem, recv_sem = take(2)
    if share:
        share_send, share_recv = take(2)
        for slot, index in enumerate(share):
            outs[index] = Shared(
                outs[index], peers[slot], share_send.at[slot], share_recv.at[slot]
            )
    if greet is not None:
        me = Share()
        if greet == "all":
            me.greet_all(extra=("xa", "xb") if "side" in hops else ())
        else:
            me.greet(greet)
    if hops:
        (chains,) = make_groups(me, carried, carried, FEED_PLAN, send_sem, recv_sem)
        for chain, hop in zip(chains, hops):
            if hop is not None:
                moved.append(chain.hop(hop))
    if pair_hops:
        pair_send, pair_recv = take(2)
        for slot, (name, side) in enumerate(pair_hops):
            blocks = carried[3].at[me.x_hi if side == "near" else 1 - me.x_hi, :, me.core]
            moved.append(
                me.send(name, blocks, blocks, pair_send.at[slot], pair_recv.at[slot])
            )
    if load_carry:
        targets, load_sem = take(3), take(1)[0]
        last = [[moved[0]], [moved[1]], []]
        staged += [
            Deferred(last[i], carried[i], targets[i], load_sem.at[i]) for i in range(3)
        ]
    if greet != "all":
        staged = [ref() for ref in staged]
    kernel(*staged, *outs, *refs)
    if greet == "all":
        for ref in staged[:n_in]:
            ref()
    for copy in moved:
        if load_carry:
            copy.wait_send()
        else:
            copy.wait()
    for index in share:
        outs[index].copy.wait()


def staged_call(
    kernel, name, args, shapes, scratch, collective_id=None, greet=None, carry=(), hops=(), share=(),
    load_carry=False, pair_hops=(),
):
    carry = tuple(carry)
    shapes = tuple(shapes)
    n_out = len(shapes)
    shapes = shapes + tuple(shapes[index] for index in share)
    outs = pl.pallas_call(
        functools.partial(
            staged_kernel, kernel, len(args), n_out, len(carry), greet, hops, tuple(share),
            load_carry, pair_hops,
        ),
        out_shape=[jax.ShapeDtypeStruct(shape, kind) for shape, kind in shapes]
        + [jax.ShapeDtypeStruct(array.shape, array.dtype) for array in carry],
        in_specs=[HBM] * len(args) + [ANY] * len(carry),
        out_specs=[VMEM] * len(shapes) + [ANY] * len(carry),
        scratch_shapes=[pltpu.VMEM(arg.shape, arg.dtype) for arg in args]
        + [pltpu.SemaphoreType.DMA((len(args),))]
        + ([pltpu.SemaphoreType.DMA((6, 7))] * 2 if hops else [])
        + ([pltpu.SemaphoreType.DMA((len(share),))] * 2 if share else [])
        + ([pltpu.SemaphoreType.DMA((len(pair_hops),))] * 2 if pair_hops else [])
        + (
            [pltpu.VMEM((8 * array.shape[2], array.shape[3]), array.dtype) for array in carry]
            + [pltpu.SemaphoreType.DMA((3, 8))]
            if load_carry
            else []
        )
        + scratch,
        input_output_aliases={len(args) + i: len(shapes) + i for i in range(len(carry))},
        compiler_params=pltpu.CompilerParams(
            collective_id=collective_id,
            has_side_effects=greet is not None,
            vmem_limit_bytes=VMEM_BYTES,
        ),
        name=name,
    )(*args, *carry)
    return (outs[: len(shapes)], outs[len(shapes) :]) if carry else outs

AXES = ("y", "x", "z")


ACT_OF = (0, 0, 0, 1, 2, 3, 3, 4)


class Outer:
    def __init__(self, me, ins, acc, acts, grads, feeds, cots, turned, mixed_t, sem):
        self.me, self.acc = me, acc
        self.acts, self.grads, self.feeds, self.cots = acts, grads, feeds, cots
        self.turned, self.mixed_t = turned, mixed_t
        self.copies = []
        half = pl.ds(pl.multiple_of(me.core * 384, 128), 384)
        for side in range(2):
            begin = pl.ds(128 * side, 128)
            own = ins[18 * side : 18 * side + 18]
            for index in range(6):
                self.fetch(own[index], acts.at[index, begin], sem)
            for index in range(8):
                self.fetch(own[6 + index].at[:, half], grads.at[index, begin], sem)
            for index in range(3):
                self.fetch(own[14 + index], feeds.at[index, begin], sem)
            self.fetch(own[17], cots.at[begin], sem)

    def fetch(self, src, dst, sem):
        copy = pltpu.make_async_copy(src, dst, sem.at[len(self.copies)])
        copy.start()
        self.copies.append(copy)

    def ready(self):
        for copy in self.copies:
            copy.wait()
        for index in range(6):
            self.turned[index] = self.acts[index].T.reshape(8, 6, 16, 256)
        self.mixed_t[...] = self.feeds[2].T.reshape(8, 8, 2, 16, 256)

    def put(self, part, block, cols, value):
        width = value.shape[1]
        value = value.astype(jnp.bfloat16).reshape(4, 2, 16, width)
        for x_lo in range(2):
            self.acc[part, :, 2 * x_lo + block // 4, block % 4, :, cols] = value[:, x_lo]

    def compute(self, part):
        def dot(left, right):
            return jnp.dot(left, right, preferred_element_type=jnp.float32)

        for index in range(8):
            left = self.turned[ACT_OF[index], :, part].reshape(128, 256)
            self.put(part, index, slice(0, 384), dot(left, self.grads[index]))
        left = self.turned[5, :, part].reshape(128, 256)
        for block in range(8):
            cols = pl.ds(pl.multiple_of((2 * block + self.me.core) * 128, 128), 128)
            right = jnp.concatenate([self.feeds[0, :, cols], self.feeds[1, :, cols]], axis=1)
            self.put(part, block, slice(384, 640), dot(left, right))
        left = self.mixed_t[:, :, self.me.core].reshape(1024, 256)
        down = dot(left, self.cots[:, 128 * part : 128 * part + 128])
        down = down.astype(jnp.bfloat16).reshape(4, 2, 2, 4, 16, 128)
        for x_lo in range(2):
            for x_hi in range(2):
                self.acc[part, :, 2 * x_lo + x_hi, :, :, 640:768] = down[:, x_lo, x_hi]


def reduce_kernel(*refs):
    ins, small = refs[:36], refs[36]
    full, small_out = refs[37:39]
    (acc, r1, r2, r3, r4, r5, r6, sm_in,
     send_sem, recv_sem, sm_send, sm_recv, ag_send, ag_recv, *outer) = refs[39:]
    recvs = (r1, r2, r3, r4, r5, r6)
    me = Place()
    outer = Outer(me, ins, acc, *outer)
    me.greet(("core", "ya", "yb", "xa", "xb", "za", "zb", "xab"))
    spots = {
        "y": (me.y, me.y_a, me.y_b, me.y_ab),
        "x": (me.x, me.x_a, me.x_b, me.x_ab),
        "z": (me.z, me.z_a, me.z_b, me.z_ab),
    }
    parts = range(6)
    started = []

    def go(name, src, dst, send, recv):
        copy = me.send(name, src, dst, send, recv)
        started.append(copy)
        return copy

    small_out[...] = small[...]
    small_steps = ("core", "ya", "yb", "xa", "xb", "za", "zb")
    small_copies = []

    def small_start(step):
        small_copies.append(
            me.send(small_steps[step], small_out, sm_in.at[step], sm_send.at[step], sm_recv.at[step])
        )

    def small_end(step):
        small_copies[step].wait()
        small_out[...] = small_out[...] + sm_in[step]

    small_start(0)

    def order(part):
        first = (part // 2) % 3
        return [AXES[(first + k) % 3] for k in range(3)]

    def region(part, picks):
        return (part,) + tuple(picks.get(axis, slice(None)) for axis in AXES)

    def at(ref, index):
        return ref.at[index]

    def add(index, source, source_index):
        acc[index] = acc[index] + source[source_index]

    def dims(part):
        return ("a", "b") if part % 2 == 0 else ("b", "a")

    outer.ready()
    pending = {}
    for part in parts:
        axis = order(part)[0]
        me_at, a_at, b_at, ab_at = spots[axis]
        first, second = dims(part)
        sent = (a_at, ab_at) if first == "a" else (b_at, ab_at)
        outer.compute(part)
        pending[part] = []
        for slot, spot in enumerate(sent):
            pending[part].append(
                go(
                    axis + first,
                    at(acc, region(part, {axis: spot})),
                    r1.at[part, slot],
                    send_sem.at[part, 1 + slot],
                    recv_sem.at[part, 1 + slot],
                )
            )
    small_end(0)
    small_start(1)
    sem_at = {part: 3 for part in parts}

    def next_sem(part):
        sem_at[part] += 1
        return send_sem.at[part, sem_at[part] - 1], recv_sem.at[part, sem_at[part] - 1]

    for level in range(3):
        one, two = recvs[2 * level], recvs[2 * level + 1]
        for part in parts:
            axes = order(part)
            axis = axes[level]
            first, second = dims(part)
            me_at, a_at, b_at, ab_at = spots[axis]
            kept = b_at if first == "a" else a_at
            fixed = {name: spots[name][0] for name in axes[:level]}
            for copy in pending[part]:
                copy.wait_recv()
            add(region(part, {**fixed, axis: kept}), one, (part, 1))
            send, recv = next_sem(part)
            pending[part] = [
                go(axis + second, at(acc, region(part, {**fixed, axis: kept})), two.at[part], send, recv)
            ]
        for part in parts:
            axes = order(part)
            fixed = {name: spots[name][0] for name in axes[: level + 1]}
            add(region(part, fixed), one, (part, 0))
        small_end(2 * level + 1)
        small_start(2 * level + 2)
        for part in parts:
            axes = order(part)
            fixed = {name: spots[name][0] for name in axes[: level + 1]}
            for copy in pending[part]:
                copy.wait_recv()
            add(region(part, fixed), two, (part,))
            if level == 2:
                continue
            axis = axes[level + 1]
            first, second = dims(part)
            me_at, a_at, b_at, ab_at = spots[axis]
            sent = (a_at, ab_at) if first == "a" else (b_at, ab_at)
            pending[part] = []
            for slot, spot in enumerate(sent):
                send, recv = next_sem(part)
                pending[part].append(
                    go(
                        axis + first,
                        at(acc, region(part, {**fixed, axis: spot})),
                        recvs[2 * level + 2].at[part, slot],
                        send,
                        recv,
                    )
                )
        small_end(2 * level + 2)
        if level < 2:
            small_start(2 * level + 3)

    here = me.x_hi * 4 + me.z
    there = (1 - me.x_hi) * 4 + me.z
    for part in parts:
        full[here, me.core, part] = acc[part, me.y, me.x, me.z]
    used = [0]

    def pass_on(name, group, half):
        index = used[0]
        used[0] += 1
        src = full.at[group, me.core, pl.ds(3 * half, 3)]
        return go(name, src, src, ag_send.at[index], ag_recv.at[index])

    early = [pass_on("xab", here, half) for half in range(2)]
    near = [pass_on("za", here, 0), pass_on("zb", here, 1)]
    far = []
    for half in range(2):
        early[half].wait_recv()
        far.append(pass_on(("za", "zb")[half], there, half))
    base, base_far = me.x_hi * 4, (1 - me.x_hi) * 4
    ends = [pass_on("zb", here, 0), pass_on("za", here, 1)]
    ends += [pass_on("zb", there, 0), pass_on("za", there, 1)]
    for half in range(2):
        got = (me.z_a, me.z_b)[half]
        near[half].wait_recv()
        ends.append(pass_on(("zb", "za")[half], base + got, half))
    for half in range(2):
        got = (me.z_a, me.z_b)[half]
        far[half].wait_recv()
        ends.append(pass_on(("zb", "za")[half], base_far + got, half))
    for copy in ends:
        copy.wait_recv()
    last = go("core", full.at[:, me.core], full.at[:, me.core], ag_send.at[used[0]], ag_recv.at[used[0]])

    last.wait_recv()
    for copy in started:
        copy.wait_send()


def reduce_weights(own, peer, small, collective_id):
    bf = jnp.bfloat16
    return pl.pallas_call(
        reduce_kernel,
        out_shape=[
            jax.ShapeDtypeStruct((8, 2, 6, 16, 768), bf),
            jax.ShapeDtypeStruct(small.shape, small.dtype),
        ],
        in_specs=[HBM] * 36 + [VMEM],
        out_specs=[VMEM] * 2,
        scratch_shapes=[
            pltpu.VMEM((6, 4, 4, 4, 16, 768), bf),
            pltpu.VMEM((6, 2, 4, 4, 16, 768), bf),
            pltpu.VMEM((6, 4, 4, 16, 768), bf),
            pltpu.VMEM((6, 2, 4, 16, 768), bf),
            pltpu.VMEM((6, 4, 16, 768), bf),
            pltpu.VMEM((6, 2, 16, 768), bf),
            pltpu.VMEM((6, 16, 768), bf),
            pltpu.VMEM((7,) + small.shape, small.dtype),
            pltpu.SemaphoreType.DMA((6, 10)),
            pltpu.SemaphoreType.DMA((6, 10)),
            pltpu.SemaphoreType.DMA((7,)),
            pltpu.SemaphoreType.DMA((7,)),
            pltpu.SemaphoreType.DMA((16,)),
            pltpu.SemaphoreType.DMA((16,)),
            pltpu.VMEM((6, 256, 768), bf),
            pltpu.VMEM((8, 256, 384), bf),
            pltpu.VMEM((3, 256, 2048), bf),
            pltpu.VMEM((256, 768), bf),
            pltpu.VMEM((6, 8, 6, 16, 256), bf),
            pltpu.VMEM((8, 8, 2, 16, 256), bf),
            pltpu.SemaphoreType.DMA((36,)),
        ],
        compiler_params=pltpu.CompilerParams(
            collective_id=collective_id, has_side_effects=True, vmem_limit_bytes=VMEM_BYTES
        ),
        name="reduce_weights",
    )(*own, *peer, small)


def place_kernel(full, *refs):
    passed, outs = refs[:3], refs[3:]
    wide = jnp.float32
    for o in range(16):
        group, core = o // 2, o % 2
        for part in range(6):
            rows = slice(16 * part, 16 * part + 16)
            block = full[group, core, part]
            outs[group][rows, core * 384 : core * 384 + 384] = block[:, 0:384].astype(wide)
            outs[8][rows, 128 * o : 128 * o + 128] = block[:, 384:512].astype(wide)
            outs[9][rows, 128 * o : 128 * o + 128] = block[:, 512:640].astype(wide)
            outs[10][16 * o : 16 * o + 16, 128 * part : 128 * part + 128] = block[
                :, 640:768
            ].astype(wide)
    for source, target in zip(passed, outs[11:]):
        target[...] = source[...]


def place_all(full, passed):
    wide = jnp.float32
    shapes = [((96, 768), wide)] * 8 + [((96, 2048), wide)] * 2 + [((256, 768), wide)]
    shapes += [(array.shape, array.dtype) for array in passed]
    return staged_call(place_kernel, "place", (full,) + tuple(passed), shapes, [])

NEGATIVE = -1e30
EPSILON = 1e-06
TILES = 23
USED = 16


class Share(Place):
    def __init__(self):
        super().__init__()
        self.dev["zab"] = (self.x_hi * 8 + self.z_ab * 2 + self.core, self.d)
        self.mine = self.x_hi * 2 + self.core
        self.slot = self.c // 4
        rest = self.c % 4
        self.owner = rest + (self.slot % 2) * (3 - 2 * rest)
        self.at_home = self.owner == self.mine

    def block(self, slot):
        return 4 * slot + (self.mine if slot % 2 == 0 else 3 - self.mine)

    def worker(self, group):
        return (self.owner // 2) * 8 + group * 2 + self.owner % 2

    def greet_all(self, extra=()):
        barrier = pltpu.get_barrier_semaphore()
        for name in extra:
            pl.semaphore_signal(
                barrier, inc=1, device_id=self.dev[name], device_id_type=MESH
            )
        for step in range(1, 16):
            pl.semaphore_signal(
                barrier, inc=1, device_id=((self.c + step) % 16, self.d), device_id_type=MESH
            )
        pl.semaphore_wait(barrier, 15 + len(extra))

    def copy_to(self, ctx, src, dst, send_sem, recv_sem):
        return pltpu.make_async_remote_copy(
            src_ref=src,
            dst_ref=dst,
            send_sem=send_sem,
            recv_sem=recv_sem,
            device_id=(ctx, self.d),
            device_id_type=MESH,
        )


class Rows:
    def __init__(self, me, src, dst, send_sem, recv_sem, back):
        self.me, self.src, self.dst = me, src, dst
        self.send_sem, self.recv_sem, self.back = send_sem, recv_sem, back

    def to_worker(self, group, ours):
        me = self.me
        away = jnp.logical_not(jnp.logical_and(me.at_home, me.z == group))
        if self.back:
            copy = me.copy_to(
                me.worker(group), self.src.at[0], self.dst.at[group],
                self.send_sem.at[0], self.recv_sem.at[group],
            )
        else:
            copy = me.copy_to(
                me.worker(group), self.src.at[group], self.dst.at[me.slot],
                self.send_sem.at[group], self.recv_sem.at[me.slot],
            )
        return away, copy

    def to_home(self, slot):
        me = self.me
        away = me.block(slot) != me.c
        if self.back:
            copy = me.copy_to(
                me.block(slot), self.src.at[slot], self.dst.at[me.z],
                self.send_sem.at[slot], self.recv_sem.at[me.z],
            )
        else:
            copy = me.copy_to(
                me.block(slot), self.src.at[0], self.dst.at[slot],
                self.send_sem.at[0], self.recv_sem.at[slot],
            )
        return away, copy

    def each(self, sending, action):
        for index in range(4):
            if sending != self.back:
                away, copy = self.to_worker(index, sending)
            else:
                away, copy = self.to_home(index)

            @pl.when(away)
            def _():
                action(copy)

    def start(self):
        me = self.me
        self.each(True, lambda copy: copy.start())

        @pl.when(me.at_home)
        def _():
            if self.back:
                self.dst[me.z] = self.src[me.slot]
            else:
                self.dst[me.slot] = self.src[me.z]

    def arrive(self):
        self.each(False, lambda copy: copy.wait_recv())

    def end(self):
        self.each(True, lambda copy: copy.wait_send())


class Pairs:
    def __init__(self, me, src, out, send_sem, recv_sem):
        self.me, self.src, self.out = me, src, out
        self.send_sem, self.recv_sem, self.done = send_sem, recv_sem, []
        self.groups = (me.z_a, me.z_b, me.z_ab)

    def go(self, name, src, dst, slot):
        copy = self.me.send(name, src, dst, self.send_sem.at[slot], self.recv_sem.at[slot])
        self.done.append(copy)
        return copy

    def start(self):
        me = self.me
        self.out[me.c] = self.src[me.z]
        self.first = [
            self.go(name, self.src.at[group], self.out.at[me.c], slot)
            for slot, (name, group) in enumerate(zip(("za", "zb", "zab"), self.groups))
        ]
        self.over_x, self.over_core = [], []
        self.pass_on(0)

    def pass_on(self, step):
        me = self.me
        block = me.x_hi * 8 + ((me.z,) + self.groups)[step] * 2 + me.core
        spot = self.out.at[block]
        self.over_x.append(self.go("xab", spot, spot, 3 + step))
        self.over_core.append(self.go("core", spot, spot, 7 + step))

    def second(self):
        for step in range(1, 4):
            self.first[step - 1].wait_recv()
            self.pass_on(step)

    def third(self):
        me = self.me
        for step, group in enumerate((me.z,) + self.groups):
            self.over_x[step].wait_recv()
            spot = self.out.at[(1 - me.x_hi) * 8 + group * 2 + me.core]
            self.over_core.append(self.go("core", spot, spot, 11 + step))

    def arrive(self):
        for copy in self.over_core:
            copy.wait_recv()

    def end(self):
        for copy in self.done:
            copy.wait_send()


class Sums:
    def __init__(self, me, src, total, send_sem, recv_sem, got_core, part, got_x):
        self.me, self.src, self.total = me, src, total
        self.send_sem, self.recv_sem, self.done = send_sem, recv_sem, []
        self.got_core, self.part, self.got_x = got_core, part, got_x
        self.order = (me.z_ab, me.z_a, me.z_b, me.z)

    def go(self, name, src, dst, slot):
        copy = self.me.send(name, src, dst, self.send_sem.at[slot], self.recv_sem.at[slot])
        self.done.append(copy)
        return copy

    def start(self):
        me = self.me
        self.near, self.far = me.x_hi * 4, (1 - me.x_hi) * 4
        self.core_copies = [
            self.go(
                "core",
                self.src.at[side + group, 1 - me.core],
                self.got_core.at[side + group],
                4 * index + step,
            )
            for index, side in enumerate((self.far, self.near))
            for step, group in enumerate(self.order)
        ]

    def join(self):
        for index, side in enumerate((self.far, self.near)):
            for step, group in enumerate(self.order):
                self.core_copies[4 * index + step].wait_recv()
                block = side + group
                self.total[block] = self.src[block, self.me.core] + self.got_core[block]

    def over(self):
        me = self.me
        self.over_x = []
        for step, group in enumerate(self.order):
            self.core_copies[step].wait_recv()
            block = self.far + group
            self.part[block] = self.src[block, me.core] + self.got_core[block]
            self.over_x.append(self.go("xab", self.part.at[block], self.got_x.at[group], 8 + step))
        for step, group in enumerate(self.order):
            self.core_copies[4 + step].wait_recv()
            block = self.near + group
            self.part[block] = self.src[block, me.core] + self.got_core[block]

    def finish(self, then=None):
        for step, group in enumerate(self.order):
            self.over_x[step].wait_recv()
            self.total[group] = self.part[self.near + group] + self.got_x[group]
            if then is not None and step < 3:
                then.send(step)

    def end(self):
        for copy in self.done:
            copy.wait_send()


class Owners:
    def __init__(self, me, total, out, send_sem, recv_sem):
        self.me, self.total, self.out = me, total, out
        self.send_sem, self.recv_sem, self.copies = send_sem, recv_sem, []

    def send(self, step):
        me = self.me
        group, name = ((me.z_ab, "zab"), (me.z_a, "za"), (me.z_b, "zb"))[step]
        self.copies.append(
            me.send(
                name, self.total.at[group], self.out.at[me.z],
                self.send_sem.at[step], self.recv_sem.at[step],
            )
        )

    def arrive(self):
        self.out[self.me.z] = self.total[self.me.z]
        for copy in self.copies:
            copy.wait_recv()

    def end(self):
        for copy in self.copies:
            copy.wait_send()


def lane_mask(value, begin, end):
    lane = lax.broadcasted_iota(jnp.int32, value.shape, 1)
    return jnp.where(jnp.logical_and(lane >= begin, lane < end), value, jnp.zeros_like(value))


def cut_heads(value, after):
    groups = []
    for half in range(2):
        left = value[:, 384 * half : 384 * half + 256]
        right = value[:, 384 * half + 128 : 384 * half + 384]
        if after:
            groups += [lane_mask(left, 0, 192), lane_mask(pltpu.roll(right, 192, 1), 0, 192)]
        else:
            groups += [lane_mask(pltpu.roll(left, 64, 1), 64, 256), lane_mask(right, 64, 256)]
    return groups


def join_heads(groups, after):
    pieces = []
    for half in range(2):
        left, right = groups[2 * half], groups[2 * half + 1]
        if after:
            right = pltpu.roll(right, 64, 1)
        else:
            left = pltpu.roll(left, 192, 1)
        pieces += [left[:, :128], left[:, 128:] + right[:, :128], right[:, 128:]]
    return jnp.concatenate(pieces, axis=1)


def put_rows(ref, value, after):
    for group, part in enumerate(cut_heads(value, after)):
        ref[group] = part.astype(jnp.bfloat16)


def get_rows(ref, after):
    return join_heads([ref[group].astype(jnp.float32) for group in range(4)], after)


def put_pairs(ref, keys, values):
    for group, (left, right) in enumerate(zip(cut_heads(keys, True), cut_heads(values, False))):
        ref[group, :, 0:128] = left[:, :128].astype(jnp.bfloat16)
        ref[group, :, 128:256] = (left[:, 128:] + right[:, :128]).astype(jnp.bfloat16)
        ref[group, :, 256:384] = right[:, 128:].astype(jnp.bfloat16)


def get_pairs(ref):
    keys = [lane_mask(ref[group, :, 0:256].astype(jnp.float32), 0, 192) for group in range(4)]
    values = [lane_mask(ref[group, :, 128:384].astype(jnp.float32), 64, 256) for group in range(4)]
    return join_heads(keys, True), join_heads(values, False)


def scale_of(value):
    return lax.rsqrt(jnp.mean(value * value, axis=-1, keepdims=True) + EPSILON)


def norm_back(value, gain, grad):
    scale = scale_of(value)
    weighted = grad * gain
    middle = jnp.mean(value * weighted, axis=-1, keepdims=True)
    dgain = jnp.sum(grad * (value * scale), axis=0, keepdims=True)
    return scale * weighted - value * (scale * scale * scale) * middle, dgain


def open_kernel(
    layer_input, encoder, gain, cotangent, *refs
):
    shards = refs[:11]
    q_out, kv_out, ckv_out, normed_out, normed_peer, encoder_peer, cotangent_peer = refs[11:18]
    outs = refs[18:29]
    (q_mine, kv_mine, ckv_mine, q_send, q_recv, kv_send, kv_recv, ckv_send, ckv_recv,
     early_send, early_recv, late_send, late_recv, feed_send, feed_recv, held, held_sem,
     share_send, share_recv) = refs[29:]
    me = Share()
    me.greet_all(extra=("ya", "yb", "xa", "xb"))
    early = make_groups(me, shards[:5], outs[:5], EARLY_PLAN, early_send, early_recv)
    late = make_groups(me, shards[5:8], outs[5:8], LATE_PLAN, late_send, late_recv)
    feed = make_groups(me, shards[8:], outs[8:], FEED_PLAN, feed_send, feed_recv)
    run_stage(early[0], 0)
    run_stage(early[1], 0)
    run_stage(late[0], 0)
    run_stage(late[1], 0)
    run_stage(early[0], 1)
    run_stage(early[1], 1)
    run_stage(feed[0], 0)
    run_stage(early[0], 2)
    run_stage(early[1], 2)
    residual = layer_input[...].astype(jnp.float32)
    normed = (residual * scale_of(residual) * gain[...]).astype(jnp.bfloat16)
    normed_out[...] = normed
    shared = [
        me.send("core", src, dst, share_send.at[slot], share_recv.at[slot])
        for slot, (src, dst) in enumerate(
            ((normed_out, normed_peer), (encoder, encoder_peer), (cotangent, cotangent_peer))
        )
    ]
    run_stage(late[0], 1)
    run_stage(late[1], 1)
    run_stage(feed[0], 1)
    run_stage(early[0], 3)
    run_stage(early[1], 3)
    run_stage(late[0], 2)
    run_stage(late[1], 2)
    sooner = [feed[0][index] for index in (0, 1, 4)]
    later = [feed[0][index] for index in (2, 3, 5)]
    run_stage(sooner, 2)
    run_stage(early[0], 4)

    def fetch(index):
        fetched = []
        for y in range(4):
            for x in range(2):
                begin = 96 * (2 * y + x)
                fetched.append(
                    pltpu.make_async_copy(
                        outs[index].at[y, x],
                        held.at[index, pl.ds(begin, 96)],
                        held_sem.at[index, 2 * y + x],
                    )
                )
                fetched[-1].start()
        return fetched

    def wait_all(copies):
        for copy in copies:
            copy.wait()

    fetched = [fetch(index) for index in range(3)]
    run_stage(early[1], 4)
    fetched += [fetch(index) for index in range(3, 5)]
    wait_all(fetched[1])
    wait_all(fetched[2])
    put_pairs(kv_mine, dot_nn(normed, held[1]), dot_nn(normed, held[2]))
    self_kv = Pairs(me, kv_mine, kv_out, kv_send, kv_recv)
    self_kv.start()
    wait_all(fetched[0])
    put_rows(q_mine, dot_nn(normed, held[0]), True)
    rows = Rows(me, q_mine, q_out, q_send, q_recv, False)
    rows.start()
    wait_all(fetched[3])
    wait_all(fetched[4])
    put_pairs(ckv_mine, dot_nn(encoder[...], held[3]), dot_nn(encoder[...], held[4]))
    spot = ckv_out.at[me.x_hi, me.z, me.core]
    own_kv = pltpu.make_async_copy(ckv_mine.at[me.z], spot, ckv_send.at[3])
    own_kv.start()
    cross_kv = [
        me.send(name, ckv_mine.at[group], spot, ckv_send.at[slot], ckv_recv.at[slot])
        for slot, (name, group) in enumerate(
            (("za", me.z_a), ("zb", me.z_b), ("zab", me.z_ab))
        )
    ]
    run_stage(late[0], 3)
    self_kv.second()
    run_stage(late[1], 3)
    run_stage(late[0], 4)
    self_kv.third()
    run_stage(late[1], 4)
    run_stage(late[0], 5)
    rows.arrive()
    self_kv.arrive()
    own_kv.wait()
    for copy in cross_kv:
        copy.wait_recv()
    for chain in sooner:
        chain.last.wait_recv()
    for chain in later:
        chain.second_copy.wait_recv()
        chain.third_copy.wait_recv()
        chain.own_copy.wait_recv()
    for chains in early + late + feed:
        for chain in chains:
            wait_sent(chain.copies)
    rows.end()
    self_kv.end()
    wait_sent(cross_kv)
    for copy in shared:
        copy.wait()


def wait_sent(copies):
    for copy in copies:
        copy.wait_send()


def open_layer(layer_input, encoder, gain, cotangent, shards, collective_id):
    bf = jnp.bfloat16
    early, late = chain_count(EARLY_PLAN), chain_count(LATE_PLAN)
    outs = pl.pallas_call(
        open_kernel,
        out_shape=[
            jax.ShapeDtypeStruct((4, 128, 256), bf),
            jax.ShapeDtypeStruct((16, 128, 384), bf),
            jax.ShapeDtypeStruct((2, 4, 2, 128, 384), bf),
        ]
        + [jax.ShapeDtypeStruct((128, 768), bf)] * 4
        + [jax.ShapeDtypeStruct((4, 2) + shard.shape, bf) for shard in shards],
        in_specs=[VMEM] * 3 + [ANY] * 12,
        out_specs=[VMEM] * 2 + [ANY] + [VMEM] * 3 + [ANY] * 12,
        scratch_shapes=[
            pltpu.VMEM((4, 128, 256), bf),
            pltpu.VMEM((4, 128, 384), bf),
            pltpu.VMEM((4, 128, 384), bf),
            pltpu.SemaphoreType.DMA((4,)),
            pltpu.SemaphoreType.DMA((4,)),
            pltpu.SemaphoreType.DMA((15,)),
            pltpu.SemaphoreType.DMA((15,)),
            pltpu.SemaphoreType.DMA((15,)),
            pltpu.SemaphoreType.DMA((15,)),
            pltpu.SemaphoreType.DMA((early, 7)),
            pltpu.SemaphoreType.DMA((early, 7)),
            pltpu.SemaphoreType.DMA((late, 7)),
            pltpu.SemaphoreType.DMA((late, 7)),
            pltpu.SemaphoreType.DMA((6, 7)),
            pltpu.SemaphoreType.DMA((6, 7)),
            pltpu.VMEM((5, 768, 768), bf),
            pltpu.SemaphoreType.DMA((5, 8)),
            pltpu.SemaphoreType.DMA((3,)),
            pltpu.SemaphoreType.DMA((3,)),
        ],
        compiler_params=pltpu.CompilerParams(
            collective_id=collective_id, has_side_effects=True, vmem_limit_bytes=VMEM_BYTES
        ),
        name="open_layer",
    )(layer_input, encoder, gain, cotangent, *shards)
    return outs[:7], [whole(out) for out in outs[7:15]], outs[15:]


def whole(gathered):
    return gathered.reshape(8 * gathered.shape[2], gathered.shape[3])


def row_scratch():
    return [
        pltpu.VMEM((4, 128, 256), jnp.bfloat16),
        pltpu.SemaphoreType.DMA((4,)),
        pltpu.SemaphoreType.DMA((4,)),
    ]


def sum_scratch():
    bf = jnp.bfloat16
    return [
        pltpu.SemaphoreType.DMA((12,)),
        pltpu.SemaphoreType.DMA((12,)),
        pltpu.VMEM((8, 128, 384), bf),
        pltpu.VMEM((8, 128, 384), bf),
        pltpu.VMEM((4, 128, 384), bf),
    ]


def owner_scratch():
    return [
        pltpu.VMEM((4, 128, 384), jnp.bfloat16),
        pltpu.SemaphoreType.DMA((3,)),
        pltpu.SemaphoreType.DMA((3,)),
    ]


def shared_call(
    kernel, name, args, shapes, scratch, collective_id, carry=(), hops=(), share=(),
    load_carry=False, pair_hops=(),
):
    return staged_call(
        kernel, name, args, shapes, scratch, collective_id, "all", carry, hops, share, load_carry,
        pair_hops,
    )


def middle_kernel(
    o_in, layer_input, gain, w_out, w_query,
    q_out, attended_out, middle_out, normed_out,
    o_mine, o_send, o_recv, q_mine, q_send, q_recv,
):
    me = Share()
    back = Rows(me, o_in, o_mine, o_send, o_recv, True)
    back.start()
    back.arrive()
    attended = get_rows(o_mine, False).astype(jnp.bfloat16)
    middle = layer_input[...].astype(jnp.float32) + dot_nn(attended, w_out[...])
    normed = (middle * scale_of(middle) * gain[...]).astype(jnp.bfloat16)
    put_rows(q_mine, dot_nn(normed, w_query[...]), True)
    rows = Rows(me, q_mine, q_out, q_send, q_recv, False)
    rows.start()
    attended_out[...] = attended
    middle_out[...] = middle
    normed_out[...] = normed
    rows.arrive()
    back.end()
    rows.end()


def feed_kernel(
    o_in, middle, gain, w_out, cotangent, w_gate, w_up, w_down,
    g_out, final_out, crossed_out, normed_out, grad_gate, grad_up, mixed, branch_out, after_out,
    dgain_out,
    o_mine, o_send, o_recv, g_mine, g_send, g_recv, grad_mixed,
):
    low = jnp.bfloat16
    me = Share()
    back = Rows(me, o_in, o_mine, o_send, o_recv, True)
    back.start()
    w_down.prepare()
    w_gate.prepare()
    w_up.prepare()
    grad_mixed[...] = dot_nt(cotangent[...], w_down[...])
    back.arrive()
    crossed = get_rows(o_mine, False).astype(low)
    crossed_out[...] = crossed
    after = middle[...] + dot_nn(crossed, w_out[...])
    normed = (after * scale_of(after) * gain[...]).astype(low)
    normed_out[...] = normed
    root = math.sqrt(2.0 / math.pi)
    for chunk in range(8):
        cols = slice(256 * chunk, 256 * chunk + 256)
        gate = dot_nn(normed, w_gate[:, cols])
        up = dot_nn(normed, w_up[:, cols])
        square = gate * gate
        curve = jnp.tanh(root * gate * (1.0 + 0.044715 * square))
        half = 0.5 * (1.0 + curve)
        gelu = gate * half
        slope = half + 0.5 * gate * (1.0 - curve * curve) * (
            root * (1.0 + 3 * 0.044715 * square)
        )
        incoming = grad_mixed[:, cols]
        mixed[:, cols] = (gelu * up).astype(low)
        grad_gate[:, cols] = (incoming * up * slope).astype(low)
        grad_up[:, cols] = (incoming * gelu).astype(low)
    for ref in (mixed, grad_gate, grad_up):
        ref.tell()
    grad_normed = dot_nt(grad_gate[...], w_gate[...]) + dot_nt(grad_up[...], w_up[...])
    grad_value, dgain = norm_back(after, gain[...], grad_normed)
    dgain_out[...] = dgain
    grad_after = cotangent[...].astype(jnp.float32) + grad_value
    branch = grad_after.astype(low)
    put_rows(g_mine, dot_nt(branch, w_out[...]), False)
    rows = Rows(me, g_mine, g_out, g_send, g_recv, False)
    rows.start()
    branch_out[...] = branch
    after_out[...] = grad_after
    final_out[...] = (after + dot_nn(mixed[...], w_down[...])).astype(low)
    rows.arrive()
    back.end()
    rows.end()


def turn_kernel(
    dq_in, dkv_in, middle, gain, grad_after, w_query, w_out,
    g_out, dq_out, part_out, branch_out, grad_out, dgain_out,
    dq_mine, dq_send, dq_recv, g_mine, g_send, g_recv, kv_send, kv_recv, got_core,
):
    low = jnp.bfloat16
    me = Share()
    back = Rows(me, dq_in, dq_mine, dq_send, dq_recv, True)
    back.start()
    pairs = Sums(me, dkv_in, part_out, kv_send, kv_recv, got_core, None, None)
    pairs.start()
    back.arrive()
    grad_query = get_rows(dq_mine, True).astype(low)
    dq_out[...] = grad_query
    grad_value, dgain = norm_back(middle[...], gain[...], dot_nt(grad_query, w_query[...]))
    dgain_out[...] = dgain
    grad_middle = grad_after[...] + grad_value
    branch = grad_middle.astype(low)
    put_rows(g_mine, dot_nt(branch, w_out[...]), False)
    rows = Rows(me, g_mine, g_out, g_send, g_recv, False)
    rows.start()
    branch_out[...] = branch
    grad_out[...] = grad_middle
    pairs.join()
    rows.arrive()
    back.end()
    rows.end()
    pairs.end()


def close_kernel(
    dq_in, dkv_in, layer_input, gain, grad_middle, w_query, w_key, w_value,
    cross_part, cross_got, w_ckey, w_cvalue,
    grad_out, encoder_out, dq_out, dk_out, dv_out, cross_dk, cross_dv, dgain_out,
    dq_mine, dq_send, dq_recv, total, *scratch,
):
    low = jnp.bfloat16
    me = Share()
    sums, self_own, cross_own, cross_total = scratch[:5], scratch[5:8], scratch[8:11], scratch[11]
    pairs = Sums(me, dkv_in, total, *sums)
    pairs.start()
    back = Rows(me, dq_in, dq_mine, dq_send, dq_recv, True)
    back.start()
    cross_total[...] = cross_part()[pl.ds(me.x_hi * 4, 4)] + cross_got[...]
    cross = Owners(me, cross_total, *cross_own)
    for step in range(3):
        cross.send(step)
    pairs.over()
    cross.arrive()
    keys, values = get_pairs(cross_own[0])
    keys, values = keys.astype(low), values.astype(low)
    cross_dk[...] = keys
    cross_dv[...] = values
    encoder_out[...] = dot_nt(keys, w_ckey[...]) + dot_nt(values, w_cvalue[...])
    back.arrive()
    grad_query = get_rows(dq_mine, True).astype(low)
    dq_out[...] = grad_query
    grad_normed = dot_nt(grad_query, w_query[...])
    owners = Owners(me, total, *self_own)
    pairs.finish(owners)
    owners.arrive()
    keys, values = get_pairs(self_own[0])
    keys, values = keys.astype(low), values.astype(low)
    dk_out[...] = keys
    dv_out[...] = values
    grad_normed = grad_normed + dot_nt(keys, w_key[...]) + dot_nt(values, w_value[...])
    residual = layer_input[...].astype(jnp.float32)
    grad_value, dgain = norm_back(residual, gain[...], grad_normed)
    dgain_out[...] = dgain
    grad_out[...] = grad_middle[...] + grad_value
    back.end()
    pairs.end()
    cross.end()
    owners.end()


def dot_nn(left, right):
    return jnp.dot(left, right, preferred_element_type=jnp.float32)


def dot_nt(left, right):
    return lax.dot_general(
        left, right, (((1,), (1,)), ((), ())), preferred_element_type=jnp.float32
    )


def head_lanes(value, head):
    lane = lax.broadcasted_iota(jnp.int32, value.shape, 1)
    return jnp.where(lane // 64 == head, value, jnp.zeros_like(value))


def head_rows(value, head):
    row = lax.broadcasted_iota(jnp.int32, value.shape, 0)
    return jnp.where(row // 64 == head, value, jnp.zeros_like(value))


def bias_offset(pair, side, chunk):
    c = lax.axis_index("ctx")
    mine = (c // 8) * 2 + c % 2
    block = 8 * pair + (mine if side == 0 else 7 - mine)
    return pl.multiple_of((15 - block) * 128 + chunk * 256, 128)


def bias_at(wide, head, pair, chunk):
    return jnp.concatenate(
        [wide[head, pl.ds(bias_offset(pair, side, chunk), 256), :] for side in range(2)], axis=1
    )


def forward_kernel(causal, *refs):
    if causal:
        q, kv, waves, o_low, o_full, lse, wide, values_t, score, total = refs
        def build(head, carry):
            for tile in range(USED):
                row = jnp.broadcast_to(waves[head, tile : tile + 1, :], (128, 256))
                turned = pltpu.roll(row, 129, 1, stride=1, stride_axis=0)
                wide[head, tile * 128 : tile * 128 + 128, :] = turned[:, :128]
            wide[head, USED * 128 :, :] = jnp.full(
                ((TILES - USED) * 128, 128), NEGATIVE, jnp.float32
            )
            return carry

        lax.fori_loop(0, 3, build, 0)
    else:
        q, kv, o_low, o_full, lse, values_t, score, total = refs

    for chunk in range(8):
        values_t[chunk] = kv[2 * chunk : 2 * chunk + 2, :, 128:384].reshape(256, 256).T
    for pair in range(2):
        chunks = 4 if causal and pair == 0 else 8
        rows = q[2 * pair : 2 * pair + 2].reshape(256, 256)
        total[...] = jnp.zeros_like(total)

        def one_head(head, carry):
            masked = head_lanes(rows, head)

            top = jnp.full((8, 256), NEGATIVE, jnp.float32)
            for chunk in range(chunks):
                keys = kv[2 * chunk : 2 * chunk + 2, :, 0:256].reshape(256, 256)
                block = dot_nt(keys, masked)
                if causal:
                    block = block + bias_at(wide, head, pair, chunk)
                score[chunk] = block
                top = jnp.maximum(top, jnp.max(block.reshape(32, 8, 256), axis=0))
            top = jnp.max(top, axis=0, keepdims=True)
            summed = jnp.zeros((8, 256), jnp.float32)
            held = jnp.zeros((256, 256), jnp.float32)
            for chunk in range(chunks):
                expo = jnp.exp(score[chunk] - top)
                summed = summed + jnp.sum(expo.reshape(32, 8, 256), axis=0)
                held = held + dot_nn(values_t[chunk], expo.astype(jnp.bfloat16))
            summed = jnp.sum(summed, axis=0, keepdims=True)
            total[...] += head_rows(held * (1.0 / summed), head + 1)
            lse[head, pair] = top + jnp.log(summed)
            return carry

        lax.fori_loop(0, 3, one_head, 0)
        final = total[...].T.reshape(2, 128, 256)
        o_full[2 * pair : 2 * pair + 2] = final
        o_low[2 * pair : 2 * pair + 2] = final.astype(jnp.bfloat16)


def attend(q, kv, waves, collective_id, greet, carry, hops, pair_hops=()):
    causal = waves is not None
    shapes = [
        ((4, 128, 256), jnp.bfloat16),
        ((4, 128, 256), jnp.float32),
        ((3, 2, 1, 256), jnp.float32),
    ]
    args = [q, kv]
    if causal:
        shapes.append(((3, TILES * 128, 128), jnp.float32))
        args.append(waves)
    return staged_call(
        functools.partial(forward_kernel, causal),
        "attend_self" if causal else "attend_cross",
        args,
        shapes,
        [
            pltpu.VMEM((8, 256, 256), jnp.bfloat16),
            pltpu.VMEM((8, 256, 256), jnp.float32),
            pltpu.VMEM((256, 256), jnp.float32),
        ],
        collective_id,
        greet,
        carry,
        hops,
        pair_hops=pair_hops,
    )


def backward_kernel(causal, *refs):
    if causal:
        (q, kv, grad, o_full, lse, wide, cross_part, dq, dkv, waves, cross_got,
         keys_t, dk, dv, dq_t, turned, along, cross_send, cross_recv) = refs
        along[...] = jnp.zeros_like(along)
        me = Place()
        passing = me.send(
            "xab", cross_part.at[pl.ds((1 - me.x_hi) * 4, 4)], cross_got, cross_send, cross_recv
        )
    else:
        q, kv, grad, o_full, lse, dq, dkv, keys_t, dk, dv, dq_t, turned = refs
    dk[...] = jnp.zeros_like(dk)
    dv[...] = jnp.zeros_like(dv)

    for chunk in range(8):
        keys_t[chunk] = kv[2 * chunk : 2 * chunk + 2, :, 0:256].reshape(256, 256).T
    for pair in range(2):
        chunks = 4 if causal and pair == 0 else 8
        both = slice(2 * pair, 2 * pair + 2)
        rows = q[both].reshape(256, 256)
        grads = grad[both].reshape(256, 256)
        turned[...] = (grads.astype(jnp.float32) * o_full[both].reshape(256, 256)).T
        dq_t[...] = jnp.zeros_like(dq_t)

        def one_head(head, carry):
            masked = head_lanes(rows, head)
            masked_grads = head_lanes(grads, head + 1)
            delta = jnp.sum(head_rows(turned[...], head + 1), axis=0, keepdims=True)
            row_lse = lse[head, pair]

            held = jnp.zeros((256, 256), jnp.float32)
            for chunk in range(chunks):
                block = kv[2 * chunk : 2 * chunk + 2].reshape(256, 384)
                scores = dot_nt(block[:, 0:256], masked)
                if causal:
                    scores = scores + bias_at(wide, head, pair, chunk)
                probs = jnp.exp(scores - row_lse)
                grad_probs = dot_nt(block[:, 128:384], masked_grads)
                grad_scores = probs * (grad_probs - delta)
                low = grad_scores.astype(jnp.bfloat16)
                spot = slice(chunk * 256, chunk * 256 + 256)
                dk[spot] += dot_nn(low, masked)
                dv[spot] += dot_nn(probs.astype(jnp.bfloat16), masked_grads)
                if causal:
                    for side in range(2):
                        where = pl.ds(bias_offset(pair, side, chunk), 256)
                        along[head, where, :] += grad_scores[:, 128 * side : 128 * side + 128]
                held = held + dot_nn(keys_t[chunk], low)
            dq_t[...] += head_rows(held, head)
            return carry

        lax.fori_loop(0, 3, one_head, 0)
        dq[both] = dq_t[...].T.reshape(2, 128, 256).astype(jnp.bfloat16)

    def pack(block, carry):
        spot = pl.ds(pl.multiple_of(block * 128, 128), 128)
        key_part, value_part = dk[spot], dv[spot]
        dkv[block, :, 0:128] = key_part[:, 0:128].astype(jnp.bfloat16)
        dkv[block, :, 128:256] = (key_part[:, 128:256] + value_part[:, 0:128]).astype(jnp.bfloat16)
        dkv[block, :, 256:384] = value_part[:, 128:256].astype(jnp.bfloat16)
        return carry

    lax.fori_loop(0, 16, pack, 0)
    if causal:
        waves[...] = jnp.zeros_like(waves)

        def fold(head, carry):
            for tile in range(USED):
                value = along[head, tile * 128 : tile * 128 + 128, :]
                value = jnp.concatenate([value, jnp.zeros_like(value)], axis=1)
                count = 64
                while count >= 1:
                    value = pltpu.roll(value[:count], count, 1) + value[count:]
                    count //= 2
                waves[head, tile : tile + 1, :] = value
            return carry

        lax.fori_loop(0, 3, fold, 0)
        passing.wait()


def attend_back(q, kv, grad, o_full, lse, wide, cross_part):
    causal = wide is not None
    shapes = [((4, 128, 256), jnp.bfloat16), ((16, 128, 384), jnp.bfloat16)]
    args = [q, kv, grad, o_full, lse]
    scratch = [
        pltpu.VMEM((8, 256, 256), jnp.bfloat16),
        pltpu.VMEM((2048, 256), jnp.float32),
        pltpu.VMEM((2048, 256), jnp.float32),
        pltpu.VMEM((256, 256), jnp.float32),
        pltpu.VMEM((256, 256), jnp.float32),
    ]
    if causal:
        shapes += [((3, TILES, 256), jnp.float32), ((4, 128, 384), jnp.bfloat16)]
        args += [wide, cross_part]
        scratch.append(pltpu.VMEM((3, TILES * 128, 128), jnp.float32))
        scratch += [pltpu.SemaphoreType.DMA] * 2
    return staged_call(
        functools.partial(backward_kernel, causal),
        "attend_back_self" if causal else "attend_back_cross",
        args,
        shapes,
        scratch,
        9 if causal else None,
        ("xab",) if causal else None,
    )


PRECISE = lax.Precision.HIGHEST


def body(
    layer_input,
    encoder_states,
    cotangent,
    bucket_ids,
    bias_table,
    gain_first,
    gain_second,
    gain_third,
    self_query,
    self_key,
    self_value,
    self_output,
    cross_query,
    cross_key,
    cross_value,
    cross_output,
    gate_weight,
    up_weight,
    down_weight,
):
    bucket_count, head_count = bias_table.shape
    width = layer_input.shape[-1]
    layer_input, encoder_states, cotangent = layer_input[0], encoder_states[0], cotangent[0]
    gain_first, gain_second, gain_third = (
        gain.reshape(1, width) for gain in (gain_first, gain_second, gain_third)
    )
    low, full = jnp.bfloat16, jnp.float32
    grouped, rows, wide_rows, line = (4, 128, 256), (128, 768), (128, 2048), (1, 768)
    first_head = 3 * ((lax.axis_index("ctx") // 2) % 4)
    padded = jnp.pad(bucket_ids, (TILES * 128 - bucket_ids.shape[0] + 128, 0), constant_values=-1)
    last = padded.shape[0]
    ids = jnp.stack([padded[last - 255 - 128 * k : last - 128 * k] for k in range(TILES)])
    ids = jnp.pad(ids, ((0, 0), (0, 1)), constant_values=-1)
    hot = (ids[:, :, None] == jnp.arange(bucket_count, dtype=jnp.int32)).astype(jnp.float32)
    own_table = lax.dynamic_slice_in_dim(bias_table, first_head, 3, 1)
    waves = jnp.einsum("kxb,bh->hkx", hot, own_table, precision=PRECISE)
    waves = jnp.where((ids >= 0)[None], waves, NEGATIVE)

    (
        (self_q, self_kv, cross_kv, normed_one, normed_one_peer, encoder_peer, cotangent_peer),
        weights,
        feed,
    ) = open_layer(
        layer_input,
        encoder_states,
        gain_first,
        cotangent,
        (
            self_query, self_key, self_value, cross_key, cross_value,
            self_output, cross_query, cross_output, gate_weight, up_weight, down_weight,
        ),
        2,
    )
    w_query, w_key, w_value, w_ckey, w_cvalue, w_out, w_cquery, w_cout = weights
    (self_low, self_full, self_lse, wide), feed = attend(
        self_q, self_kv, waves, 7, ("xab", "core", "za", "zb"), (*feed, cross_kv),
        ("za", "zb", None, None, "core", None),
        (("xab", "near"), ("core", "near")),
    )
    (
        (cross_q, attended, middle, normed_two, attended_peer, normed_two_peer), feed
    ) = shared_call(
        middle_kernel,
        "middle",
        (self_low, layer_input, gain_second, w_out, w_cquery),
        ((grouped, low), (rows, low), (rows, full), (rows, low)),
        row_scratch() + row_scratch(),
        3,
        feed,
        ("core", "core", "side", "side", None, "side"),
        (1, 3),
        pair_hops=(("core", "far"),),
    )
    *feed, cross_kv = feed
    cross_kv = cross_kv.reshape(16, 128, 384)
    (cross_low, cross_full, cross_lse), feed = attend(
        cross_q, cross_kv, None, 8, ("core", "za", "zb"), feed,
        (None, None, "za", "zb", None, "core"),
    )
    feed_results, _ = shared_call(
        feed_kernel,
        "feed_forward",
        (cross_low, middle, gain_third, w_cout, cotangent),
        (
            (grouped, low), (rows, low), (rows, low), (rows, low), (wide_rows, low),
            (wide_rows, low), (wide_rows, low), (rows, low), (rows, full), (line, full),
        ),
        row_scratch() + row_scratch() + [pltpu.VMEM(wide_rows, full)],
        4,
        feed,
        (None, None, "core", "core", None, None),
        (2, 3, 7, 4, 5, 6),
        True,
    )
    (
        cross_grads, layer_output, crossed, normed_three, grad_gate, grad_up, mixed,
        branch_after, grad_after, dgain_third,
        *feed_peers,
    ) = feed_results
    cross_dq, cross_dkv = attend_back(
        cross_q, cross_kv, cross_grads, cross_full, cross_lse, None, None
    )
    (
        self_grads, grad_cquery, cross_part, branch_middle, grad_middle, dgain_second,
        grad_cquery_peer, branch_middle_peer,
    ) = shared_call(
        turn_kernel,
        "turn",
        (
            cross_dq, cross_dkv.reshape(8, 2, 128, 384), middle, gain_second, grad_after,
            w_cquery, w_out,
        ),
        (
            (grouped, low), (rows, low), ((8, 128, 384), low), (rows, low), (rows, full),
            (line, full),
        ),
        row_scratch() + row_scratch() + sum_scratch()[:3],
        5,
        share=(1, 3),
    )
    self_dq, self_dkv, grad_waves, cross_got = attend_back(
        self_q, self_kv, self_grads, self_full, self_lse, wide, cross_part
    )
    (
        grad_input, grad_encoder, grad_queries, grad_keys, grad_values, grad_ckeys, grad_cvalues,
        dgain_first, *close_peers,
    ) = shared_call(
        close_kernel,
        "close",
        (
            self_dq, self_dkv.reshape(8, 2, 128, 384), layer_input, gain_first, grad_middle,
            w_query, w_key, w_value, cross_part, cross_got, w_ckey, w_cvalue,
        ),
        ((rows, full), (rows, full)) + ((rows, low),) * 5 + ((line, full),),
        row_scratch()
        + [pltpu.VMEM((4, 128, 384), low)]
        + sum_scratch()
        + owner_scratch()
        + owner_scratch()
        + [pltpu.VMEM((4, 128, 384), low)],
        6,
        share=(2, 3, 4, 5, 6),
    )
    own_grads = jnp.einsum("kxb,hkx->bh", hot, grad_waves, precision=PRECISE)
    local_table = lax.dynamic_update_slice_in_dim(
        jnp.zeros_like(bias_table), own_grads, first_head, 1
    )
    small = jnp.concatenate(
        [dgain_first[0], dgain_second[0], dgain_third[0], local_table.reshape(-1)]
    )
    small = jnp.pad(small, (0, 24 * 128 - small.shape[0])).reshape(24, 128)
    crossed_peer, normed_three_peer, branch_after_peer, *feed_peers = feed_peers
    full_sums, sums = reduce_weights(
        (
            normed_one, attended, normed_two, encoder_states, crossed, normed_three,
            grad_queries, grad_keys, grad_values, branch_middle,
            grad_cquery, grad_ckeys, grad_cvalues, branch_after,
            grad_gate, grad_up, mixed, cotangent,
        ),
        (
            normed_one_peer, attended_peer, normed_two_peer, encoder_peer, crossed_peer,
            normed_three_peer,
            *close_peers[:3], branch_middle_peer,
            grad_cquery_peer, *close_peers[3:], branch_after_peer,
            *feed_peers, cotangent_peer,
        ),
        small,
        1,
    )
    *shards, layer_output, grad_input, grad_encoder = place_all(
        full_sums, (layer_output, grad_input, grad_encoder)
    )
    sums = sums.reshape(-1)
    return (
        layer_output[None],
        grad_input[None],
        grad_encoder[None],
        sums[3 * width : 3 * width + bucket_count * head_count].reshape(bucket_count, head_count),
        sums[:width],
        sums[width : 2 * width],
        sums[2 * width : 3 * width],
    ) + tuple(shards)


def solution(mesh):
    placed = (
        P("dp", "ctx", None),
        P("dp", "ctx", None),
        P("dp", "ctx", None),
        P(),
        P(),
        P(),
        P(),
        P(),
        P("dp", None),
        P("dp", None),
        P("dp", None),
        P("dp", None),
        P("dp", None),
        P("dp", None),
        P("dp", None),
        P("dp", None),
        P("dp", None),
        P("dp", None),
        P("dp", None),
    )
    return jax.shard_map(
        body,
        mesh=mesh,
        in_specs=placed,
        out_specs=(
            P("dp", "ctx", None),
            P("dp", "ctx", None),
            P("dp", "ctx", None),
            P(),
            P(),
            P(),
            P(),
            P("dp", None),
            P("dp", None),
            P("dp", None),
            P("dp", None),
            P("dp", None),
            P("dp", None),
            P("dp", None),
            P("dp", None),
            P("dp", None),
            P("dp", None),
            P("dp", None),
        ),
        check_vma=False,
    )
```

```python
import functools
import math
import jax
import jax.numpy as jnp
from jax import lax
from jax.experimental import pallas as pl
from jax.experimental.pallas import tpu as pltpu
from jax.sharding import PartitionSpec as P

MESH = pl.DeviceIdType.MESH
VMEM_BYTES = 62 * 2**20
ANY = pl.BlockSpec(memory_space=pl.ANY)
HBM = pl.BlockSpec(memory_space=pltpu.HBM)
VMEM = pl.BlockSpec(memory_space=pltpu.VMEM)


class Place:
    def __init__(self):
        c = lax.axis_index("ctx")
        d = lax.axis_index("dp")
        self.c, self.d = c, d
        self.x_hi = c // 8
        self.z = (c // 2) % 4
        self.core = c % 2
        self.y = d // 2
        self.x_lo = d % 2
        self.y_a = self.y + 1 - 2 * (self.y % 2)
        self.y_b = 3 - self.y
        self.y_ab = 3 - self.y_a
        self.z_a = self.z + 1 - 2 * (self.z % 2)
        self.z_b = 3 - self.z
        self.z_ab = 3 - self.z_a
        far_lo, far_hi = 1 - self.x_lo, 1 - self.x_hi
        self.x = self.x_lo * 2 + self.x_hi
        self.x_a = far_lo * 2 + self.x_hi
        self.x_b = far_lo * 2 + far_hi
        self.x_ab = self.x_lo * 2 + far_hi
        same = self.x_hi * 8 + self.z * 2 + self.core
        self.dev = {
            "core": (self.x_hi * 8 + self.z * 2 + 1 - self.core, d),
            "ya": (same, self.y_a * 2 + self.x_lo),
            "yb": (same, self.y_b * 2 + self.x_lo),
            "za": (self.x_hi * 8 + self.z_a * 2 + self.core, d),
            "zb": (self.x_hi * 8 + self.z_b * 2 + self.core, d),
            "xa": (same, self.y * 2 + far_lo),
            "xb": (far_hi * 8 + self.z * 2 + self.core, self.y * 2 + far_lo),
            "xab": (far_hi * 8 + self.z * 2 + self.core, d),
        }

    def greet(self, names):
        barrier = pltpu.get_barrier_semaphore()
        for name in names:
            pl.semaphore_signal(
                barrier, inc=1, device_id=self.dev[name], device_id_type=MESH
            )
        pl.semaphore_wait(barrier, len(names))

    def send(self, name, src, dst, send_sem, recv_sem):
        copy = pltpu.make_async_remote_copy(
            src_ref=src,
            dst_ref=dst,
            send_sem=send_sem,
            recv_sem=recv_sem,
            device_id=self.dev[name],
            device_id_type=MESH,
        )
        copy.start()
        return copy


EARLY_PLAN = (
    ((0, "pair", 0), (1, "pair", 0), (2, "pair", 0)),
    ((3, "pair", 0), (4, "pair", 0)),
)
LATE_PLAN = (((0, "zb", 0), (1, "za", 0)), ((2, "pair", 0),))
FEED_PLAN = (((0, "za", 0), (1, "zb", 0), (0, "za", 1), (1, "zb", 1), (2, "pair", 0)),)


class Chain:
    def __init__(self, me, source, target, kind, half, piece, pieces, sems):
        rows, cols = source.shape[-2:]
        width = cols // 2 // pieces
        self.me, self.source, self.target, self.kind = me, source, target, kind
        self.sems, self.slot, self.copies = sems, 0, []
        self.all_rows = pl.ds(0, rows)
        if kind == "pair":
            self.rows = pl.ds(half * (rows // 2), rows // 2)
            self.all_rows = self.rows
            flip = half == 1
        else:
            bit = me.z % 2 if kind == "za" else me.z // 2
            self.rows = pl.ds(pl.multiple_of(bit * (rows // 2), 16), rows // 2)
            flip = kind == "zb"
        self.cols = pl.ds(pl.multiple_of(me.core * (cols // 2) + piece * width, 128), width)
        self.other = pl.ds(pl.multiple_of((1 - me.core) * (cols // 2) + piece * width, 128), width)
        self.first, self.second = ("yb", "ya") if flip else ("ya", "yb")
        self.near = me.y_b if flip else me.y_a
        self.side = "xb" if flip else "xa"
        if kind != "pair" and pieces == 2:
            self.side = ("xb", "xa")[piece]
        self.stages = 4 if kind == "pair" else 5

    def go(self, name, src, dst):
        send_sem, recv_sem, index = self.sems
        copy = self.me.send(
            name, src, dst, send_sem.at[index, self.slot], recv_sem.at[index, self.slot]
        )
        self.slot += 1
        self.copies.append(copy)
        return copy

    def hop(self, name):
        me, out = self.me, self.target
        if name == "side":
            got = out.at[:, me.x_lo, self.rows, self.cols]
            return self.go(self.side, got, got)
        if name == "core":
            got = out.at[:, :, self.all_rows, self.cols]
            return self.go("core", got, got)
        got = out.at[:, :, self.rows, self.cols]
        return self.go(self.kind, got, got)

    def run(self, stage):
        me, out = self.me, self.target
        if stage == 0:
            mine = self.source.at[self.rows, self.cols]
            spot = out.at[me.y, me.x_lo, self.rows, self.cols]
            self.first_copy = self.go(self.first, mine, spot)
            self.second_copy = self.go(self.second, mine, spot)
            self.own_copy = self.go(
                "core",
                self.source.at[self.rows, self.other],
                out.at[me.y, me.x_lo, self.rows, self.other],
            )
        elif stage == 1:
            self.first_copy.wait_recv()
            got = out.at[self.near, me.x_lo, self.rows, self.cols]
            self.third_copy = self.go(self.second, got, got)
        elif stage == 2:
            self.second_copy.wait_recv()
            self.own_copy.wait_recv()
            self.third_copy.wait_recv()
            got = out.at[:, me.x_lo, self.rows, self.cols]
            self.last = self.go(self.side, got, got)
        elif stage == 3 and self.kind != "pair":
            self.last.wait_recv()
            got = out.at[:, :, self.rows, self.cols]
            self.last = self.go(self.kind, got, got)
        elif stage == self.stages - 1:
            self.last.wait_recv()
            got = out.at[:, :, self.all_rows, self.cols]
            self.last = self.go("core", got, got)
        elif stage == self.stages:
            self.last.wait_recv()


def make_groups(me, ins, outs, plan, send_sem, recv_sem):
    pieces = {}
    for group in plan:
        for array, kind, piece in group:
            pieces[array] = max(pieces.get(array, 0), piece + 1)
    groups = []
    index = 0
    for group in plan:
        chains = []
        for array, kind, piece in group:
            for half in range(2 if kind == "pair" else 1):
                chains.append(
                    Chain(
                        me, ins[array], outs[array], kind, half, piece, pieces[array],
                        (send_sem, recv_sem, index),
                    )
                )
                index += 1
        groups.append(chains)
    return groups


def run_stage(chains, stage):
    for chain in chains:
        chain.run(stage)


def chain_count(plan):
    return sum(2 if kind == "pair" else 1 for group in plan for _, kind, _ in group)


class Staged:
    def __init__(self, source, target, sem):
        self.copy = pltpu.make_async_copy(source, target, sem)
        self.copy.start()
        self.target, self.here = target, False

    def __call__(self):
        if not self.here:
            self.copy.wait()
            self.here = True
        return self.target

    def __getitem__(self, index):
        return self()[index]

    @property
    def at(self):
        return self().at


class Shared:
    def __init__(self, ref, peer, send_sem, recv_sem):
        self.ref, self.peer, self.sems = ref, peer, (send_sem, recv_sem)

    def __getitem__(self, index):
        return self.ref[index]

    def __setitem__(self, index, value):
        self.ref[index] = value
        if index is Ellipsis:
            self.tell()

    def tell(self):
        self.copy = Place().send("core", self.ref, self.peer, *self.sems)


class Deferred:
    def __init__(self, copies, source, target, sem):
        self.copies, self.source, self.target, self.here = copies, source, target, False
        rows = source.shape[2]
        self.loads = [
            pltpu.make_async_copy(
                source.at[y, x], target.at[pl.ds((2 * y + x) * rows, rows)], sem.at[2 * y + x]
            )
            for y in range(4)
            for x in range(2)
        ]

    def prepare(self):
        for copy in self.copies:
            copy.wait_recv()
        for load in self.loads:
            load.start()

    def __getitem__(self, index):
        if not self.here:
            for load in self.loads:
                load.wait()
            self.here = True
        return self.target[index]


def staged_kernel(kernel, n_in, n_out, n_carry, greet, hops, share, load_carry, pair_hops, *refs):
    refs = list(refs)

    def take(count):
        taken = refs[:count]
        del refs[:count]
        return taken

    ins, _, outs, peers, carried, targets = (
        take(n_in), take(n_carry), take(n_out), take(len(share)), take(n_carry), take(n_in)
    )
    (sem,) = take(1)
    staged = [Staged(ref, target, sem.at[i]) for i, (ref, target) in enumerate(zip(ins, targets))]
    moved = []
    if hops:
        send_sem, recv_sem = take(2)
    if share:
        share_send, share_recv = take(2)
        for slot, index in enumerate(share):
            outs[index] = Shared(
                outs[index], peers[slot], share_send.at[slot], share_recv.at[slot]
            )
    if greet is not None:
        me = Share()
        if greet == "all":
            me.greet_all(extra=("xa", "xb") if "side" in hops else ())
        else:
            me.greet(greet)
    if hops:
        (chains,) = make_groups(me, carried, carried, FEED_PLAN, send_sem, recv_sem)
        delayed = []
        for chain, hop in zip(chains, hops):
            if hop == "side" and greet == "all":
                delayed.append(chain)
            elif hop is not None:
                moved.append(chain.hop(hop))
        if delayed:
            staged.append(lambda: moved.extend(chain.hop("side") for chain in delayed))
    if pair_hops:
        pair_send, pair_recv = take(2)
        for slot, (name, side) in enumerate(pair_hops):
            blocks = carried[3].at[me.x_hi if side == "near" else 1 - me.x_hi, :, me.core]
            moved.append(
                me.send(name, blocks, blocks, pair_send.at[slot], pair_recv.at[slot])
            )
    if load_carry:
        targets, load_sem = take(3), take(1)[0]
        last = [[moved[0]], [moved[1]], []]
        staged += [
            Deferred(last[i], carried[i], targets[i], load_sem.at[i]) for i in range(3)
        ]
    if greet != "all":
        staged = [ref() for ref in staged]
    kernel(*staged, *outs, *refs)
    if greet == "all":
        for ref in staged[:n_in]:
            ref()
    for copy in moved:
        if load_carry:
            copy.wait_send()
        else:
            copy.wait()
    for index in share:
        outs[index].copy.wait()


def staged_call(
    kernel, name, args, shapes, scratch, collective_id=None, greet=None, carry=(), hops=(), share=(),
    load_carry=False, pair_hops=(),
):
    carry = tuple(carry)
    shapes = tuple(shapes)
    n_out = len(shapes)
    shapes = shapes + tuple(shapes[index] for index in share)
    outs = pl.pallas_call(
        functools.partial(
            staged_kernel, kernel, len(args), n_out, len(carry), greet, hops, tuple(share),
            load_carry, pair_hops,
        ),
        out_shape=[jax.ShapeDtypeStruct(shape, kind) for shape, kind in shapes]
        + [jax.ShapeDtypeStruct(array.shape, array.dtype) for array in carry],
        in_specs=[HBM] * len(args) + [ANY] * len(carry),
        out_specs=[VMEM] * len(shapes) + [ANY] * len(carry),
        scratch_shapes=[pltpu.VMEM(arg.shape, arg.dtype) for arg in args]
        + [pltpu.SemaphoreType.DMA((len(args),))]
        + ([pltpu.SemaphoreType.DMA((6, 7))] * 2 if hops else [])
        + ([pltpu.SemaphoreType.DMA((len(share),))] * 2 if share else [])
        + ([pltpu.SemaphoreType.DMA((len(pair_hops),))] * 2 if pair_hops else [])
        + (
            [pltpu.VMEM((8 * array.shape[2], array.shape[3]), array.dtype) for array in carry]
            + [pltpu.SemaphoreType.DMA((3, 8))]
            if load_carry
            else []
        )
        + scratch,
        input_output_aliases={len(args) + i: len(shapes) + i for i in range(len(carry))},
        compiler_params=pltpu.CompilerParams(
            collective_id=collective_id,
            has_side_effects=greet is not None,
            vmem_limit_bytes=VMEM_BYTES,
        ),
        name=name,
    )(*args, *carry)
    return (outs[: len(shapes)], outs[len(shapes) :]) if carry else outs

AXES = ("y", "x", "z")


ACT_OF = (0, 0, 0, 1, 2, 3, 3, 4)


class Outer:
    def __init__(self, me, ins, acc, grads, feeds, cots, turned, mixed_t, sem):
        self.me, self.acc = me, acc
        self.grads, self.feeds, self.cots = grads, feeds, cots
        self.turned, self.mixed_t = turned, mixed_t
        self.copies = []
        half = pl.ds(pl.multiple_of(me.core * 384, 128), 384)
        self.fetch(ins[0], turned, sem)
        self.fetch(ins[1], mixed_t, sem)
        for side in range(2):
            begin = pl.ds(128 * side, 128)
            own = ins[2 + 11 * side : 13 + 11 * side]
            for index in range(8):
                self.fetch(own[index].at[:, half], grads.at[index, begin], sem)
            for index in range(2):
                self.fetch(own[8 + index], feeds.at[index, begin], sem)
            self.fetch(own[10], cots.at[begin], sem)

    def fetch(self, src, dst, sem):
        copy = pltpu.make_async_copy(src, dst, sem.at[len(self.copies)])
        copy.start()
        self.copies.append(copy)

    def ready(self):
        for copy in self.copies:
            copy.wait()

    def put(self, first, block, cols, value):
        width = value.shape[1]
        value = value.astype(jnp.bfloat16).reshape(4, 2, 2, 16, width)
        for x_lo in range(2):
            for part in range(2):
                self.acc[
                    first + part, :, 2 * x_lo + block // 4, block % 4, :, cols
                ] = value[:, x_lo, part]

    def compute(self, first):
        def dot(left, right):
            return jnp.dot(left, right, preferred_element_type=jnp.float32)

        both = slice(first, first + 2)
        for index in range(8):
            left = self.turned[ACT_OF[index], :, both].reshape(256, 256)
            self.put(first, index, slice(0, 384), dot(left, self.grads[index]))
        left = self.turned[5, :, both].reshape(256, 256)
        for block in range(8):
            cols = pl.ds(pl.multiple_of((2 * block + self.me.core) * 128, 128), 128)
            right = jnp.concatenate([self.feeds[0, :, cols], self.feeds[1, :, cols]], axis=1)
            self.put(first, block, slice(384, 640), dot(left, right))
        left = self.mixed_t[:, :, self.me.core].reshape(1024, 256)
        down = dot(left, self.cots[:, 128 * first : 128 * first + 256])
        down = down.astype(jnp.bfloat16).reshape(4, 2, 2, 4, 16, 256)
        for x_lo in range(2):
            for x_hi in range(2):
                for part in range(2):
                    self.acc[first + part, :, 2 * x_lo + x_hi, :, :, 640:768] = down[
                        :, x_lo, x_hi, :, :, 128 * part : 128 * part + 128
                    ]


def reduce_kernel(*refs):
    ins, small = refs[:24], refs[24]
    full, small_out = refs[25:27]
    (acc, r1, r2, r3, r4, r5, r6, sm_in,
     send_sem, recv_sem, sm_send, sm_recv, ag_send, ag_recv, *outer) = refs[27:]
    recvs = (r1, r2, r3, r4, r5, r6)
    me = Place()
    outer = Outer(me, ins, acc, *outer)
    me.greet(("core", "ya", "yb", "xa", "xb", "za", "zb", "xab"))
    spots = {
        "y": (me.y, me.y_a, me.y_b, me.y_ab),
        "x": (me.x, me.x_a, me.x_b, me.x_ab),
        "z": (me.z, me.z_a, me.z_b, me.z_ab),
    }
    parts = range(6)
    started = []

    def go(name, src, dst, send, recv):
        copy = me.send(name, src, dst, send, recv)
        started.append(copy)
        return copy

    small_out[...] = small[...]
    small_steps = ("core", "ya", "yb", "xa", "xb", "za", "zb")
    small_copies = []

    def small_start(step):
        small_copies.append(
            me.send(small_steps[step], small_out, sm_in.at[step], sm_send.at[step], sm_recv.at[step])
        )

    def small_end(step):
        small_copies[step].wait()
        small_out[...] = small_out[...] + sm_in[step]

    small_start(0)

    def order(part):
        first = (part // 2) % 3
        return [AXES[(first + k) % 3] for k in range(3)]

    def region(part, picks):
        return (part,) + tuple(picks.get(axis, slice(None)) for axis in AXES)

    def at(ref, index):
        return ref.at[index]

    def add(index, source, source_index):
        acc[index] = acc[index] + source[source_index]

    def dims(part):
        return ("a", "b") if part % 2 == 0 else ("b", "a")

    outer.ready()
    pending = {}
    for part in parts:
        axis = order(part)[0]
        me_at, a_at, b_at, ab_at = spots[axis]
        first, second = dims(part)
        sent = (a_at, ab_at) if first == "a" else (b_at, ab_at)
        if part % 2 == 0:
            outer.compute(part)
        pending[part] = []
        for slot, spot in enumerate(sent):
            pending[part].append(
                go(
                    axis + first,
                    at(acc, region(part, {axis: spot})),
                    r1.at[part, slot],
                    send_sem.at[part, 1 + slot],
                    recv_sem.at[part, 1 + slot],
                )
            )
    small_end(0)
    small_start(1)
    sem_at = {part: 3 for part in parts}

    def next_sem(part):
        sem_at[part] += 1
        return send_sem.at[part, sem_at[part] - 1], recv_sem.at[part, sem_at[part] - 1]

    for level in range(3):
        one, two = recvs[2 * level], recvs[2 * level + 1]
        for part in parts:
            axes = order(part)
            axis = axes[level]
            first, second = dims(part)
            me_at, a_at, b_at, ab_at = spots[axis]
            kept = b_at if first == "a" else a_at
            fixed = {name: spots[name][0] for name in axes[:level]}
            for copy in pending[part]:
                copy.wait_recv()
            add(region(part, {**fixed, axis: kept}), one, (part, 1))
            send, recv = next_sem(part)
            pending[part] = [
                go(axis + second, at(acc, region(part, {**fixed, axis: kept})), two.at[part], send, recv)
            ]
        for part in parts:
            axes = order(part)
            fixed = {name: spots[name][0] for name in axes[: level + 1]}
            add(region(part, fixed), one, (part, 0))
        small_end(2 * level + 1)
        small_start(2 * level + 2)
        for part in parts:
            axes = order(part)
            fixed = {name: spots[name][0] for name in axes[: level + 1]}
            for copy in pending[part]:
                copy.wait_recv()
            add(region(part, fixed), two, (part,))
            if level == 2:
                continue
            axis = axes[level + 1]
            first, second = dims(part)
            me_at, a_at, b_at, ab_at = spots[axis]
            sent = (a_at, ab_at) if first == "a" else (b_at, ab_at)
            pending[part] = []
            for slot, spot in enumerate(sent):
                send, recv = next_sem(part)
                pending[part].append(
                    go(
                        axis + first,
                        at(acc, region(part, {**fixed, axis: spot})),
                        recvs[2 * level + 2].at[part, slot],
                        send,
                        recv,
                    )
                )
        small_end(2 * level + 2)
        if level < 2:
            small_start(2 * level + 3)

    here = me.x_hi * 4 + me.z
    there = (1 - me.x_hi) * 4 + me.z
    for part in parts:
        full[here, me.core, part] = acc[part, me.y, me.x, me.z]
    used = [0]

    def pass_on(name, group, half):
        index = used[0]
        used[0] += 1
        src = full.at[group, me.core, pl.ds(3 * half, 3)]
        return go(name, src, src, ag_send.at[index], ag_recv.at[index])

    early = [pass_on("xab", here, half) for half in range(2)]
    near = [pass_on("za", here, 0), pass_on("zb", here, 1)]
    far = []
    for half in range(2):
        early[half].wait_recv()
        far.append(pass_on(("za", "zb")[half], there, half))
    base, base_far = me.x_hi * 4, (1 - me.x_hi) * 4
    ends = [pass_on("zb", here, 0), pass_on("za", here, 1)]
    ends += [pass_on("zb", there, 0), pass_on("za", there, 1)]
    for half in range(2):
        got = (me.z_a, me.z_b)[half]
        near[half].wait_recv()
        ends.append(pass_on(("zb", "za")[half], base + got, half))
    for half in range(2):
        got = (me.z_a, me.z_b)[half]
        far[half].wait_recv()
        ends.append(pass_on(("zb", "za")[half], base_far + got, half))
    for copy in ends:
        copy.wait_recv()
    last = go("core", full.at[:, me.core], full.at[:, me.core], ag_send.at[used[0]], ag_recv.at[used[0]])

    last.wait_recv()
    for copy in started:
        copy.wait_send()


def reduce_weights(turned, mixed, own, peer, small, collective_id):
    bf = jnp.bfloat16
    return pl.pallas_call(
        reduce_kernel,
        out_shape=[
            jax.ShapeDtypeStruct((8, 2, 6, 16, 768), bf),
            jax.ShapeDtypeStruct(small.shape, small.dtype),
        ],
        in_specs=[HBM] * 24 + [VMEM],
        out_specs=[VMEM] * 2,
        scratch_shapes=[
            pltpu.VMEM((6, 4, 4, 4, 16, 768), bf),
            pltpu.VMEM((6, 2, 4, 4, 16, 768), bf),
            pltpu.VMEM((6, 4, 4, 16, 768), bf),
            pltpu.VMEM((6, 2, 4, 16, 768), bf),
            pltpu.VMEM((6, 4, 16, 768), bf),
            pltpu.VMEM((6, 2, 16, 768), bf),
            pltpu.VMEM((6, 16, 768), bf),
            pltpu.VMEM((7,) + small.shape, small.dtype),
            pltpu.SemaphoreType.DMA((6, 10)),
            pltpu.SemaphoreType.DMA((6, 10)),
            pltpu.SemaphoreType.DMA((7,)),
            pltpu.SemaphoreType.DMA((7,)),
            pltpu.SemaphoreType.DMA((16,)),
            pltpu.SemaphoreType.DMA((16,)),
            pltpu.VMEM((8, 256, 384), bf),
            pltpu.VMEM((2, 256, 2048), bf),
            pltpu.VMEM((256, 768), bf),
            pltpu.VMEM((6, 8, 6, 16, 256), bf),
            pltpu.VMEM((8, 8, 2, 16, 256), bf),
            pltpu.SemaphoreType.DMA((24,)),
        ],
        compiler_params=pltpu.CompilerParams(
            collective_id=collective_id, has_side_effects=True, vmem_limit_bytes=VMEM_BYTES
        ),
        name="reduce_weights",
    )(turned, mixed, *own, *peer, small)


def place_kernel(full, *refs):
    passed, outs = refs[:3], refs[3:]
    wide = jnp.float32
    for o in range(16):
        group, core = o // 2, o % 2
        for part in range(6):
            rows = slice(16 * part, 16 * part + 16)
            block = full[group, core, part]
            outs[group][rows, core * 384 : core * 384 + 384] = block[:, 0:384].astype(wide)
            outs[8][rows, 128 * o : 128 * o + 128] = block[:, 384:512].astype(wide)
            outs[9][rows, 128 * o : 128 * o + 128] = block[:, 512:640].astype(wide)
            outs[10][16 * o : 16 * o + 16, 128 * part : 128 * part + 128] = block[
                :, 640:768
            ].astype(wide)
    for source, target in zip(passed, outs[11:]):
        target[...] = source[...]


def place_all(full, passed):
    wide = jnp.float32
    shapes = [((96, 768), wide)] * 8 + [((96, 2048), wide)] * 2 + [((256, 768), wide)]
    shapes += [(array.shape, array.dtype) for array in passed]
    return staged_call(place_kernel, "place", (full,) + tuple(passed), shapes, [])

NEGATIVE = -1e30
EPSILON = 1e-06
TILES = 23
USED = 16


class Share(Place):
    def __init__(self):
        super().__init__()
        self.dev["zab"] = (self.x_hi * 8 + self.z_ab * 2 + self.core, self.d)
        self.mine = self.x_hi * 2 + self.core
        self.slot = self.c // 4
        rest = self.c % 4
        self.owner = rest + (self.slot % 2) * (3 - 2 * rest)
        self.at_home = self.owner == self.mine

    def block(self, slot):
        return 4 * slot + (self.mine if slot % 2 == 0 else 3 - self.mine)

    def worker(self, group):
        return (self.owner // 2) * 8 + group * 2 + self.owner % 2

    def greet_all(self, extra=()):
        barrier = pltpu.get_barrier_semaphore()
        for name in extra:
            pl.semaphore_signal(
                barrier, inc=1, device_id=self.dev[name], device_id_type=MESH
            )
        for step in range(1, 16):
            pl.semaphore_signal(
                barrier, inc=1, device_id=((self.c + step) % 16, self.d), device_id_type=MESH
            )
        pl.semaphore_wait(barrier, 15 + len(extra))

    def copy_to(self, ctx, src, dst, send_sem, recv_sem):
        return pltpu.make_async_remote_copy(
            src_ref=src,
            dst_ref=dst,
            send_sem=send_sem,
            recv_sem=recv_sem,
            device_id=(ctx, self.d),
            device_id_type=MESH,
        )


class Rows:
    def __init__(self, me, src, dst, send_sem, recv_sem, back):
        self.me, self.src, self.dst = me, src, dst
        self.send_sem, self.recv_sem, self.back = send_sem, recv_sem, back

    def to_worker(self, group, ours):
        me = self.me
        away = jnp.logical_not(jnp.logical_and(me.at_home, me.z == group))
        if self.back:
            copy = me.copy_to(
                me.worker(group), self.src.at[0], self.dst.at[group],
                self.send_sem.at[0], self.recv_sem.at[group],
            )
        else:
            copy = me.copy_to(
                me.worker(group), self.src.at[group], self.dst.at[me.slot],
                self.send_sem.at[group], self.recv_sem.at[me.slot],
            )
        return away, copy

    def to_home(self, slot):
        me = self.me
        away = me.block(slot) != me.c
        if self.back:
            copy = me.copy_to(
                me.block(slot), self.src.at[slot], self.dst.at[me.z],
                self.send_sem.at[slot], self.recv_sem.at[me.z],
            )
        else:
            copy = me.copy_to(
                me.block(slot), self.src.at[0], self.dst.at[slot],
                self.send_sem.at[0], self.recv_sem.at[slot],
            )
        return away, copy

    def each(self, sending, action):
        for index in range(4):
            if sending != self.back:
                away, copy = self.to_worker(index, sending)
            else:
                away, copy = self.to_home(index)

            @pl.when(away)
            def _():
                action(copy)

    def start(self):
        me = self.me
        self.each(True, lambda copy: copy.start())

        @pl.when(me.at_home)
        def _():
            if self.back:
                self.dst[me.z] = self.src[me.slot]
            else:
                self.dst[me.slot] = self.src[me.z]

    def arrive(self):
        self.each(False, lambda copy: copy.wait_recv())

    def end(self):
        self.each(True, lambda copy: copy.wait_send())


class Pairs:
    def __init__(self, me, src, out, send_sem, recv_sem):
        self.me, self.src, self.out = me, src, out
        self.send_sem, self.recv_sem, self.done = send_sem, recv_sem, []
        self.groups = (me.z_a, me.z_b, me.z_ab)

    def go(self, name, src, dst, slot):
        copy = self.me.send(name, src, dst, self.send_sem.at[slot], self.recv_sem.at[slot])
        self.done.append(copy)
        return copy

    def start(self):
        me = self.me
        self.out[me.c] = self.src[me.z]
        self.first = [
            self.go(name, self.src.at[group], self.out.at[me.c], slot)
            for slot, (name, group) in enumerate(zip(("za", "zb", "zab"), self.groups))
        ]
        self.over_x, self.over_core = [], []
        self.pass_on(0)

    def pass_on(self, step):
        me = self.me
        block = me.x_hi * 8 + ((me.z,) + self.groups)[step] * 2 + me.core
        spot = self.out.at[block]
        self.over_x.append(self.go("xab", spot, spot, 3 + step))
        self.over_core.append(self.go("core", spot, spot, 7 + step))

    def second(self):
        for step in range(1, 4):
            self.first[step - 1].wait_recv()
            self.pass_on(step)

    def third(self):
        me = self.me
        for step, group in enumerate((me.z,) + self.groups):
            self.over_x[step].wait_recv()
            spot = self.out.at[(1 - me.x_hi) * 8 + group * 2 + me.core]
            self.over_core.append(self.go("core", spot, spot, 11 + step))

    def arrive(self):
        for copy in self.over_core:
            copy.wait_recv()

    def end(self):
        for copy in self.done:
            copy.wait_send()


class Sums:
    def __init__(self, me, src, total, send_sem, recv_sem, got_core, part, got_x):
        self.me, self.src, self.total = me, src, total
        self.send_sem, self.recv_sem, self.done = send_sem, recv_sem, []
        self.got_core, self.part, self.got_x = got_core, part, got_x
        self.order = (me.z_ab, me.z_a, me.z_b, me.z)

    def go(self, name, src, dst, slot):
        copy = self.me.send(name, src, dst, self.send_sem.at[slot], self.recv_sem.at[slot])
        self.done.append(copy)
        return copy

    def start(self):
        me = self.me
        self.near, self.far = me.x_hi * 4, (1 - me.x_hi) * 4
        self.core_copies = [
            self.go(
                "core",
                self.src.at[side + group, 1 - me.core],
                self.got_core.at[side + group],
                4 * index + step,
            )
            for index, side in enumerate((self.far, self.near))
            for step, group in enumerate(self.order)
        ]

    def join(self):
        for index, side in enumerate((self.far, self.near)):
            for step, group in enumerate(self.order):
                self.core_copies[4 * index + step].wait_recv()
                block = side + group
                self.total[block] = self.src[block, self.me.core] + self.got_core[block]

    def over(self):
        me = self.me
        self.over_x = []
        for step, group in enumerate(self.order):
            self.core_copies[step].wait_recv()
            block = self.far + group
            self.part[block] = self.src[block, me.core] + self.got_core[block]
            self.over_x.append(self.go("xab", self.part.at[block], self.got_x.at[group], 8 + step))
        for step, group in enumerate(self.order):
            self.core_copies[4 + step].wait_recv()
            block = self.near + group
            self.part[block] = self.src[block, me.core] + self.got_core[block]

    def finish(self, then=None):
        for step, group in enumerate(self.order):
            self.over_x[step].wait_recv()
            self.total[group] = self.part[self.near + group] + self.got_x[group]
            if then is not None and step < 3:
                then.send(step)

    def end(self):
        for copy in self.done:
            copy.wait_send()


class Owners:
    def __init__(self, me, total, out, send_sem, recv_sem):
        self.me, self.total, self.out = me, total, out
        self.send_sem, self.recv_sem, self.copies = send_sem, recv_sem, []

    def send(self, step):
        me = self.me
        group, name = ((me.z_ab, "zab"), (me.z_a, "za"), (me.z_b, "zb"))[step]
        self.copies.append(
            me.send(
                name, self.total.at[group], self.out.at[me.z],
                self.send_sem.at[step], self.recv_sem.at[step],
            )
        )

    def arrive(self):
        self.out[self.me.z] = self.total[self.me.z]
        for copy in self.copies:
            copy.wait_recv()

    def end(self):
        for copy in self.copies:
            copy.wait_send()


def lane_mask(value, begin, end):
    lane = lax.broadcasted_iota(jnp.int32, value.shape, 1)
    return jnp.where(jnp.logical_and(lane >= begin, lane < end), value, jnp.zeros_like(value))


def cut_heads(value, after):
    groups = []
    for half in range(2):
        left = value[:, 384 * half : 384 * half + 256]
        right = value[:, 384 * half + 128 : 384 * half + 384]
        if after:
            groups += [lane_mask(left, 0, 192), lane_mask(pltpu.roll(right, 192, 1), 0, 192)]
        else:
            groups += [lane_mask(pltpu.roll(left, 64, 1), 64, 256), lane_mask(right, 64, 256)]
    return groups


def join_heads(groups, after):
    pieces = []
    for half in range(2):
        left, right = groups[2 * half], groups[2 * half + 1]
        if after:
            right = pltpu.roll(right, 64, 1)
        else:
            left = pltpu.roll(left, 192, 1)
        pieces += [left[:, :128], left[:, 128:] + right[:, :128], right[:, 128:]]
    return jnp.concatenate(pieces, axis=1)


def put_rows(ref, value, after):
    for group, part in enumerate(cut_heads(value, after)):
        ref[group] = part.astype(jnp.bfloat16)


def get_rows(ref, after):
    return join_heads([ref[group].astype(jnp.float32) for group in range(4)], after)


def put_pairs(ref, keys, values):
    for group, (left, right) in enumerate(zip(cut_heads(keys, True), cut_heads(values, False))):
        ref[group, :, 0:128] = left[:, :128].astype(jnp.bfloat16)
        ref[group, :, 128:256] = (left[:, 128:] + right[:, :128]).astype(jnp.bfloat16)
        ref[group, :, 256:384] = right[:, 128:].astype(jnp.bfloat16)


def get_pairs(ref):
    keys = [lane_mask(ref[group, :, 0:256].astype(jnp.float32), 0, 192) for group in range(4)]
    values = [lane_mask(ref[group, :, 128:384].astype(jnp.float32), 64, 256) for group in range(4)]
    return join_heads(keys, True), join_heads(values, False)


def scale_of(value):
    return lax.rsqrt(jnp.mean(value * value, axis=-1, keepdims=True) + EPSILON)


def norm_back(value, gain, grad):
    scale = scale_of(value)
    weighted = grad * gain
    middle = jnp.mean(value * weighted, axis=-1, keepdims=True)
    dgain = jnp.sum(grad * (value * scale), axis=0, keepdims=True)
    return scale * weighted - value * (scale * scale * scale) * middle, dgain


def open_kernel(
    layer_input, encoder, gain, cotangent, *refs
):
    shards = refs[:11]
    q_out, kv_out, ckv_out, normed_out, normed_peer, encoder_peer, cotangent_peer = refs[11:18]
    outs = refs[18:29]
    (q_mine, kv_mine, ckv_mine, q_send, q_recv, kv_send, kv_recv, ckv_send, ckv_recv,
     early_send, early_recv, late_send, late_recv, feed_send, feed_recv, held, held_sem,
     share_send, share_recv) = refs[29:]
    me = Share()
    me.greet_all(extra=("ya", "yb", "xa", "xb"))
    early = make_groups(me, shards[:5], outs[:5], EARLY_PLAN, early_send, early_recv)
    late = make_groups(me, shards[5:8], outs[5:8], LATE_PLAN, late_send, late_recv)
    feed = make_groups(me, shards[8:], outs[8:], FEED_PLAN, feed_send, feed_recv)
    run_stage(early[0], 0)
    run_stage(early[1], 0)
    run_stage(late[0], 0)
    run_stage(late[1], 0)
    run_stage(early[0], 1)
    run_stage(early[1], 1)
    run_stage(feed[0], 0)
    run_stage(early[0], 2)
    run_stage(early[1], 2)
    residual = layer_input[...].astype(jnp.float32)
    normed = (residual * scale_of(residual) * gain[...]).astype(jnp.bfloat16)
    normed_out[...] = normed
    shared = [
        me.send("core", src, dst, share_send.at[slot], share_recv.at[slot])
        for slot, (src, dst) in enumerate(
            ((normed_out, normed_peer), (encoder, encoder_peer), (cotangent, cotangent_peer))
        )
    ]
    run_stage(late[0], 1)
    run_stage(late[1], 1)
    run_stage(feed[0], 1)
    run_stage(early[0], 3)
    run_stage(early[0], 4)

    def fetch(index):
        fetched = []
        for y in range(4):
            for x in range(2):
                begin = 96 * (2 * y + x)
                fetched.append(
                    pltpu.make_async_copy(
                        outs[index].at[y, x],
                        held.at[index, pl.ds(begin, 96)],
                        held_sem.at[index, 2 * y + x],
                    )
                )
                fetched[-1].start()
        return fetched

    def wait_all(copies):
        for copy in copies:
            copy.wait()

    fetched = [fetch(index) for index in range(3)]
    wait_all(fetched[1])
    wait_all(fetched[2])
    put_pairs(kv_mine, dot_nn(normed, held[1]), dot_nn(normed, held[2]))
    self_kv = Pairs(me, kv_mine, kv_out, kv_send, kv_recv)
    self_kv.start()
    wait_all(fetched[0])
    put_rows(q_mine, dot_nn(normed, held[0]), True)
    rows = Rows(me, q_mine, q_out, q_send, q_recv, False)
    rows.start()
    run_stage(early[1], 3)
    self_kv.second()
    run_stage(late[0], 2)
    run_stage(late[1], 2)
    sooner = [feed[0][index] for index in (0, 1, 4)]
    later = [feed[0][index] for index in (2, 3, 5)]
    run_stage(sooner, 2)
    run_stage(early[1], 4)
    fetched += [fetch(index) for index in range(3, 5)]
    wait_all(fetched[3])
    wait_all(fetched[4])
    put_pairs(ckv_mine, dot_nn(encoder[...], held[3]), dot_nn(encoder[...], held[4]))
    spot = ckv_out.at[me.x_hi, me.z, me.core]
    own_kv = pltpu.make_async_copy(ckv_mine.at[me.z], spot, ckv_send.at[3])
    own_kv.start()
    cross_kv = [
        me.send(name, ckv_mine.at[group], spot, ckv_send.at[slot], ckv_recv.at[slot])
        for slot, (name, group) in enumerate(
            (("za", me.z_a), ("zb", me.z_b), ("zab", me.z_ab))
        )
    ]
    run_stage(late[0], 3)
    run_stage(late[1], 3)
    run_stage(late[0], 4)
    self_kv.third()
    run_stage(late[1], 4)
    run_stage(late[0], 5)
    rows.arrive()
    self_kv.arrive()
    own_kv.wait()
    for copy in cross_kv:
        copy.wait_recv()
    for chain in sooner:
        chain.last.wait_recv()
    for chain in later:
        chain.second_copy.wait_recv()
        chain.third_copy.wait_recv()
        chain.own_copy.wait_recv()
    for chains in early + late + feed:
        for chain in chains:
            wait_sent(chain.copies)
    rows.end()
    self_kv.end()
    wait_sent(cross_kv)
    for copy in shared:
        copy.wait()


def wait_sent(copies):
    for copy in copies:
        copy.wait_send()


def open_layer(layer_input, encoder, gain, cotangent, shards, collective_id):
    bf = jnp.bfloat16
    early, late = chain_count(EARLY_PLAN), chain_count(LATE_PLAN)
    outs = pl.pallas_call(
        open_kernel,
        out_shape=[
            jax.ShapeDtypeStruct((4, 128, 256), bf),
            jax.ShapeDtypeStruct((16, 128, 384), bf),
            jax.ShapeDtypeStruct((2, 4, 2, 128, 384), bf),
        ]
        + [jax.ShapeDtypeStruct((128, 768), bf)] * 4
        + [jax.ShapeDtypeStruct((4, 2) + shard.shape, bf) for shard in shards],
        in_specs=[VMEM] * 3 + [ANY] * 12,
        out_specs=[VMEM] * 2 + [ANY] + [VMEM] * 3 + [ANY] * 12,
        scratch_shapes=[
            pltpu.VMEM((4, 128, 256), bf),
            pltpu.VMEM((4, 128, 384), bf),
            pltpu.VMEM((4, 128, 384), bf),
            pltpu.SemaphoreType.DMA((4,)),
            pltpu.SemaphoreType.DMA((4,)),
            pltpu.SemaphoreType.DMA((15,)),
            pltpu.SemaphoreType.DMA((15,)),
            pltpu.SemaphoreType.DMA((15,)),
            pltpu.SemaphoreType.DMA((15,)),
            pltpu.SemaphoreType.DMA((early, 7)),
            pltpu.SemaphoreType.DMA((early, 7)),
            pltpu.SemaphoreType.DMA((late, 7)),
            pltpu.SemaphoreType.DMA((late, 7)),
            pltpu.SemaphoreType.DMA((6, 7)),
            pltpu.SemaphoreType.DMA((6, 7)),
            pltpu.VMEM((5, 768, 768), bf),
            pltpu.SemaphoreType.DMA((5, 8)),
            pltpu.SemaphoreType.DMA((3,)),
            pltpu.SemaphoreType.DMA((3,)),
        ],
        compiler_params=pltpu.CompilerParams(
            collective_id=collective_id, has_side_effects=True, vmem_limit_bytes=VMEM_BYTES
        ),
        name="open_layer",
    )(layer_input, encoder, gain, cotangent, *shards)
    return outs[:7], [whole(out) for out in outs[7:15]], outs[15:]


def whole(gathered):
    return gathered.reshape(8 * gathered.shape[2], gathered.shape[3])


def row_scratch():
    return [
        pltpu.VMEM((4, 128, 256), jnp.bfloat16),
        pltpu.SemaphoreType.DMA((4,)),
        pltpu.SemaphoreType.DMA((4,)),
    ]


def sum_scratch():
    bf = jnp.bfloat16
    return [
        pltpu.SemaphoreType.DMA((12,)),
        pltpu.SemaphoreType.DMA((12,)),
        pltpu.VMEM((8, 128, 384), bf),
        pltpu.VMEM((8, 128, 384), bf),
        pltpu.VMEM((4, 128, 384), bf),
    ]


def owner_scratch():
    return [
        pltpu.VMEM((4, 128, 384), jnp.bfloat16),
        pltpu.SemaphoreType.DMA((3,)),
        pltpu.SemaphoreType.DMA((3,)),
    ]


def shared_call(
    kernel, name, args, shapes, scratch, collective_id, carry=(), hops=(), share=(),
    load_carry=False, pair_hops=(),
):
    return staged_call(
        kernel, name, args, shapes, scratch, collective_id, "all", carry, hops, share, load_carry,
        pair_hops,
    )


def middle_kernel(
    o_in, layer_input, gain, w_out, w_query, start_hops,
    q_out, attended_out, middle_out, normed_out,
    o_mine, o_send, o_recv, q_mine, q_send, q_recv,
):
    me = Share()
    back = Rows(me, o_in, o_mine, o_send, o_recv, True)
    back.start()
    back.arrive()
    start_hops()
    attended = get_rows(o_mine, False).astype(jnp.bfloat16)
    middle = layer_input[...].astype(jnp.float32) + dot_nn(attended, w_out[...])
    normed = (middle * scale_of(middle) * gain[...]).astype(jnp.bfloat16)
    put_rows(q_mine, dot_nn(normed, w_query[...]), True)
    rows = Rows(me, q_mine, q_out, q_send, q_recv, False)
    rows.start()
    attended_out[...] = attended
    middle_out[...] = middle
    normed_out[...] = normed
    rows.arrive()
    back.end()
    rows.end()


def feed_kernel(
    o_in, middle, gain, w_out, cotangent, w_gate, w_up, w_down,
    g_out, final_out, crossed_out, normed_out, grad_gate, grad_up, mixed, branch_out, after_out,
    dgain_out,
    o_mine, o_send, o_recv, g_mine, g_send, g_recv, grad_mixed,
):
    low = jnp.bfloat16
    me = Share()
    back = Rows(me, o_in, o_mine, o_send, o_recv, True)
    back.start()
    w_down.prepare()
    w_gate.prepare()
    w_up.prepare()
    grad_mixed[...] = dot_nt(cotangent[...], w_down[...])
    back.arrive()
    crossed = get_rows(o_mine, False).astype(low)
    crossed_out[...] = crossed
    after = middle[...] + dot_nn(crossed, w_out[...])
    normed = (after * scale_of(after) * gain[...]).astype(low)
    normed_out[...] = normed
    root = math.sqrt(2.0 / math.pi)
    for chunk in range(8):
        cols = slice(256 * chunk, 256 * chunk + 256)
        gate = dot_nn(normed, w_gate[:, cols])
        up = dot_nn(normed, w_up[:, cols])
        square = gate * gate
        curve = jnp.tanh(root * gate * (1.0 + 0.044715 * square))
        half = 0.5 * (1.0 + curve)
        gelu = gate * half
        slope = half + 0.5 * gate * (1.0 - curve * curve) * (
            root * (1.0 + 3 * 0.044715 * square)
        )
        incoming = grad_mixed[:, cols]
        mixed[:, cols] = (gelu * up).astype(low)
        grad_gate[:, cols] = (incoming * up * slope).astype(low)
        grad_up[:, cols] = (incoming * gelu).astype(low)
    for ref in (mixed, grad_gate, grad_up):
        ref.tell()
    grad_normed = dot_nt(grad_gate[...], w_gate[...]) + dot_nt(grad_up[...], w_up[...])
    grad_value, dgain = norm_back(after, gain[...], grad_normed)
    dgain_out[...] = dgain
    grad_after = cotangent[...].astype(jnp.float32) + grad_value
    branch = grad_after.astype(low)
    put_rows(g_mine, dot_nt(branch, w_out[...]), False)
    rows = Rows(me, g_mine, g_out, g_send, g_recv, False)
    rows.start()
    branch_out[...] = branch
    after_out[...] = grad_after
    final_out[...] = (after + dot_nn(mixed[...], w_down[...])).astype(low)
    rows.arrive()
    back.end()
    rows.end()


def turn_kernel(
    dq_in, dkv_in, middle, gain, grad_after, w_query, w_out,
    g_out, dq_out, part_out, branch_out, grad_out, dgain_out,
    dq_mine, dq_send, dq_recv, g_mine, g_send, g_recv, kv_send, kv_recv, got_core,
):
    low = jnp.bfloat16
    me = Share()
    back = Rows(me, dq_in, dq_mine, dq_send, dq_recv, True)
    back.start()
    pairs = Sums(me, dkv_in, part_out, kv_send, kv_recv, got_core, None, None)
    pairs.start()
    back.arrive()
    grad_query = get_rows(dq_mine, True).astype(low)
    dq_out[...] = grad_query
    grad_value, dgain = norm_back(middle[...], gain[...], dot_nt(grad_query, w_query[...]))
    dgain_out[...] = dgain
    grad_middle = grad_after[...] + grad_value
    branch = grad_middle.astype(low)
    put_rows(g_mine, dot_nt(branch, w_out[...]), False)
    rows = Rows(me, g_mine, g_out, g_send, g_recv, False)
    rows.start()
    branch_out[...] = branch
    grad_out[...] = grad_middle
    pairs.join()
    rows.arrive()
    back.end()
    rows.end()
    pairs.end()


def close_kernel(
    dq_in, dkv_in, layer_input, gain, grad_middle, w_query, w_key, w_value,
    cross_part, cross_got, w_ckey, w_cvalue, *rest,
):
    acts, peers, rest = rest[:7], rest[7:14], rest[14:]
    grad_out, encoder_out, dq_out, dk_out, dv_out, cross_dk, cross_dv, dgain_out = rest[:8]
    turned_out, mixed_out, dq_mine, dq_send, dq_recv, total, *scratch = rest[8:]
    low = jnp.bfloat16
    me = Share()
    sums, self_own, cross_own, cross_total = scratch[:5], scratch[5:8], scratch[8:11], scratch[11]
    pairs = Sums(me, dkv_in, total, *sums)
    pairs.start()
    back = Rows(me, dq_in, dq_mine, dq_send, dq_recv, True)
    back.start()
    cross_total[...] = cross_part()[pl.ds(me.x_hi * 4, 4)] + cross_got[...]
    cross = Owners(me, cross_total, *cross_own)
    for step in range(3):
        cross.send(step)
    pairs.over()
    for index in range(6):
        both = jnp.concatenate([acts[index][...], peers[index][...]], axis=0)
        turned_out[index] = both.T.reshape(8, 6, 16, 256)
    cross.arrive()
    keys, values = get_pairs(cross_own[0])
    keys, values = keys.astype(low), values.astype(low)
    cross_dk[...] = keys
    cross_dv[...] = values
    encoder_out[...] = dot_nt(keys, w_ckey[...]) + dot_nt(values, w_cvalue[...])
    back.arrive()
    grad_query = get_rows(dq_mine, True).astype(low)
    dq_out[...] = grad_query
    grad_normed = dot_nt(grad_query, w_query[...])
    owners = Owners(me, total, *self_own)
    pairs.finish(owners)
    both = jnp.concatenate([acts[6][...], peers[6][...]], axis=0)
    mixed_out[...] = both.T.reshape(8, 8, 2, 16, 256)
    owners.arrive()
    keys, values = get_pairs(self_own[0])
    keys, values = keys.astype(low), values.astype(low)
    dk_out[...] = keys
    dv_out[...] = values
    grad_normed = grad_normed + dot_nt(keys, w_key[...]) + dot_nt(values, w_value[...])
    residual = layer_input[...].astype(jnp.float32)
    grad_value, dgain = norm_back(residual, gain[...], grad_normed)
    dgain_out[...] = dgain
    grad_out[...] = grad_middle[...] + grad_value
    back.end()
    pairs.end()
    cross.end()
    owners.end()


def dot_nn(left, right):
    return jnp.dot(left, right, preferred_element_type=jnp.float32)


def dot_nt(left, right):
    return lax.dot_general(
        left, right, (((1,), (1,)), ((), ())), preferred_element_type=jnp.float32
    )


def head_lanes(value, head):
    lane = lax.broadcasted_iota(jnp.int32, value.shape, 1)
    return jnp.where(lane // 64 == head, value, jnp.zeros_like(value))


def head_rows(value, head):
    row = lax.broadcasted_iota(jnp.int32, value.shape, 0)
    return jnp.where(row // 64 == head, value, jnp.zeros_like(value))


def bias_offset(pair, side, chunk):
    c = lax.axis_index("ctx")
    mine = (c // 8) * 2 + c % 2
    block = 8 * pair + (mine if side == 0 else 7 - mine)
    return pl.multiple_of((15 - block) * 128 + chunk * 256, 128)


def bias_at(wide, head, pair, chunk):
    return jnp.concatenate(
        [wide[head, pl.ds(bias_offset(pair, side, chunk), 256), :] for side in range(2)], axis=1
    )


def forward_kernel(causal, *refs):
    if causal:
        q, kv, waves, o_low, o_full, lse, wide, values_t, score, total = refs
        def build(head, carry):
            for tile in range(USED):
                row = jnp.broadcast_to(waves[head, tile : tile + 1, :], (128, 256))
                turned = pltpu.roll(row, 129, 1, stride=1, stride_axis=0)
                wide[head, tile * 128 : tile * 128 + 128, :] = turned[:, :128]
            wide[head, USED * 128 :, :] = jnp.full(
                ((TILES - USED) * 128, 128), NEGATIVE, jnp.float32
            )
            return carry

        lax.fori_loop(0, 3, build, 0)
    else:
        q, kv, o_low, o_full, lse, values_t, score, total = refs

    for chunk in range(8):
        values_t[chunk] = kv[2 * chunk : 2 * chunk + 2, :, 128:384].reshape(256, 256).T
    for pair in range(2):
        chunks = 4 if causal and pair == 0 else 8
        rows = q[2 * pair : 2 * pair + 2].reshape(256, 256)
        total[...] = jnp.zeros_like(total)

        def one_head(head, carry):
            masked = head_lanes(rows, head)

            top = jnp.full((8, 256), NEGATIVE, jnp.float32)
            for chunk in range(chunks):
                keys = kv[2 * chunk : 2 * chunk + 2, :, 0:256].reshape(256, 256)
                block = dot_nt(keys, masked)
                if causal:
                    block = block + bias_at(wide, head, pair, chunk)
                score[chunk] = block
                top = jnp.maximum(top, jnp.max(block.reshape(32, 8, 256), axis=0))
            top = jnp.max(top, axis=0, keepdims=True)
            summed = jnp.zeros((8, 256), jnp.float32)
            held = jnp.zeros((256, 256), jnp.float32)
            for chunk in range(chunks):
                expo = jnp.exp(score[chunk] - top)
                summed = summed + jnp.sum(expo.reshape(32, 8, 256), axis=0)
                held = held + dot_nn(values_t[chunk], expo.astype(jnp.bfloat16))
            summed = jnp.sum(summed, axis=0, keepdims=True)
            total[...] += head_rows(held * (1.0 / summed), head + 1)
            lse[head, pair] = top + jnp.log(summed)
            return carry

        lax.fori_loop(0, 3, one_head, 0)
        final = total[...].T.reshape(2, 128, 256)
        o_full[2 * pair : 2 * pair + 2] = final
        o_low[2 * pair : 2 * pair + 2] = final.astype(jnp.bfloat16)


def attend(q, kv, waves, collective_id, greet, carry, hops, pair_hops=()):
    causal = waves is not None
    shapes = [
        ((4, 128, 256), jnp.bfloat16),
        ((4, 128, 256), jnp.float32),
        ((3, 2, 1, 256), jnp.float32),
    ]
    args = [q, kv]
    if causal:
        shapes.append(((3, TILES * 128, 128), jnp.float32))
        args.append(waves)
    return staged_call(
        functools.partial(forward_kernel, causal),
        "attend_self" if causal else "attend_cross",
        args,
        shapes,
        [
            pltpu.VMEM((8, 256, 256), jnp.bfloat16),
            pltpu.VMEM((8, 256, 256), jnp.float32),
            pltpu.VMEM((256, 256), jnp.float32),
        ],
        collective_id,
        greet,
        carry,
        hops,
        pair_hops=pair_hops,
    )


def backward_kernel(causal, *refs):
    if causal:
        (q, kv, grad, o_full, lse, wide, cross_part, dq, dkv, waves, cross_got,
         keys_t, dk, dv, dq_t, turned, along, cross_send, cross_recv) = refs
        along[...] = jnp.zeros_like(along)
        me = Place()
        passing = me.send(
            "xab", cross_part.at[pl.ds((1 - me.x_hi) * 4, 4)], cross_got, cross_send, cross_recv
        )
    else:
        q, kv, grad, o_full, lse, dq, dkv, keys_t, dk, dv, dq_t, turned = refs
    dk[...] = jnp.zeros_like(dk)
    dv[...] = jnp.zeros_like(dv)

    for chunk in range(8):
        keys_t[chunk] = kv[2 * chunk : 2 * chunk + 2, :, 0:256].reshape(256, 256).T
    for pair in range(2):
        chunks = 4 if causal and pair == 0 else 8
        both = slice(2 * pair, 2 * pair + 2)
        rows = q[both].reshape(256, 256)
        grads = grad[both].reshape(256, 256)
        turned[...] = (grads.astype(jnp.float32) * o_full[both].reshape(256, 256)).T
        dq_t[...] = jnp.zeros_like(dq_t)

        def one_head(head, carry):
            masked = head_lanes(rows, head)
            masked_grads = head_lanes(grads, head + 1)
            delta = jnp.sum(head_rows(turned[...], head + 1), axis=0, keepdims=True)
            row_lse = lse[head, pair]

            held = jnp.zeros((256, 256), jnp.float32)
            for chunk in range(chunks):
                block = kv[2 * chunk : 2 * chunk + 2].reshape(256, 384)
                scores = dot_nt(block[:, 0:256], masked)
                if causal:
                    scores = scores + bias_at(wide, head, pair, chunk)
                probs = jnp.exp(scores - row_lse)
                grad_probs = dot_nt(block[:, 128:384], masked_grads)
                grad_scores = probs * (grad_probs - delta)
                low = grad_scores.astype(jnp.bfloat16)
                spot = slice(chunk * 256, chunk * 256 + 256)
                dk[spot] += dot_nn(low, masked)
                dv[spot] += dot_nn(probs.astype(jnp.bfloat16), masked_grads)
                if causal:
                    for side in range(2):
                        where = pl.ds(bias_offset(pair, side, chunk), 256)
                        along[head, where, :] += grad_scores[:, 128 * side : 128 * side + 128]
                held = held + dot_nn(keys_t[chunk], low)
            dq_t[...] += head_rows(held, head)
            return carry

        lax.fori_loop(0, 3, one_head, 0)
        dq[both] = dq_t[...].T.reshape(2, 128, 256).astype(jnp.bfloat16)

    def pack(block, carry):
        spot = pl.ds(pl.multiple_of(block * 128, 128), 128)
        key_part, value_part = dk[spot], dv[spot]
        dkv[block, :, 0:128] = key_part[:, 0:128].astype(jnp.bfloat16)
        dkv[block, :, 128:256] = (key_part[:, 128:256] + value_part[:, 0:128]).astype(jnp.bfloat16)
        dkv[block, :, 256:384] = value_part[:, 128:256].astype(jnp.bfloat16)
        return carry

    lax.fori_loop(0, 16, pack, 0)
    if causal:
        waves[...] = jnp.zeros_like(waves)

        def fold(head, carry):
            for tile in range(USED):
                value = along[head, tile * 128 : tile * 128 + 128, :]
                value = jnp.concatenate([value, jnp.zeros_like(value)], axis=1)
                count = 64
                while count >= 1:
                    value = pltpu.roll(value[:count], count, 1) + value[count:]
                    count //= 2
                waves[head, tile : tile + 1, :] = value
            return carry

        lax.fori_loop(0, 3, fold, 0)
        passing.wait()


def attend_back(q, kv, grad, o_full, lse, wide, cross_part):
    causal = wide is not None
    shapes = [((4, 128, 256), jnp.bfloat16), ((16, 128, 384), jnp.bfloat16)]
    args = [q, kv, grad, o_full, lse]
    scratch = [
        pltpu.VMEM((8, 256, 256), jnp.bfloat16),
        pltpu.VMEM((2048, 256), jnp.float32),
        pltpu.VMEM((2048, 256), jnp.float32),
        pltpu.VMEM((256, 256), jnp.float32),
        pltpu.VMEM((256, 256), jnp.float32),
    ]
    if causal:
        shapes += [((3, TILES, 256), jnp.float32), ((4, 128, 384), jnp.bfloat16)]
        args += [wide, cross_part]
        scratch.append(pltpu.VMEM((3, TILES * 128, 128), jnp.float32))
        scratch += [pltpu.SemaphoreType.DMA] * 2
    return staged_call(
        functools.partial(backward_kernel, causal),
        "attend_back_self" if causal else "attend_back_cross",
        args,
        shapes,
        scratch,
        9 if causal else None,
        ("xab",) if causal else None,
    )


PRECISE = lax.Precision.HIGHEST


def body(
    layer_input,
    encoder_states,
    cotangent,
    bucket_ids,
    bias_table,
    gain_first,
    gain_second,
    gain_third,
    self_query,
    self_key,
    self_value,
    self_output,
    cross_query,
    cross_key,
    cross_value,
    cross_output,
    gate_weight,
    up_weight,
    down_weight,
):
    bucket_count, head_count = bias_table.shape
    width = layer_input.shape[-1]
    layer_input, encoder_states, cotangent = layer_input[0], encoder_states[0], cotangent[0]
    gain_first, gain_second, gain_third = (
        gain.reshape(1, width) for gain in (gain_first, gain_second, gain_third)
    )
    low, full = jnp.bfloat16, jnp.float32
    grouped, rows, wide_rows, line = (4, 128, 256), (128, 768), (128, 2048), (1, 768)
    first_head = 3 * ((lax.axis_index("ctx") // 2) % 4)
    padded = jnp.pad(bucket_ids, (TILES * 128 - bucket_ids.shape[0] + 128, 0), constant_values=-1)
    last = padded.shape[0]
    ids = jnp.stack([padded[last - 255 - 128 * k : last - 128 * k] for k in range(TILES)])
    ids = jnp.pad(ids, ((0, 0), (0, 1)), constant_values=-1)
    hot = (ids[:, :, None] == jnp.arange(bucket_count, dtype=jnp.int32)).astype(jnp.float32)
    own_table = lax.dynamic_slice_in_dim(bias_table, first_head, 3, 1)
    waves = jnp.einsum("kxb,bh->hkx", hot, own_table, precision=PRECISE)
    waves = jnp.where((ids >= 0)[None], waves, NEGATIVE)

    (
        (self_q, self_kv, cross_kv, normed_one, normed_one_peer, encoder_peer, cotangent_peer),
        weights,
        feed,
    ) = open_layer(
        layer_input,
        encoder_states,
        gain_first,
        cotangent,
        (
            self_query, self_key, self_value, cross_key, cross_value,
            self_output, cross_query, cross_output, gate_weight, up_weight, down_weight,
        ),
        2,
    )
    w_query, w_key, w_value, w_ckey, w_cvalue, w_out, w_cquery, w_cout = weights
    (self_low, self_full, self_lse, wide), feed = attend(
        self_q, self_kv, waves, 7, ("xab", "core", "za", "zb"), (*feed, cross_kv),
        ("za", "zb", None, None, "core", None),
        (("xab", "near"), ("core", "near")),
    )
    (
        (cross_q, attended, middle, normed_two, attended_peer, normed_two_peer), feed
    ) = shared_call(
        middle_kernel,
        "middle",
        (self_low, layer_input, gain_second, w_out, w_cquery),
        ((grouped, low), (rows, low), (rows, full), (rows, low)),
        row_scratch() + row_scratch(),
        3,
        feed,
        ("core", "core", "side", "side", None, "side"),
        (1, 3),
        pair_hops=(("core", "far"),),
    )
    *feed, cross_kv = feed
    cross_kv = cross_kv.reshape(16, 128, 384)
    (cross_low, cross_full, cross_lse), feed = attend(
        cross_q, cross_kv, None, 8, ("core", "za", "zb"), feed,
        (None, None, "za", "zb", None, "core"),
    )
    feed_results, _ = shared_call(
        feed_kernel,
        "feed_forward",
        (cross_low, middle, gain_third, w_cout, cotangent),
        (
            (grouped, low), (rows, low), (rows, low), (rows, low), (wide_rows, low),
            (wide_rows, low), (wide_rows, low), (rows, low), (rows, full), (line, full),
        ),
        row_scratch() + row_scratch() + [pltpu.VMEM(wide_rows, full)],
        4,
        feed,
        (None, None, "core", "core", None, None),
        (2, 3, 7, 4, 5, 6),
        True,
    )
    (
        cross_grads, layer_output, crossed, normed_three, grad_gate, grad_up, mixed,
        branch_after, grad_after, dgain_third,
        *feed_peers,
    ) = feed_results
    (
        crossed_peer, normed_three_peer, branch_after_peer, gate_peer, up_peer, mixed_peer
    ) = feed_peers
    cross_dq, cross_dkv = attend_back(
        cross_q, cross_kv, cross_grads, cross_full, cross_lse, None, None
    )
    (
        self_grads, grad_cquery, cross_part, branch_middle, grad_middle, dgain_second,
        grad_cquery_peer, branch_middle_peer,
    ) = shared_call(
        turn_kernel,
        "turn",
        (
            cross_dq, cross_dkv.reshape(8, 2, 128, 384), middle, gain_second, grad_after,
            w_cquery, w_out,
        ),
        (
            (grouped, low), (rows, low), ((8, 128, 384), low), (rows, low), (rows, full),
            (line, full),
        ),
        row_scratch() + row_scratch() + sum_scratch()[:3],
        5,
        share=(1, 3),
    )
    self_dq, self_dkv, grad_waves, cross_got = attend_back(
        self_q, self_kv, self_grads, self_full, self_lse, wide, cross_part
    )
    (
        grad_input, grad_encoder, grad_queries, grad_keys, grad_values, grad_ckeys, grad_cvalues,
        dgain_first, turned, mixed_turned, *close_peers,
    ) = shared_call(
        close_kernel,
        "close",
        (
            self_dq, self_dkv.reshape(8, 2, 128, 384), layer_input, gain_first, grad_middle,
            w_query, w_key, w_value, cross_part, cross_got, w_ckey, w_cvalue,
            normed_one, attended, normed_two, encoder_states, crossed, normed_three, mixed,
            normed_one_peer, attended_peer, normed_two_peer, encoder_peer, crossed_peer,
            normed_three_peer, mixed_peer,
        ),
        ((rows, full), (rows, full)) + ((rows, low),) * 5 + ((line, full),)
        + (((6, 8, 6, 16, 256), low), ((8, 8, 2, 16, 256), low)),
        row_scratch()
        + [pltpu.VMEM((4, 128, 384), low)]
        + sum_scratch()
        + owner_scratch()
        + owner_scratch()
        + [pltpu.VMEM((4, 128, 384), low)],
        6,
        share=(2, 3, 4, 5, 6),
    )
    own_grads = jnp.einsum("kxb,hkx->bh", hot, grad_waves, precision=PRECISE)
    local_table = lax.dynamic_update_slice_in_dim(
        jnp.zeros_like(bias_table), own_grads, first_head, 1
    )
    small = jnp.concatenate(
        [dgain_first[0], dgain_second[0], dgain_third[0], local_table.reshape(-1)]
    )
    small = jnp.pad(small, (0, 24 * 128 - small.shape[0])).reshape(24, 128)
    full_sums, sums = reduce_weights(
        turned,
        mixed_turned,
        (
            grad_queries, grad_keys, grad_values, branch_middle,
            grad_cquery, grad_ckeys, grad_cvalues, branch_after,
            grad_gate, grad_up, cotangent,
        ),
        (
            *close_peers[:3], branch_middle_peer,
            grad_cquery_peer, *close_peers[3:], branch_after_peer,
            gate_peer, up_peer, cotangent_peer,
        ),
        small,
        1,
    )
    *shards, layer_output, grad_input, grad_encoder = place_all(
        full_sums, (layer_output, grad_input, grad_encoder)
    )
    sums = sums.reshape(-1)
    return (
        layer_output[None],
        grad_input[None],
        grad_encoder[None],
        sums[3 * width : 3 * width + bucket_count * head_count].reshape(bucket_count, head_count),
        sums[:width],
        sums[width : 2 * width],
        sums[2 * width : 3 * width],
    ) + tuple(shards)


def solution(mesh):
    placed = (
        P("dp", "ctx", None),
        P("dp", "ctx", None),
        P("dp", "ctx", None),
        P(),
        P(),
        P(),
        P(),
        P(),
        P("dp", None),
        P("dp", None),
        P("dp", None),
        P("dp", None),
        P("dp", None),
        P("dp", None),
        P("dp", None),
        P("dp", None),
        P("dp", None),
        P("dp", None),
        P("dp", None),
    )
    return jax.shard_map(
        body,
        mesh=mesh,
        in_specs=placed,
        out_specs=(
            P("dp", "ctx", None),
            P("dp", "ctx", None),
            P("dp", "ctx", None),
            P(),
            P(),
            P(),
            P(),
            P("dp", None),
            P("dp", None),
            P("dp", None),
            P("dp", None),
            P("dp", None),
            P("dp", None),
            P("dp", None),
            P("dp", None),
            P("dp", None),
            P("dp", None),
            P("dp", None),
        ),
        check_vma=False,
    )
```
